256 devices in a mesh: tile: 64 (over y, z, core), mode: 4 (over x).
Axes of the slice: x: 4, y: 4, z: 8, core: 2. Of those that a mesh axis runs over, the one named last changes fastest.
Arguments:
- object_pieces: float32 [1536, 2, 64, 128], P('tile'), may hold values from -5 to 5
- probe_modes: float32 [12, 2, 256, 256], P('mode'), may hold values from -1.6 to 1.6
- intensity: float32 [128, 256, 256], P('tile'), may hold values from 0.05 to 5
- positions: int32 [128, 2], P('tile'), may hold values from 0 to 3840, as said below
- counts: int32 [64], P('tile'), may hold values from 0 to 2, as said below
Outputs:
- object_new: float32 [1536, 2, 64, 128], P('tile')
- probe_grad: float32 [12, 2, 256, 256], P('mode')
The draws below stay inside these ranges and needn't reach their ends.
Inputs may be any that keep to these rules, and one draw needn't show every extreme that they name: `positions`: rows are multiples of 64 and columns multiples of 128; every live patch lies inside the object, and its top-left piece lies in its own device's tile (device d holds piece rows from (d // 8) * 6 and piece columns from (d mod 8) * 4, 6 x 4 of them); slots at or past their device's count hold zeros. counts[d] + counts[d + 32] = 2 for d < 32, and some device has 2.
All inputs are finite; a program needn't handle non-finite values.
Results may differ from the reference program's by a relative error of at most 0.0052.
Values sent between devices are 32-bit elements; how exact they have to be, the bound alone decides.
No kernel may reach another device: no remote copies, remote signals or barrier semaphores. Data moves between devices by JAX's collectives and lax.ppermute only.
A program may use at most 64 MiB of HBM per device.

```python
import math
import jax
import jax.numpy as jnp
from jax import lax

PATCH = 256
MODES = 12
DEV_COLS = 8
POS_CAP = 2
TILE_R = 6
TILE_C = 4
PIECE_R = 64
PIECE_C = 128
DEV_ROWS = 8
GRID_R = 48
GRID_C = 32
PIECES = 1536
SLOTS = 128
LIVE = 64
N_TILE = 64


def scan_layout(key):
    subkeys = jax.random.split(key, 5)
    half_dev = N_TILE // 2
    half_cap = POS_CAP // 2
    pair_ids = jnp.arange(half_dev, dtype=jnp.int32)
    offsets = jax.random.randint(subkeys[0], (half_dev,), -half_cap, half_cap + 1)
    offsets = jnp.where(pair_ids == half_dev - 1, jnp.minimum(offsets, 0), offsets)
    forced = jax.random.randint(subkeys[1], (), 0, half_dev - 1)
    signed = jax.random.randint(subkeys[2], (), 0, 2) * 2 - 1
    offsets = jnp.where(pair_ids == forced, signed * half_cap, offsets)
    counts = jnp.concatenate([half_cap + offsets, half_cap - offsets]).astype(jnp.int32)
    device_ids = jnp.arange(N_TILE, dtype=jnp.int32)
    dev_row = device_ids // DEV_COLS
    dev_col = device_ids % DEV_COLS
    row_most = jnp.where(dev_row == DEV_ROWS - 1, TILE_R - 4, TILE_R - 1)
    col_most = jnp.where(dev_col == DEV_COLS - 1, TILE_C - 2, TILE_C - 1)
    row_pick = jax.random.randint(subkeys[3], (N_TILE, POS_CAP), 0, row_most[:, None] + 1)
    col_pick = jax.random.randint(subkeys[4], (N_TILE, POS_CAP), 0, col_most[:, None] + 1)
    slot_ids = jnp.arange(POS_CAP, dtype=jnp.int32)
    row_pick = jnp.where(slot_ids[None, :] == 0, row_most[:, None], row_pick)
    col_pick = jnp.where(slot_ids[None, :] == 0, col_most[:, None], col_pick)
    is_live = (slot_ids[None, :] < counts[:, None]).astype(jnp.int32)
    rows = (dev_row[:, None] * TILE_R + row_pick) * PIECE_R * is_live
    cols = (dev_col[:, None] * TILE_C + col_pick) * PIECE_C * is_live
    positions = jnp.stack([rows, cols], axis=-1).reshape(N_TILE * POS_CAP, 2)
    return (positions.astype(jnp.int32), counts)


def draw_positions(key, part):
    return scan_layout(key)[0]


def draw_counts(key, part):
    return scan_layout(key)[1]


def draw_probe_modes(key, part):
    key = jax.random.fold_in(key, 17)
    order_key, value_key = jax.random.split(key, 2)
    ranked = jax.random.permutation(order_key, MODES).astype(jnp.float32)
    scales = 0.4 * 10.0 ** (-ranked / (MODES - 1))
    values = jnp.clip(jax.random.normal(value_key, (MODES, 2, PATCH, PATCH), jnp.float32), -4.0, 4.0)
    return values * scales[:, None, None, None]


def steps_of(key, dims, shards, low, largest):
    factor_of = 1.0
    for dim, blocks in shards:
        heights = jax.random.uniform(jax.random.fold_in(jax.random.fold_in(key, 6), dim), (blocks,), jnp.float32, low / len(shards), largest / len(shards))
        factor_of = factor_of * jnp.repeat(jnp.exp(heights), dims[dim] // blocks).reshape((-1,) + (1,) * (len(dims) - 1 - dim))
    return factor_of


def normal_values(rng, shape, spread, reach, pieces=(), kind=jnp.bfloat16):
    level = steps_of(rng, shape, pieces, -0.22, 0.18) if pieces else 1.0
    drawn = jax.random.normal(rng, shape, jnp.float32) * spread * level
    return jnp.minimum(jnp.maximum(drawn, -reach), reach).astype(kind)


def setup_inputs(seed: int = 0) -> dict:
    arg_keys = jax.random.split(jax.random.key(seed), 6)
    return {
        "object_pieces": normal_values(arg_keys[0], (PIECES, 2, PIECE_R, PIECE_C), 0.7, 5.0, ((0, 64),), jnp.float32),
        "probe_modes": draw_probe_modes(jax.random.fold_in(arg_keys[5], 71), 0),
        "intensity": jnp.clip(jnp.exp(math.log(5.0) - 4.6051702 * jax.random.uniform(arg_keys[2], (SLOTS, PATCH, PATCH), jnp.float32) ** steps_of(arg_keys[2], (SLOTS, PATCH, PATCH), ((0, 64),), -0.2, 0.2)), 0.05, 5.0),
        "positions": draw_positions(jax.random.fold_in(arg_keys[5], 71), 0),
        "counts": draw_counts(jax.random.fold_in(arg_keys[5], 71), 0),
    }


far_floor = 0.1
object_floor = 0.1

def fourier_tables(length):
    indices = jnp.arange(length, dtype=jnp.int32)
    phases = (indices[:, None] * indices[None, :] % length).astype(jnp.float32) * (2.0 * math.pi / length)
    scaling = 1.0 / math.sqrt(length)
    return ((jnp.cos(phases) * scaling).astype(jnp.bfloat16), (-jnp.sin(phases) * scaling).astype(jnp.bfloat16))

def wide_product(formula, left_side, right_side):
    return jnp.einsum(formula, left_side.astype(jnp.float32), right_side.astype(jnp.float32), precision=lax.Precision.HIGHEST)

def left_apply(tables, data_re, data_im, conj_sign):
    table_re, table_im = tables
    real_part = wide_product('ux,kxy->kuy', table_re, data_re) - conj_sign * wide_product('ux,kxy->kuy', table_im, data_im)
    imag_part = wide_product('ux,kxy->kuy', table_re, data_im) + conj_sign * wide_product('ux,kxy->kuy', table_im, data_re)
    return (real_part, imag_part)

def right_apply(tables, data_re, data_im, conj_sign):
    table_re, table_im = tables
    real_part = wide_product('kuy,yv->kuv', data_re, table_re) - conj_sign * wide_product('kuy,yv->kuv', data_im, table_im)
    imag_part = conj_sign * wide_product('kuy,yv->kuv', data_re, table_im) + wide_product('kuy,yv->kuv', data_im, table_re)
    return (real_part, imag_part)

def reference(object_pieces, probe_modes, intensity, positions, counts):
    tables = fourier_tables(PATCH)
    slot_ids = jnp.arange(SLOTS, dtype=jnp.int32)
    is_live = slot_ids % POS_CAP < counts[slot_ids // POS_CAP]
    live_slots = jnp.nonzero(is_live, size=LIVE)[0].astype(jnp.int32)
    object_grid = object_pieces.reshape(DEV_ROWS, DEV_COLS, TILE_R, TILE_C, 2, PIECE_R, PIECE_C)
    object_grid = object_grid.transpose(0, 2, 1, 3, 4, 5, 6).reshape(GRID_R, GRID_C, 2, PIECE_R, PIECE_C)
    probe_re = probe_modes[:, 0]
    probe_im = probe_modes[:, 1]
    light_sum = lax.optimization_barrier(jnp.sum(probe_re * probe_re + probe_im * probe_im, axis=0))
    light_blocks = light_sum.reshape(4, PIECE_R, 2, PIECE_C).transpose(0, 2, 1, 3)
    anchor = jnp.zeros((), jnp.int32)

    def one_slot(running, slot_id):
        probe_sum, summed_terms, weight = running
        piece_row = (positions[slot_id, 0] // PIECE_R).astype(jnp.int32)
        piece_col = (positions[slot_id, 1] // PIECE_C).astype(jnp.int32)
        corner_at = (piece_row, piece_col, anchor, anchor, anchor)
        piece_block = lax.dynamic_slice(object_grid, corner_at, (4, 2, 2, PIECE_R, PIECE_C))
        patch_image = piece_block.transpose(2, 0, 3, 1, 4).reshape(2, PATCH, PATCH)
        patch_re = patch_image[0]
        patch_im = patch_image[1]
        exit_re = (probe_re * patch_re - probe_im * patch_im).astype(jnp.bfloat16)
        exit_im = (probe_re * patch_im + probe_im * patch_re).astype(jnp.bfloat16)
        half_re, half_im = left_apply(tables, exit_re, exit_im, 1.0)
        far_re, far_im = right_apply(tables, half_re.astype(jnp.bfloat16), half_im.astype(jnp.bfloat16), 1.0)
        model_power = lax.optimization_barrier(jnp.sum(far_re * far_re + far_im * far_im, axis=0))
        factor = jnp.sqrt(intensity[slot_id]) / jnp.sqrt(model_power + far_floor) - 1.0
        change_re = (factor * far_re).astype(jnp.bfloat16)
        change_im = (factor * far_im).astype(jnp.bfloat16)
        back_re, back_im = left_apply(tables, change_re, change_im, -1.0)
        delta_re, delta_im = right_apply(tables, back_re.astype(jnp.bfloat16), back_im.astype(jnp.bfloat16), -1.0)
        grad_re = lax.optimization_barrier(jnp.sum(probe_re * delta_re + probe_im * delta_im, axis=0))
        grad_im = lax.optimization_barrier(jnp.sum(probe_re * delta_im - probe_im * delta_re, axis=0))
        term_re = patch_re * delta_re + patch_im * delta_im
        term_im = patch_re * delta_im - patch_im * delta_re
        grad_image = jnp.stack([grad_re, grad_im])
        grad_block = grad_image.reshape(2, 4, PIECE_R, 2, PIECE_C).transpose(1, 3, 0, 2, 4)
        current = lax.dynamic_slice(summed_terms, corner_at, (4, 2, 2, PIECE_R, PIECE_C))
        summed_terms = lax.dynamic_update_slice(summed_terms, current + grad_block, corner_at)
        light_at = (piece_row, piece_col, anchor, anchor)
        current_light = lax.dynamic_slice(weight, light_at, (4, 2, PIECE_R, PIECE_C))
        weight = lax.dynamic_update_slice(weight, current_light + light_blocks, light_at)
        return ((probe_sum + jnp.stack([term_re, term_im], axis=1), summed_terms, weight), None)
    start_state = (jnp.zeros((MODES, 2, PATCH, PATCH), jnp.float32), jnp.zeros((GRID_R, GRID_C, 2, PIECE_R, PIECE_C), jnp.float32), jnp.zeros((GRID_R, GRID_C, PIECE_R, PIECE_C), jnp.float32))
    final_state, unused = lax.scan(one_slot, start_state, live_slots)
    probe_grad, summed_terms, weight = final_state
    new_grid = object_grid + summed_terms / (weight[:, :, None] + object_floor)
    object_new = new_grid.reshape(DEV_ROWS, TILE_R, DEV_COLS, TILE_C, 2, PIECE_R, PIECE_C)
    object_new = object_new.transpose(0, 2, 1, 3, 4, 5, 6).reshape(PIECES, 2, PIECE_R, PIECE_C)
    return (object_new, probe_grad)
```

```python
import math

import jax
import jax.numpy as jnp
import numpy as np
from jax import lax
from jax.experimental import pallas as pl
from jax.experimental.pallas import tpu as pltpu
from jax.sharding import PartitionSpec as P

DEV_COLS = 8
TILE_R = 6
TILE_C = 4
SIDE = 256
PIECE_R = 64
PIECE_C = 128
N_MODE = 4
N_TILE = 64
SUB = PIECE_R // N_MODE

far_floor = 0.1
object_floor = 0.1

F32 = jnp.float32
BF16 = jnp.bfloat16
ANY = pl.BlockSpec(memory_space=pl.ANY)
SMEM = pl.BlockSpec(memory_space=pltpu.SMEM)
VMEM = pl.BlockSpec(memory_space=pltpu.VMEM)


def shifted(block, axis, distance):
    devices = range(lax.axis_size(axis))
    route = [(i - distance, i) for i in devices if i - distance in devices]
    return lax.ppermute(block, axis, route)


def turned(block, distance):
    return lax.ppermute(block, "mode", [(i, (i + distance) % N_MODE) for i in range(N_MODE)])


def core_swap(block):
    return lax.ppermute(block, "tile", [(d, d ^ 1) for d in range(N_TILE)])


def fourier_blocks():
    indices = np.arange(SIDE)
    phases = (indices[:, None] * indices[None, :] % SIDE) * (2.0 * math.pi / SIDE)
    scaling = 1.0 / math.sqrt(SIDE)
    re = (np.cos(phases) * scaling).astype(np.float32)
    im = (-np.sin(phases) * scaling).astype(np.float32)
    left = np.block([[re, -im], [im, re]])
    right = np.block([[re, im], [-im, re]])
    return jnp.asarray(left.astype(jnp.bfloat16)), jnp.asarray(right.astype(jnp.bfloat16))


def canvas_index(row, col):
    inside = jnp.where(col < TILE_C, row * TILE_C + col, 24 + row)
    below = jnp.where(col < TILE_C, 30 + (row - TILE_R) * TILE_C + col, 42 + row - TILE_R)
    return jnp.where(row < TILE_R, inside, below)


def forward_kernel(info, own, right, low, corner, probe, left_table, right_table,
                   far, patch, p0, p1, p2, p3, power, sems):
    slot = pl.program_id(0)
    mode = pl.program_id(1)

    def piece_copy(s, q, source, index):
        target = patch.at[s, :, pl.ds(PIECE_R * (q // 2), PIECE_R), pl.ds(PIECE_C * (q % 2), PIECE_C)]
        return pltpu.make_async_copy(source.at[index], target, sems.at[s, q])

    @pl.when((slot == 0) & (mode == 0))
    def _():
        for s in range(2):
            for q in range(8):
                row = info[2 * s] + q // 2
                col = info[2 * s + 1] + q % 2
                upper = row < TILE_R
                inner = col < TILE_C

                @pl.when(upper & inner)
                def _():
                    piece_copy(s, q, own, row * TILE_C + col).start()

                @pl.when(upper & jnp.logical_not(inner))
                def _():
                    piece_copy(s, q, right, row).start()

                @pl.when(jnp.logical_not(upper) & inner)
                def _():
                    piece_copy(s, q, low, (row - TILE_R) * TILE_C + col).start()

                @pl.when(jnp.logical_not(upper) & jnp.logical_not(inner))
                def _():
                    piece_copy(s, q, corner, row - TILE_R).start()

    for s in range(2):

        @pl.when((slot == s) & (mode == 0))
        def _():
            for q in range(8):
                piece_copy(s, q, own, 0).wait()

    probe_re, probe_im = probe[0, 0], probe[0, 1]
    patch_re, patch_im = patch[slot, 0], patch[slot, 1]
    exit_re = (probe_re * patch_re - probe_im * patch_im).astype(BF16)
    exit_im = (probe_re * patch_im + probe_im * patch_re).astype(BF16)
    half = jnp.dot(left_table[...], jnp.concatenate([exit_re, exit_im], axis=0),
                   preferred_element_type=F32).astype(BF16)
    half = jnp.concatenate([half[:SIDE], half[SIDE:]], axis=1)
    both = jnp.dot(half, right_table[...], preferred_element_type=F32)
    far_re, far_im = both[:, :SIDE], both[:, SIDE:]
    far[0, 0, 0] = far_re
    far[0, 0, 1] = far_im
    local = far_re * far_re + far_im * far_im

    @pl.when(mode == 0)
    def _():
        power[...] = local

    @pl.when(mode > 0)
    def _():
        power[...] += local

    @pl.when(mode == 2)
    def _():
        me = info[5]
        for j, out in enumerate((p0, p1, p2, p3)):
            start = pl.multiple_of(lax.rem(me + j, N_MODE) * 64, 64)
            out[slot] = power[pl.ds(start, 64), :]


def forward(info, own, right, low, corner, probe, tables):
    full = lambda *shape: pl.BlockSpec(shape, lambda s, k: (0,) * len(shape))
    return pl.pallas_call(
        forward_kernel,
        grid=(2, 3),
        in_specs=[SMEM, ANY, ANY, ANY, ANY,
                  pl.BlockSpec((1, 2, SIDE, SIDE), lambda s, k: (k, 0, 0, 0)),
                  full(512, 512), full(512, 512)],
        out_specs=[pl.BlockSpec((1, 1, 2, SIDE, SIDE), lambda s, k: (s, k, 0, 0, 0)),
                   full(2, 2, SIDE, SIDE)] + [full(2, 64, SIDE)] * 4,
        out_shape=[jax.ShapeDtypeStruct((2, 3, 2, SIDE, SIDE), F32),
                   jax.ShapeDtypeStruct((2, 2, SIDE, SIDE), F32)]
        + [jax.ShapeDtypeStruct((2, 64, SIDE), F32)] * 4,
        scratch_shapes=[pltpu.VMEM((SIDE, SIDE), F32), pltpu.SemaphoreType.DMA((2, 8))],
        compiler_params=pltpu.CompilerParams(vmem_limit_bytes=32 * 1024 * 1024),
        cost_estimate=pl.CostEstimate(flops=1700000000, bytes_accessed=12000000, transcendentals=0),
        name="forward",
    )(info, own, right, low, corner, probe, *tables)


def backward_kernel(info, far, probe, patch, f0, f1, f2, f3, left_table, right_table,
                    mine, theirs, g0, g1, g2, g3, factor, grad):
    mode = pl.program_id(0)
    slot = pl.program_id(1)
    me = info[5]
    core = info[6]

    @pl.when((slot == 0) & (mode == 0))
    def _():
        for j, part in enumerate((f0, f1, f2, f3)):
            start = pl.multiple_of(lax.rem(me + N_MODE - j, N_MODE) * 64, 64)
            factor[:, pl.ds(start, 64), :] = part[...]

    scale = factor[slot]
    change_re = (scale * far[0, 0, 0]).astype(BF16)
    change_im = (scale * far[0, 0, 1]).astype(BF16)
    back = jnp.dot(right_table[...], jnp.concatenate([change_re, change_im], axis=0),
                   preferred_element_type=F32).astype(BF16)
    back = jnp.concatenate([back[:SIDE], back[SIDE:]], axis=1)
    both = jnp.dot(back, left_table[...], preferred_element_type=F32)
    delta_re, delta_im = both[:, :SIDE], both[:, SIDE:]
    patch_re, patch_im = patch[slot, 0], patch[slot, 1]
    term_re = patch_re * delta_re + patch_im * delta_im
    term_im = patch_re * delta_im - patch_im * delta_re
    first = core == 0
    own_term = jnp.where(first, term_re, term_im)
    other_term = jnp.where(first, term_im, term_re)

    @pl.when(slot == 0)
    def _():
        mine[0] = own_term
        theirs[0] = other_term

    @pl.when(slot == 1)
    def _():
        mine[0] += own_term
        theirs[0] += other_term

    probe_re, probe_im = probe[0, 0], probe[0, 1]
    grad_re = probe_re * delta_re + probe_im * delta_im
    grad_im = probe_re * delta_im - probe_im * delta_re

    @pl.when(mode == 0)
    def _():
        grad[slot, 0] = grad_re
        grad[slot, 1] = grad_im

    @pl.when(mode > 0)
    def _():
        grad[slot, 0] += grad_re
        grad[slot, 1] += grad_im

    @pl.when(mode == 2)
    def _():
        for j, out in enumerate((g0, g1, g2, g3)):
            base = lax.rem(me + j, N_MODE) * SUB
            for q in range(8):
                start = pl.multiple_of(base + PIECE_R * (q // 2), SUB)
                for channel in range(2):
                    out[slot, q, channel] = grad[
                        slot, channel, pl.ds(start, SUB),
                        PIECE_C * (q % 2):PIECE_C * (q % 2 + 1)]


def backward(info, far, probe, patch, factors, tables):
    full = lambda *shape: pl.BlockSpec(shape, lambda k, s: (0,) * len(shape))
    return pl.pallas_call(
        backward_kernel,
        grid=(3, 2),
        in_specs=[SMEM,
                  pl.BlockSpec((1, 1, 2, SIDE, SIDE), lambda k, s: (s, k, 0, 0, 0)),
                  pl.BlockSpec((1, 2, SIDE, SIDE), lambda k, s: (k, 0, 0, 0)),
                  full(2, 2, SIDE, SIDE)] + [full(2, 64, SIDE)] * 4
        + [full(512, 512), full(512, 512)],
        out_specs=[pl.BlockSpec((1, SIDE, SIDE), lambda k, s: (k, 0, 0))] * 2
        + [full(2, 8, 2, SUB, PIECE_C)] * 4,
        out_shape=[jax.ShapeDtypeStruct((3, SIDE, SIDE), F32)] * 2
        + [jax.ShapeDtypeStruct((2, 8, 2, SUB, PIECE_C), F32)] * 4,
        scratch_shapes=[pltpu.VMEM((2, SIDE, SIDE), F32), pltpu.VMEM((2, 2, SIDE, SIDE), F32)],
        compiler_params=pltpu.CompilerParams(vmem_limit_bytes=32 * 1024 * 1024),
        cost_estimate=pl.CostEstimate(flops=1700000000, bytes_accessed=12000000, transcendentals=0),
        name="backward",
    )(info, far, probe, patch, *factors, *tables)


def scatter_kernel(info, g0, g1, g2, g3, own, right, low, corner, canvas):
    canvas[...] = jnp.zeros_like(canvas)
    for s in range(2):
        for q in range(8):
            index = canvas_index(info[2 * s] + q // 2, info[2 * s + 1] + q % 2)
            canvas[index] += (g0[s, q] + g1[s, q]) + (g2[s, q] + g3[s, q])
    own[...] = canvas[:24]
    right[...] = canvas[24:30]
    low[...] = canvas[30:42]
    corner[...] = canvas[42:45]


def scatter(info, parts):
    pieces = lambda n: jax.ShapeDtypeStruct((n, 2, SUB, PIECE_C), F32)
    return pl.pallas_call(
        scatter_kernel,
        in_specs=[SMEM] + [VMEM] * 4,
        out_specs=[VMEM] * 4,
        out_shape=[pieces(24), pieces(6), pieces(12), pieces(3)],
        scratch_shapes=[pltpu.VMEM((45, 2, SUB, PIECE_C), F32)],
        cost_estimate=pl.CostEstimate(flops=1000000, bytes_accessed=2000000, transcendentals=0),
        name="scatter",
    )(info, *parts)


def weight_kernel(info, from_left, from_above, from_corner, light, weight):
    weight[...] = jnp.zeros_like(weight)
    sources = ((info, 0, 0), (from_left, 0, TILE_C), (from_above, TILE_R, 0),
               (from_corner, TILE_R, TILE_C))
    for source, down, across in sources:
        for s in range(2):
            top = source[2 * s] - down
            left = source[2 * s + 1] - across
            live = s < source[4]
            for q in range(8):
                row = top + q // 2
                col = left + q % 2
                inside = (row >= 0) & (row < TILE_R) & (col >= 0) & (col < TILE_C)

                @pl.when(live & inside)
                def _():
                    weight[row * TILE_C + col] += light[
                        q // 2, :, PIECE_C * (q % 2):PIECE_C * (q % 2 + 1)]


def weights(info, neighbours, light):
    return pl.pallas_call(
        weight_kernel,
        in_specs=[SMEM] * 4 + [VMEM],
        out_specs=VMEM,
        out_shape=jax.ShapeDtypeStruct((TILE_R * TILE_C, SUB, PIECE_C), F32),
        cost_estimate=pl.CostEstimate(flops=1000000, bytes_accessed=500000, transcendentals=0),
        name="weights",
    )(info, *neighbours, light)


def update_kernel(info, pieces, own, right, low, corner, weight, new, old, sem):
    start = pl.multiple_of(info[5] * SUB, SUB)
    fetch = pltpu.make_async_copy(pieces.at[:, :, pl.ds(start, SUB), :], old, sem)
    fetch.start()
    fetch.wait()
    for p in range(TILE_R * TILE_C):
        row, col = p // TILE_C, p % TILE_C
        total = own[p]
        if row < 3:
            total = total + low[p]
        if col == 0:
            total = total + right[row]
        if row < 3 and col == 0:
            total = total + corner[row]
        new[p] = old[p] + total / (weight[p] + object_floor)[None]


def update(info, pieces, own, right, low, corner, weight):
    shape = (TILE_R * TILE_C, 2, SUB, PIECE_C)
    return pl.pallas_call(
        update_kernel,
        in_specs=[SMEM, ANY] + [VMEM] * 5,
        out_specs=VMEM,
        out_shape=jax.ShapeDtypeStruct(shape, F32),
        scratch_shapes=[pltpu.VMEM(shape, F32), pltpu.SemaphoreType.DMA],
        cost_estimate=pl.CostEstimate(flops=1000000, bytes_accessed=2000000, transcendentals=0),
        name="update",
    )(info, pieces, own, right, low, corner, weight)


def join_pieces_kernel(info, n0, n1, n2, n3, out, sems):
    copies = []
    for j, part in enumerate((n0, n1, n2, n3)):
        start = pl.multiple_of(lax.rem(info[5] + N_MODE - j, N_MODE) * SUB, SUB)
        copies.append(pltpu.make_async_copy(part, out.at[:, :, pl.ds(start, SUB), :], sems.at[j]))
    for copy in copies:
        copy.start()
    for copy in copies:
        copy.wait()


def join_pieces(info, parts):
    return pl.pallas_call(
        join_pieces_kernel,
        in_specs=[SMEM] + [ANY] * 4,
        out_specs=ANY,
        out_shape=jax.ShapeDtypeStruct((TILE_R * TILE_C, 2, PIECE_R, PIECE_C), F32),
        scratch_shapes=[pltpu.SemaphoreType.DMA((4,))],
        cost_estimate=pl.CostEstimate(flops=0, bytes_accessed=3000000, transcendentals=0),
        name="join_pieces",
    )(info, *parts)


def join_channels_kernel(info, mine, theirs, out, sems):
    core = info[6]
    copies = [pltpu.make_async_copy(mine, out.at[:, core], sems.at[0]),
              pltpu.make_async_copy(theirs, out.at[:, 1 - core], sems.at[1])]
    for copy in copies:
        copy.start()
    for copy in copies:
        copy.wait()


def join_channels(info, mine, theirs):
    return pl.pallas_call(
        join_channels_kernel,
        in_specs=[SMEM, ANY, ANY],
        out_specs=ANY,
        out_shape=jax.ShapeDtypeStruct((3, 2, SIDE, SIDE), F32),
        scratch_shapes=[pltpu.SemaphoreType.DMA((2,))],
        cost_estimate=pl.CostEstimate(flops=0, bytes_accessed=3000000, transcendentals=0),
        name="join_channels",
    )(info, mine, theirs)


def body(object_pieces, probe_modes, intensity, positions, counts):
    tile_index = lax.axis_index("tile")
    mode_index = lax.axis_index("mode")
    tables = fourier_blocks()
    tile_grid = object_pieces.reshape(TILE_R, TILE_C, 2, PIECE_R, PIECE_C)
    low = shifted(object_pieces[:12], "tile", -DEV_COLS)
    right = shifted(tile_grid[:, 0], "tile", -1)
    corner = shifted(tile_grid[:3, 0], "tile", -DEV_COLS - 1)

    dev_row = tile_index // DEV_COLS
    dev_col = tile_index % DEV_COLS
    rows = jnp.clip(positions[:, 0] // PIECE_R - dev_row * TILE_R, 0, TILE_R - 1)
    cols = jnp.clip(positions[:, 1] // PIECE_C - dev_col * TILE_C, 0, TILE_C - 1)
    info = jnp.stack([rows[0], cols[0], rows[1], cols[1], counts[0], mode_index, tile_index % 2,
                      tile_index]).astype(jnp.int32)
    neighbours = [shifted(info, "tile", d) for d in (1, DEV_COLS, DEV_COLS + 1)]

    light_local = jnp.sum(probe_modes * probe_modes, axis=(0, 1))
    light_parts = light_local.reshape(4, N_MODE, SUB, SIDE).transpose(1, 0, 2, 3)
    light = lax.psum_scatter(light_parts, "mode", scatter_dimension=0, tiled=True)[0]
    weight = weights(info, neighbours, light)

    far, patch, *powers = forward(info, object_pieces, right, low, corner, probe_modes, tables)
    received = [turned(powers[j], j) for j in (1, 2, 3)]
    power = (powers[0] + received[0]) + (received[1] + received[2])
    own_intensity = lax.dynamic_slice_in_dim(intensity, mode_index * 64, 64, axis=1)
    live = (jnp.arange(2, dtype=jnp.int32) < counts[0]).astype(F32)
    factor = live[:, None, None] * (jnp.sqrt(own_intensity) / jnp.sqrt(power + far_floor) - 1.0)
    factors = [factor] + [turned(factor, j) for j in (1, 2, 3)]

    mine, theirs, *grads = backward(info, far, probe_modes, patch, factors, tables)

    summed = mine + core_swap(theirs)
    groups = [[y * 16 + z * 2 + c for y in range(4) for z in range(8)] for c in range(2)]
    pieces = lax.all_to_all(summed.reshape(32, 24, SIDE), "tile", 0, 0, axis_index_groups=groups, tiled=True)
    share = jnp.sum(pieces, axis=0)
    gathered = lax.all_to_all(jnp.broadcast_to(share[None], (32, 24, SIDE)), "tile", 0, 0,
                              axis_index_groups=groups, tiled=True).reshape(3, SIDE, SIDE)
    probe_grad = join_channels(info, gathered, core_swap(gathered))

    parts = [grads[0]] + [turned(grads[j], j) for j in (1, 2, 3)]
    own, to_right, to_low, to_corner = scatter(info, parts)
    from_above = shifted(to_low, "tile", DEV_COLS)
    from_left = shifted(to_right, "tile", 1)
    from_corner = shifted(to_corner, "tile", DEV_COLS + 1)
    new = update(info, object_pieces, own, from_left, from_above, from_corner, weight)
    new_parts = [new] + [turned(new, j) for j in (1, 2, 3)]
    return (join_pieces(info, new_parts), probe_grad)


def solution(mesh):
    return jax.shard_map(
        body,
        mesh=mesh,
        in_specs=(
            P("tile", None, None, None),
            P("mode", None, None, None),
            P("tile", None, None),
            P("tile", None),
            P("tile"),
        ),
        out_specs=(P("tile", None, None, None), P("mode", None, None, None)),
        check_vma=False,
    )
```

```python
import math

import jax
import jax.numpy as jnp
import numpy as np
from jax import lax
from jax.experimental import pallas as pl
from jax.experimental.pallas import tpu as pltpu
from jax.sharding import PartitionSpec as P

DEV_COLS = 8
TILE_R = 6
TILE_C = 4
SIDE = 256
PIECE_R = 64
PIECE_C = 128
N_MODE = 4
N_TILE = 64
SUB = PIECE_R // N_MODE
N_CHIP = N_TILE // 2
PART = 3 * SIDE // N_CHIP
VMEM_BYTES = 56 * 1024 * 1024

far_floor = 0.1
object_floor = 0.1

F32 = jnp.float32
BF16 = jnp.bfloat16
ANY = pl.BlockSpec(memory_space=pl.ANY)
SMEM = pl.BlockSpec(memory_space=pltpu.SMEM)
VMEM = pl.BlockSpec(memory_space=pltpu.VMEM)


def shifted(block, axis, distance):
    devices = range(lax.axis_size(axis))
    route = [(i - distance, i) for i in devices if i - distance in devices]
    return lax.ppermute(block, axis, route)


def turned(block, distance):
    return lax.ppermute(block, "mode", [(i, (i + distance) % N_MODE) for i in range(N_MODE)])


def core_swap(block):
    return lax.ppermute(block, "tile", [(d, d ^ 1) for d in range(N_TILE)])


def fourier_blocks():
    indices = np.arange(SIDE)
    phases = (indices[:, None] * indices[None, :] % SIDE) * (2.0 * math.pi / SIDE)
    scaling = 1.0 / math.sqrt(SIDE)
    re = (np.cos(phases) * scaling).astype(np.float32)
    im = (-np.sin(phases) * scaling).astype(np.float32)
    left = np.block([[re, -im], [im, re]])
    right = np.block([[re, im], [-im, re]])
    return jnp.asarray(left.astype(jnp.bfloat16)), jnp.asarray(right.astype(jnp.bfloat16))


def canvas_index(row, col):
    inside = jnp.where(col < TILE_C, row * TILE_C + col, 24 + row)
    below = jnp.where(col < TILE_C, 30 + (row - TILE_R) * TILE_C + col, 42 + row - TILE_R)
    return jnp.where(row < TILE_R, inside, below)


def forward_kernel(info, own, right, b0, b1, b2, b3, probe, left_table, right_table,
                   far, patch, p0, p1, p2, p3, power, sems):
    mode = pl.program_id(0)

    def piece_copy(s, q, source, index):
        target = patch.at[s, :, pl.ds(PIECE_R * (q // 2), PIECE_R), pl.ds(PIECE_C * (q % 2), PIECE_C)]
        return pltpu.make_async_copy(source.at[index], target, sems.at[s, q])

    @pl.when(mode == 0)
    def _():
        for s in range(2):
            for q in range(8):
                row = info[2 * s] + q // 2
                col = info[2 * s + 1] + q % 2
                upper = row < TILE_R
                inner = col < TILE_C

                @pl.when(upper & inner)
                def _():
                    piece_copy(s, q, own, row * TILE_C + col).start()

                @pl.when(upper & jnp.logical_not(inner))
                def _():
                    piece_copy(s, q, right, row).start()

                @pl.when(jnp.logical_not(upper))
                def _():
                    below = jnp.where(inner, (row - TILE_R) * TILE_C + col, 12 + row - TILE_R)
                    for j, source in enumerate((b0, b1, b2, b3)):
                        start = lax.rem(info[5] + N_MODE - j, N_MODE) * SUB + PIECE_R * (q // 2)
                        target = patch.at[s, :, pl.ds(pl.multiple_of(start, SUB), SUB),
                                          pl.ds(PIECE_C * (q % 2), PIECE_C)]
                        pltpu.make_async_copy(source.at[below], target, sems.at[s, q]).start()

        for s in range(2):
            for q in range(8):
                piece_copy(s, q, own, 0).wait()

    probe_re, probe_im = probe[0, 0], probe[0, 1]
    for s in range(2):
        patch_re, patch_im = patch[s, 0], patch[s, 1]
        exit_re = (probe_re * patch_re - probe_im * patch_im).astype(BF16)
        exit_im = (probe_re * patch_im + probe_im * patch_re).astype(BF16)
        half = jnp.dot(left_table[...], jnp.concatenate([exit_re, exit_im], axis=0),
                       preferred_element_type=F32).astype(BF16)
        half = jnp.concatenate([half[:SIDE], half[SIDE:]], axis=1)
        both = jnp.dot(half, right_table[...], preferred_element_type=F32)
        far_re, far_im = both[:, :SIDE], both[:, SIDE:]
        far[s, 0, 0] = far_re
        far[s, 0, 1] = far_im
        local = far_re * far_re + far_im * far_im
        power[s] = jnp.where(mode == 0, local, power[s] + local)

    @pl.when(mode == 2)
    def _():
        for j, out in enumerate((p0, p1, p2, p3)):
            start = pl.multiple_of(lax.rem(info[5] + j, N_MODE) * 64, 64)
            out[...] = power[:, pl.ds(start, 64), :]


def forward(info, own, right, below, probe, tables):
    full = lambda *shape: pl.BlockSpec(shape, lambda k: (0,) * len(shape))
    return pl.pallas_call(
        forward_kernel,
        grid=(3,),
        in_specs=[SMEM] + [ANY] * 6 + [
                  pl.BlockSpec((1, 2, SIDE, SIDE), lambda k: (k, 0, 0, 0)),
                  full(512, 512), full(512, 512)],
        out_specs=[pl.BlockSpec((2, 1, 2, SIDE, SIDE), lambda k: (0, k, 0, 0, 0)),
                   full(2, 2, SIDE, SIDE)] + [full(2, 64, SIDE)] * 4,
        out_shape=[jax.ShapeDtypeStruct((2, 3, 2, SIDE, SIDE), F32),
                   jax.ShapeDtypeStruct((2, 2, SIDE, SIDE), F32)]
        + [jax.ShapeDtypeStruct((2, 64, SIDE), F32)] * 4,
        scratch_shapes=[pltpu.VMEM((2, SIDE, SIDE), F32), pltpu.SemaphoreType.DMA((2, 8))],
        compiler_params=pltpu.CompilerParams(vmem_limit_bytes=VMEM_BYTES),
        cost_estimate=pl.CostEstimate(flops=1700000000, bytes_accessed=12000000, transcendentals=0),
        name="forward",
    )(info, own, right, *below, probe, *tables)


def backward_kernel(info, far, probe, patch, f0, f1, f2, f3, left_table, right_table,
                    mine, theirs, g0, g1, g2, g3, factor, grad):
    mode = pl.program_id(0)
    me = info[5]
    first = info[6] == 0

    @pl.when(mode == 0)
    def _():
        for j, part in enumerate((f0, f1, f2, f3)):
            start = pl.multiple_of(lax.rem(me + N_MODE - j, N_MODE) * 64, 64)
            factor[:, pl.ds(start, 64), :] = part[...]

    probe_re, probe_im = probe[0, 0], probe[0, 1]
    own_term, other_term = 0.0, 0.0
    for s in range(2):
        change_re = (factor[s] * far[s, 0, 0]).astype(BF16)
        change_im = (factor[s] * far[s, 0, 1]).astype(BF16)
        back = jnp.dot(right_table[...], jnp.concatenate([change_re, change_im], axis=0),
                       preferred_element_type=F32).astype(BF16)
        back = jnp.concatenate([back[:SIDE], back[SIDE:]], axis=1)
        both = jnp.dot(back, left_table[...], preferred_element_type=F32)
        delta_re, delta_im = both[:, :SIDE], both[:, SIDE:]
        patch_re, patch_im = patch[s, 0], patch[s, 1]
        term_re = patch_re * delta_re + patch_im * delta_im
        term_im = patch_re * delta_im - patch_im * delta_re
        own_term += jnp.where(first, term_re, term_im)
        other_term += jnp.where(first, term_im, term_re)
        grad_re = probe_re * delta_re + probe_im * delta_im
        grad_im = probe_re * delta_im - probe_im * delta_re
        grad[s, 0] = jnp.where(mode == 0, grad_re, grad[s, 0] + grad_re)
        grad[s, 1] = jnp.where(mode == 0, grad_im, grad[s, 1] + grad_im)
    mine[0] = own_term
    theirs[0] = other_term

    @pl.when(mode == 2)
    def _():
        for j, out in enumerate((g0, g1, g2, g3)):
            base = lax.rem(me + j, N_MODE) * SUB
            for q in range(8):
                start = pl.multiple_of(base + PIECE_R * (q // 2), SUB)
                out[:, q] = grad[:, :, pl.ds(start, SUB), PIECE_C * (q % 2):PIECE_C * (q % 2 + 1)]


def backward(info, far, probe, patch, factors, tables):
    full = lambda *shape: pl.BlockSpec(shape, lambda k: (0,) * len(shape))
    return pl.pallas_call(
        backward_kernel,
        grid=(3,),
        in_specs=[SMEM,
                  pl.BlockSpec((2, 1, 2, SIDE, SIDE), lambda k: (0, k, 0, 0, 0)),
                  pl.BlockSpec((1, 2, SIDE, SIDE), lambda k: (k, 0, 0, 0)),
                  full(2, 2, SIDE, SIDE)] + [full(2, 64, SIDE)] * 4
        + [full(512, 512), full(512, 512)],
        out_specs=[pl.BlockSpec((1, SIDE, SIDE), lambda k: (k, 0, 0))] * 2
        + [full(2, 8, 2, SUB, PIECE_C)] * 4,
        out_shape=[jax.ShapeDtypeStruct((3, SIDE, SIDE), F32)] * 2
        + [jax.ShapeDtypeStruct((2, 8, 2, SUB, PIECE_C), F32)] * 4,
        scratch_shapes=[pltpu.VMEM((2, SIDE, SIDE), F32), pltpu.VMEM((2, 2, SIDE, SIDE), F32)],
        compiler_params=pltpu.CompilerParams(vmem_limit_bytes=VMEM_BYTES),
        cost_estimate=pl.CostEstimate(flops=1700000000, bytes_accessed=12000000, transcendentals=0),
        name="backward",
    )(info, far, probe, patch, *factors, *tables)


def scatter_kernel(info, g0, g1, g2, g3, own, right, low, corner, canvas):
    canvas[...] = jnp.zeros_like(canvas)
    for s in range(2):
        for q in range(8):
            index = canvas_index(info[2 * s] + q // 2, info[2 * s + 1] + q % 2)
            canvas[index] += (g0[s, q] + g1[s, q]) + (g2[s, q] + g3[s, q])
    own[...] = canvas[:24]
    rows = lax.broadcasted_iota(jnp.int32, (2, SUB, PIECE_C), 1)
    note = jnp.zeros((2, SUB, PIECE_C), F32)
    for i in range(5):
        note = jnp.where(rows == i, info[i].astype(F32), note)
    for out, begin, size in ((right, 24, 6), (low, 30, 12), (corner, 42, 3)):
        out[:size] = canvas[begin:begin + size]
        out[size] = note


def scatter(info, parts):
    pieces = lambda n: jax.ShapeDtypeStruct((n, 2, SUB, PIECE_C), F32)
    return pl.pallas_call(
        scatter_kernel,
        in_specs=[SMEM] + [VMEM] * 4,
        out_specs=[VMEM] * 4,
        out_shape=[pieces(24), pieces(7), pieces(13), pieces(4)],
        scratch_shapes=[pltpu.VMEM((45, 2, SUB, PIECE_C), F32)],
        cost_estimate=pl.CostEstimate(flops=1000000, bytes_accessed=2000000, transcendentals=0),
        name="scatter",
    )(info, *parts)


def update_kernel(info, pieces, own, right, low, corner, light, new, old, weight, notes, sems):
    start = pl.multiple_of(info[5] * SUB, SUB)
    fetch = pltpu.make_async_copy(pieces.at[:, :, pl.ds(start, SUB), :], old, sems.at[3])
    fetch.start()
    reads = [pltpu.make_async_copy(part.at[size, 0], notes.at[n], sems.at[n])
             for n, (part, size) in enumerate(((right, 6), (low, 12), (corner, 3)))]
    for read in reads:
        read.start()
    weight[...] = jnp.zeros_like(weight)

    def add_slot(top, left, live, classes):
        @pl.when(live)
        def _():
            for q in classes:
                row = top + q // 2
                col = left + q % 2

                @pl.when((row >= 0) & (row < TILE_R) & (col >= 0) & (col < TILE_C))
                def _():
                    weight[row * TILE_C + col] += light[
                        q // 2, :, PIECE_C * (q % 2):PIECE_C * (q % 2 + 1)]

    for s in range(2):
        add_slot(info[2 * s], info[2 * s + 1], s < info[4], range(8))
    for read in reads:
        read.wait()
    for n, (down, across, classes) in enumerate((
            (0, TILE_C, (1, 3, 5, 7)), (TILE_R, 0, (2, 3, 4, 5, 6, 7)), (TILE_R, TILE_C, (3, 5, 7)))):
        for s in range(2):
            top = notes[n, 2 * s, 0].astype(jnp.int32) - down
            left = notes[n, 2 * s + 1, 0].astype(jnp.int32) - across
            live = s < notes[n, 4, 0].astype(jnp.int32)
            add_slot(top, left, live & (top > -4) & (left > -2), classes)
    fetch.wait()
    for p in range(TILE_R * TILE_C):
        row, col = p // TILE_C, p % TILE_C
        total = own[p]
        if row < 3:
            total = total + low[p]
        if col == 0:
            total = total + right[row]
        if row < 3 and col == 0:
            total = total + corner[row]
        new[p] = old[p] + total / (weight[p] + object_floor)[None]


def update(info, pieces, own, right, low, corner, light):
    shape = (TILE_R * TILE_C, 2, SUB, PIECE_C)
    return pl.pallas_call(
        update_kernel,
        in_specs=[SMEM, ANY] + [VMEM] * 5,
        out_specs=VMEM,
        out_shape=jax.ShapeDtypeStruct(shape, F32),
        scratch_shapes=[pltpu.VMEM(shape, F32), pltpu.VMEM((TILE_R * TILE_C, SUB, PIECE_C), F32),
                        pltpu.SMEM((3, SUB, PIECE_C), F32), pltpu.SemaphoreType.DMA((4,))],
        compiler_params=pltpu.CompilerParams(vmem_limit_bytes=VMEM_BYTES),
        cost_estimate=pl.CostEstimate(flops=1000000, bytes_accessed=2000000, transcendentals=0),
        name="update",
    )(info, pieces, own, right, low, corner, light)


def join_pieces_kernel(info, n0, n1, n2, n3, out):
    for j, part in enumerate((n0, n1, n2, n3)):
        start = pl.multiple_of(lax.rem(info[5] + N_MODE - j, N_MODE) * SUB, SUB)
        out[:, :, pl.ds(start, SUB), :] = part[...]


def join_pieces(info, parts):
    block = lambda rows: pl.BlockSpec((6, 2, rows, PIECE_C), lambda i: (i, 0, 0, 0))
    return pl.pallas_call(
        join_pieces_kernel,
        grid=(4,),
        in_specs=[SMEM] + [block(SUB)] * 4,
        out_specs=block(PIECE_R),
        out_shape=jax.ShapeDtypeStruct((TILE_R * TILE_C, 2, PIECE_R, PIECE_C), F32),
        compiler_params=pltpu.CompilerParams(vmem_limit_bytes=VMEM_BYTES),
        cost_estimate=pl.CostEstimate(flops=0, bytes_accessed=3000000, transcendentals=0),
        name="join_pieces",
    )(info, *parts)


def join_channels_kernel(info, mine, theirs, out):
    core = info[6]
    out[0, core] = mine[0]
    out[0, 1 - core] = theirs[0]


def join_channels(info, mine, theirs):
    block = pl.BlockSpec((1, SIDE, SIDE), lambda k: (k, 0, 0))
    return pl.pallas_call(
        join_channels_kernel,
        grid=(3,),
        in_specs=[SMEM, block, block],
        out_specs=pl.BlockSpec((1, 2, SIDE, SIDE), lambda k: (k, 0, 0, 0)),
        out_shape=jax.ShapeDtypeStruct((3, 2, SIDE, SIDE), F32),
        compiler_params=pltpu.CompilerParams(vmem_limit_bytes=VMEM_BYTES),
        cost_estimate=pl.CostEstimate(flops=0, bytes_accessed=3000000, transcendentals=0),
        name="join_channels",
    )(info, mine, theirs)


def body(object_pieces, probe_modes, intensity, positions, counts):
    tile_index = lax.axis_index("tile")
    mode_index = lax.axis_index("mode")
    tables = fourier_blocks()
    tile_grid = object_pieces.reshape(TILE_R, TILE_C, 2, PIECE_R, PIECE_C)
    own_rows = lax.dynamic_slice_in_dim(object_pieces[:12], mode_index * SUB, SUB, axis=2)
    low = shifted(own_rows, "tile", -DEV_COLS)
    corner = shifted(own_rows[::TILE_C], "tile", -DEV_COLS - 1)
    right = shifted(tile_grid[:, 0], "tile", -1)
    below = jnp.concatenate([low, corner], axis=0)
    dev_row = tile_index // DEV_COLS
    dev_col = tile_index % DEV_COLS
    rows = jnp.clip(positions[:, 0] // PIECE_R - dev_row * TILE_R, 0, TILE_R - 1)
    cols = jnp.clip(positions[:, 1] // PIECE_C - dev_col * TILE_C, 0, TILE_C - 1)
    info = jnp.stack([rows[0], cols[0], rows[1], cols[1], counts[0], mode_index,
                      tile_index % 2, tile_index]).astype(jnp.int32)
    below = [below] + [turned(below, j) for j in (1, 2, 3)]

    light_local = jnp.sum(probe_modes * probe_modes, axis=(0, 1))
    light_parts = light_local.reshape(4, N_MODE, SUB, SIDE).transpose(1, 0, 2, 3)
    light = lax.psum_scatter(light_parts, "mode", scatter_dimension=0, tiled=True)
    light, right = lax.optimization_barrier((light, right))

    far, patch, *powers = forward(info, object_pieces, right, below, probe_modes, tables)
    received = [turned(powers[j], j) for j in (1, 2, 3)]
    power = (powers[0] + received[0]) + (received[1] + received[2])
    own_intensity = lax.dynamic_slice_in_dim(intensity, mode_index * 64, 64, axis=1)
    live = (jnp.arange(2, dtype=jnp.int32) < counts[0]).astype(F32)
    factor = live[:, None, None] * (jnp.sqrt(own_intensity) / jnp.sqrt(power + far_floor) - 1.0)
    factors = [factor] + [turned(factor, j) for j in (1, 2, 3)]

    mine, theirs, *grads = backward(info, far, probe_modes, patch, factors, tables)

    parts = [grads[0]] + [turned(grads[j], j) for j in (1, 2, 3)]
    groups = [list(range(core, N_TILE, 2)) for core in range(2)]
    exchange = lambda blocks: lax.all_to_all(
        blocks, "tile", 0, 0, axis_index_groups=groups, tiled=True)
    summed = mine + core_swap(theirs)
    own, to_right, to_low, to_corner = scatter(info, parts)
    summed, own = lax.optimization_barrier((summed, own))
    pieces = exchange(summed.reshape(N_CHIP, PART, SIDE))

    from_above = shifted(to_low, "tile", DEV_COLS)
    from_corner = shifted(to_corner, "tile", DEV_COLS + 1)
    from_left = shifted(to_right, "tile", 1)

    new = update(info, object_pieces, own, from_left, from_above, from_corner, light[0])
    share = jnp.sum(pieces, axis=0)
    share, new = lax.optimization_barrier((share, new))
    gathered = exchange(jnp.broadcast_to(share[None], (N_CHIP, PART, SIDE)))
    new_parts = [new] + [turned(new, j) for j in (1, 2, 3)]
    gathered = gathered.reshape(3, SIDE, SIDE)
    probe_grad = join_channels(info, gathered, core_swap(gathered))
    return (join_pieces(info, new_parts), probe_grad)


def solution(mesh):
    return jax.shard_map(
        body,
        mesh=mesh,
        in_specs=(
            P("tile", None, None, None),
            P("mode", None, None, None),
            P("tile", None, None),
            P("tile", None),
            P("tile"),
        ),
        out_specs=(P("tile", None, None, None), P("mode", None, None, None)),
        check_vma=False,
    )
```

```python
import math

import jax
import jax.numpy as jnp
import numpy as np
from jax import lax
from jax.experimental import pallas as pl
from jax.experimental.pallas import tpu as pltpu
from jax.sharding import PartitionSpec as P

DEV_COLS = 8
TILE_R = 6
TILE_C = 4
SIDE = 256
PIECE_R = 64
PIECE_C = 128
N_MODE = 4
N_TILE = 64
SUB = PIECE_R // N_MODE
N_CHIP = N_TILE // 2
PART = 3 * SIDE // N_CHIP
VMEM_BYTES = 56 * 1024 * 1024

far_floor = 0.1
object_floor = 0.1

F32 = jnp.float32
BF16 = jnp.bfloat16
ANY = pl.BlockSpec(memory_space=pl.ANY)
SMEM = pl.BlockSpec(memory_space=pltpu.SMEM)
VMEM = pl.BlockSpec(memory_space=pltpu.VMEM)


def shifted(block, axis, distance):
    devices = range(lax.axis_size(axis))
    route = [(i - distance, i) for i in devices if i - distance in devices]
    return lax.ppermute(block, axis, route)


def turned(block, distance):
    return lax.ppermute(block, "mode", [(i, (i + distance) % N_MODE) for i in range(N_MODE)])


def core_swap(block):
    return lax.ppermute(block, "tile", [(d, d ^ 1) for d in range(N_TILE)])


def fourier_blocks():
    indices = np.arange(SIDE)
    phases = (indices[:, None] * indices[None, :] % SIDE) * (2.0 * math.pi / SIDE)
    scaling = 1.0 / math.sqrt(SIDE)
    re = (np.cos(phases) * scaling).astype(np.float32)
    im = (-np.sin(phases) * scaling).astype(np.float32)
    left = np.block([[re, -im], [im, re]])
    right = np.block([[re, im], [-im, re]])
    return jnp.asarray(left.astype(jnp.bfloat16)), jnp.asarray(right.astype(jnp.bfloat16))


def canvas_index(row, col):
    inside = jnp.where(col < TILE_C, row * TILE_C + col, 24 + row)
    below = jnp.where(col < TILE_C, 30 + (row - TILE_R) * TILE_C + col, 42 + row - TILE_R)
    return jnp.where(row < TILE_R, inside, below)


def forward_kernel(info, own, right, b0, b1, b2, b3, probe, left_table, right_table,
                   far, patch, p0, p1, p2, p3, power, sems):
    mode = pl.program_id(0)

    def piece_copy(s, q, source, index):
        target = patch.at[s, :, pl.ds(PIECE_R * (q // 2), PIECE_R), pl.ds(PIECE_C * (q % 2), PIECE_C)]
        return pltpu.make_async_copy(source.at[index], target, sems.at[s, q])

    @pl.when(mode == 0)
    def _():
        for s in range(2):
            for q in range(8):
                row = info[2 * s] + q // 2
                col = info[2 * s + 1] + q % 2
                upper = row < TILE_R
                inner = col < TILE_C

                @pl.when(upper & inner)
                def _():
                    piece_copy(s, q, own, row * TILE_C + col).start()

                @pl.when(upper & jnp.logical_not(inner))
                def _():
                    piece_copy(s, q, right, row).start()

                @pl.when(jnp.logical_not(upper))
                def _():
                    below = jnp.where(inner, (row - TILE_R) * TILE_C + col, 12 + row - TILE_R)
                    for j, source in enumerate((b0, b1, b2, b3)):
                        start = lax.rem(info[5] + N_MODE - j, N_MODE) * SUB + PIECE_R * (q // 2)
                        target = patch.at[s, :, pl.ds(pl.multiple_of(start, SUB), SUB),
                                          pl.ds(PIECE_C * (q % 2), PIECE_C)]
                        pltpu.make_async_copy(source.at[below], target, sems.at[s, q]).start()

        for s in range(2):
            for q in range(8):
                piece_copy(s, q, own, 0).wait()

    probe_re, probe_im = probe[0, 0], probe[0, 1]
    for s in range(2):
        patch_re, patch_im = patch[s, 0], patch[s, 1]
        exit_re = (probe_re * patch_re - probe_im * patch_im).astype(BF16)
        exit_im = (probe_re * patch_im + probe_im * patch_re).astype(BF16)
        half = jnp.dot(left_table[...], jnp.concatenate([exit_re, exit_im], axis=0),
                       preferred_element_type=F32).astype(BF16)
        half = jnp.concatenate([half[:SIDE], half[SIDE:]], axis=1)
        both = jnp.dot(half, right_table[...], preferred_element_type=F32)
        far_re, far_im = both[:, :SIDE], both[:, SIDE:]
        far[s, 0, 0] = far_re
        far[s, 0, 1] = far_im
        local = far_re * far_re + far_im * far_im
        power[s] = jnp.where(mode == 0, local, power[s] + local)

    @pl.when(mode == 2)
    def _():
        for j, out in enumerate((p0, p1, p2, p3)):
            start = pl.multiple_of(lax.rem(info[5] + j, N_MODE) * 64, 64)
            out[...] = power[:, pl.ds(start, 64), :]


def forward(info, own, right, below, probe, tables):
    full = lambda *shape: pl.BlockSpec(shape, lambda k: (0,) * len(shape))
    return pl.pallas_call(
        forward_kernel,
        grid=(3,),
        in_specs=[SMEM] + [ANY] * 6 + [
                  pl.BlockSpec((1, 2, SIDE, SIDE), lambda k: (k, 0, 0, 0)),
                  full(512, 512), full(512, 512)],
        out_specs=[pl.BlockSpec((2, 1, 2, SIDE, SIDE), lambda k: (0, k, 0, 0, 0)),
                   full(2, 2, SIDE, SIDE)] + [full(2, 64, SIDE)] * 4,
        out_shape=[jax.ShapeDtypeStruct((2, 3, 2, SIDE, SIDE), F32),
                   jax.ShapeDtypeStruct((2, 2, SIDE, SIDE), F32)]
        + [jax.ShapeDtypeStruct((2, 64, SIDE), F32)] * 4,
        scratch_shapes=[pltpu.VMEM((2, SIDE, SIDE), F32), pltpu.SemaphoreType.DMA((2, 8))],
        compiler_params=pltpu.CompilerParams(vmem_limit_bytes=VMEM_BYTES),
        cost_estimate=pl.CostEstimate(flops=1700000000, bytes_accessed=12000000, transcendentals=0),
        name="forward",
    )(info, own, right, *below, probe, *tables)


def backward_kernel(info, far, probe, patch, f0, f1, f2, f3, left_table, right_table,
                    mine, theirs, g0, g1, g2, g3, factor, grad):
    mode = pl.program_id(0)
    me = info[5]
    first = info[6] == 0

    @pl.when(mode == 0)
    def _():
        for j, part in enumerate((f0, f1, f2, f3)):
            start = pl.multiple_of(lax.rem(me + N_MODE - j, N_MODE) * 64, 64)
            factor[:, pl.ds(start, 64), :] = part[...]

    probe_re, probe_im = probe[0, 0], probe[0, 1]
    own_term, other_term = 0.0, 0.0
    for s in range(2):
        change_re = (factor[s] * far[s, 0, 0]).astype(BF16)
        change_im = (factor[s] * far[s, 0, 1]).astype(BF16)
        back = jnp.dot(right_table[...], jnp.concatenate([change_re, change_im], axis=0),
                       preferred_element_type=F32).astype(BF16)
        back = jnp.concatenate([back[:SIDE], back[SIDE:]], axis=1)
        both = jnp.dot(back, left_table[...], preferred_element_type=F32)
        delta_re, delta_im = both[:, :SIDE], both[:, SIDE:]
        patch_re, patch_im = patch[s, 0], patch[s, 1]
        term_re = patch_re * delta_re + patch_im * delta_im
        term_im = patch_re * delta_im - patch_im * delta_re
        own_term += jnp.where(first, term_re, term_im)
        other_term += jnp.where(first, term_im, term_re)
        grad_re = probe_re * delta_re + probe_im * delta_im
        grad_im = probe_re * delta_im - probe_im * delta_re
        grad[s, 0] = jnp.where(mode == 0, grad_re, grad[s, 0] + grad_re)
        grad[s, 1] = jnp.where(mode == 0, grad_im, grad[s, 1] + grad_im)
    mine[0] = own_term
    theirs[0] = other_term

    @pl.when(mode == 2)
    def _():
        for j, out in enumerate((g0, g1, g2, g3)):
            base = lax.rem(me + j, N_MODE) * SUB
            for q in range(8):
                start = pl.multiple_of(base + PIECE_R * (q // 2), SUB)
                out[:, q] = grad[:, :, pl.ds(start, SUB), PIECE_C * (q % 2):PIECE_C * (q % 2 + 1)]


def backward(info, far, probe, patch, factors, tables):
    full = lambda *shape: pl.BlockSpec(shape, lambda k: (0,) * len(shape))
    return pl.pallas_call(
        backward_kernel,
        grid=(3,),
        in_specs=[SMEM,
                  pl.BlockSpec((2, 1, 2, SIDE, SIDE), lambda k: (0, k, 0, 0, 0)),
                  pl.BlockSpec((1, 2, SIDE, SIDE), lambda k: (k, 0, 0, 0)),
                  full(2, 2, SIDE, SIDE)] + [full(2, 64, SIDE)] * 4
        + [full(512, 512), full(512, 512)],
        out_specs=[pl.BlockSpec((1, SIDE, SIDE), lambda k: (k, 0, 0))] * 2
        + [full(2, 8, 2, SUB, PIECE_C)] * 4,
        out_shape=[jax.ShapeDtypeStruct((3, SIDE, SIDE), F32)] * 2
        + [jax.ShapeDtypeStruct((2, 8, 2, SUB, PIECE_C), F32)] * 4,
        scratch_shapes=[pltpu.VMEM((2, SIDE, SIDE), F32), pltpu.VMEM((2, 2, SIDE, SIDE), F32)],
        compiler_params=pltpu.CompilerParams(vmem_limit_bytes=VMEM_BYTES),
        cost_estimate=pl.CostEstimate(flops=1700000000, bytes_accessed=12000000, transcendentals=0),
        name="backward",
    )(info, far, probe, patch, *factors, *tables)


def scatter_kernel(info, g0, g1, g2, g3, own, right, low, corner, canvas):
    canvas[...] = jnp.zeros_like(canvas)
    for s in range(2):
        for q in range(8):
            index = canvas_index(info[2 * s] + q // 2, info[2 * s + 1] + q % 2)
            canvas[index] += (g0[s, q] + g1[s, q]) + (g2[s, q] + g3[s, q])
    own[...] = canvas[:24]
    rows = lax.broadcasted_iota(jnp.int32, (2, SUB, PIECE_C), 1)
    note = jnp.zeros((2, SUB, PIECE_C), F32)
    for i in range(5):
        note = jnp.where(rows == i, info[i].astype(F32), note)
    for out, begin, size in ((right, 24, 6), (low, 30, 12), (corner, 42, 3)):
        out[:size] = canvas[begin:begin + size]
        out[size] = note


def scatter(info, parts):
    pieces = lambda n: jax.ShapeDtypeStruct((n, 2, SUB, PIECE_C), F32)
    return pl.pallas_call(
        scatter_kernel,
        in_specs=[SMEM] + [VMEM] * 4,
        out_specs=[VMEM] * 4,
        out_shape=[pieces(24), pieces(7), pieces(13), pieces(4)],
        scratch_shapes=[pltpu.VMEM((45, 2, SUB, PIECE_C), F32)],
        cost_estimate=pl.CostEstimate(flops=1000000, bytes_accessed=2000000, transcendentals=0),
        name="scatter",
    )(info, *parts)


def update_kernel(info, pieces, own, right, low, corner, light, new, old, weight, notes, sems):
    start = pl.multiple_of(info[5] * SUB, SUB)
    fetch = pltpu.make_async_copy(pieces.at[:, :, pl.ds(start, SUB), :], old, sems.at[3])
    fetch.start()
    reads = [pltpu.make_async_copy(part.at[size, 0], notes.at[n], sems.at[n])
             for n, (part, size) in enumerate(((right, 6), (low, 12), (corner, 3)))]
    for read in reads:
        read.start()
    weight[...] = jnp.zeros_like(weight)

    def add_slot(top, left, live, classes):
        @pl.when(live)
        def _():
            for q in classes:
                row = top + q // 2
                col = left + q % 2

                @pl.when((row >= 0) & (row < TILE_R) & (col >= 0) & (col < TILE_C))
                def _():
                    weight[row * TILE_C + col] += light[
                        q // 2, :, PIECE_C * (q % 2):PIECE_C * (q % 2 + 1)]

    for s in range(2):
        add_slot(info[2 * s], info[2 * s + 1], s < info[4], range(8))
    for read in reads:
        read.wait()
    for n, (down, across, classes) in enumerate((
            (0, TILE_C, (1, 3, 5, 7)), (TILE_R, 0, (2, 3, 4, 5, 6, 7)), (TILE_R, TILE_C, (3, 5, 7)))):
        for s in range(2):
            top = notes[n, 2 * s, 0].astype(jnp.int32) - down
            left = notes[n, 2 * s + 1, 0].astype(jnp.int32) - across
            live = s < notes[n, 4, 0].astype(jnp.int32)
            add_slot(top, left, live & (top > -4) & (left > -2), classes)
    fetch.wait()
    for p in range(TILE_R * TILE_C):
        row, col = p // TILE_C, p % TILE_C
        total = own[p]
        if row < 3:
            total = total + low[p]
        if col == 0:
            total = total + right[row]
        if row < 3 and col == 0:
            total = total + corner[row]
        new[p] = old[p] + total / (weight[p] + object_floor)[None]


def update(info, pieces, own, right, low, corner, light):
    shape = (TILE_R * TILE_C, 2, SUB, PIECE_C)
    return pl.pallas_call(
        update_kernel,
        in_specs=[SMEM, ANY] + [VMEM] * 5,
        out_specs=VMEM,
        out_shape=jax.ShapeDtypeStruct(shape, F32),
        scratch_shapes=[pltpu.VMEM(shape, F32), pltpu.VMEM((TILE_R * TILE_C, SUB, PIECE_C), F32),
                        pltpu.SMEM((3, SUB, PIECE_C), F32), pltpu.SemaphoreType.DMA((4,))],
        compiler_params=pltpu.CompilerParams(vmem_limit_bytes=VMEM_BYTES),
        cost_estimate=pl.CostEstimate(flops=1000000, bytes_accessed=2000000, transcendentals=0),
        name="update",
    )(info, pieces, own, right, low, corner, light)


def join_pieces_kernel(info, n0, n1, n2, n3, out, held, in_sems, out_sems):
    parts = (n0, n1, n2, n3)
    reads = [pltpu.make_async_copy(part, held.at[j], in_sems.at[j]) for j, part in enumerate(parts)]
    for read in reads:
        read.start()
    writes = []
    for j, read in enumerate(reads):
        start = pl.multiple_of(lax.rem(info[5] + N_MODE - j, N_MODE) * SUB, SUB)
        read.wait()
        writes.append(pltpu.make_async_copy(
            held.at[j], out.at[:, :, pl.ds(start, SUB), :], out_sems.at[j]))
        writes[j].start()
    for write in writes:
        write.wait()


def join_pieces(info, parts):
    return pl.pallas_call(
        join_pieces_kernel,
        in_specs=[SMEM] + [ANY] * 4,
        out_specs=pl.BlockSpec(memory_space=pltpu.HBM),
        out_shape=jax.ShapeDtypeStruct((TILE_R * TILE_C, 2, PIECE_R, PIECE_C), F32),
        scratch_shapes=[pltpu.VMEM((N_MODE, TILE_R * TILE_C, 2, SUB, PIECE_C), F32),
                        pltpu.SemaphoreType.DMA((N_MODE,)), pltpu.SemaphoreType.DMA((N_MODE,))],
        compiler_params=pltpu.CompilerParams(vmem_limit_bytes=VMEM_BYTES),
        cost_estimate=pl.CostEstimate(flops=0, bytes_accessed=3000000, transcendentals=0),
        name="join_pieces",
    )(info, *parts)


def join_channels_kernel(info, mine, theirs, out, held, in_sems, out_sems):
    core = info[6]
    steps = [(source, half, k) for k in range(3) for half, source in enumerate((mine, theirs))]
    reads = [pltpu.make_async_copy(source.at[k], held.at[half, k], in_sems.at[half, k])
             for source, half, k in steps]
    for read in reads:
        read.start()
    writes = []
    for (source, half, k), read in zip(steps, reads):
        read.wait()
        channel = core if half == 0 else 1 - core
        writes.append(pltpu.make_async_copy(
            held.at[half, k], out.at[k, channel], out_sems.at[half, k]))
        writes[-1].start()
    for write in writes:
        write.wait()


def join_channels(info, mine, theirs):
    return pl.pallas_call(
        join_channels_kernel,
        in_specs=[SMEM, ANY, ANY],
        out_specs=pl.BlockSpec(memory_space=pltpu.HBM),
        out_shape=jax.ShapeDtypeStruct((3, 2, SIDE, SIDE), F32),
        scratch_shapes=[pltpu.VMEM((2, 3, SIDE, SIDE), F32),
                        pltpu.SemaphoreType.DMA((2, 3)), pltpu.SemaphoreType.DMA((2, 3))],
        compiler_params=pltpu.CompilerParams(vmem_limit_bytes=VMEM_BYTES),
        cost_estimate=pl.CostEstimate(flops=0, bytes_accessed=3000000, transcendentals=0),
        name="join_channels",
    )(info, mine, theirs)


def body(object_pieces, probe_modes, intensity, positions, counts):
    tile_index = lax.axis_index("tile")
    mode_index = lax.axis_index("mode")
    tables = fourier_blocks()
    tile_grid = object_pieces.reshape(TILE_R, TILE_C, 2, PIECE_R, PIECE_C)
    own_rows = lax.dynamic_slice_in_dim(object_pieces[:12], mode_index * SUB, SUB, axis=2)
    low = shifted(own_rows, "tile", -DEV_COLS)
    corner = shifted(own_rows[::TILE_C], "tile", -DEV_COLS - 1)
    right = shifted(tile_grid[:, 0], "tile", -1)
    below = jnp.concatenate([low, corner], axis=0)
    dev_row = tile_index // DEV_COLS
    dev_col = tile_index % DEV_COLS
    rows = jnp.clip(positions[:, 0] // PIECE_R - dev_row * TILE_R, 0, TILE_R - 1)
    cols = jnp.clip(positions[:, 1] // PIECE_C - dev_col * TILE_C, 0, TILE_C - 1)
    info = jnp.stack([rows[0], cols[0], rows[1], cols[1], counts[0], mode_index,
                      tile_index % 2, tile_index]).astype(jnp.int32)
    below = [below] + [turned(below, j) for j in (1, 2, 3)]

    light_local = jnp.sum(probe_modes * probe_modes, axis=(0, 1))
    light_parts = light_local.reshape(4, N_MODE, SUB, SIDE).transpose(1, 0, 2, 3)
    light = lax.psum_scatter(light_parts, "mode", scatter_dimension=0, tiled=True)
    light, right = lax.optimization_barrier((light, right))

    far, patch, *powers = forward(info, object_pieces, right, below, probe_modes, tables)
    received = [turned(powers[j], j) for j in (1, 2, 3)]
    power = (powers[0] + received[0]) + (received[1] + received[2])
    own_intensity = lax.dynamic_slice_in_dim(intensity, mode_index * 64, 64, axis=1)
    live = (jnp.arange(2, dtype=jnp.int32) < counts[0]).astype(F32)
    factor = live[:, None, None] * (jnp.sqrt(own_intensity) / jnp.sqrt(power + far_floor) - 1.0)
    factors = [factor] + [turned(factor, j) for j in (1, 2, 3)]

    mine, theirs, *grads = backward(info, far, probe_modes, patch, factors, tables)

    groups = [list(range(core, N_TILE, 2)) for core in range(2)]
    exchange = lambda blocks: lax.all_to_all(
        blocks, "tile", 0, 0, axis_index_groups=groups, tiled=True)
    summed = mine + core_swap(theirs)
    pieces = exchange(summed.reshape(N_CHIP, PART, SIDE))
    parts = [grads[0]] + [turned(grads[j], j) for j in (1, 2, 3)]
    own, to_right, to_low, to_corner = scatter(info, parts)
    from_above = shifted(to_low, "tile", DEV_COLS)
    from_corner = shifted(to_corner, "tile", DEV_COLS + 1)
    from_left = shifted(to_right, "tile", 1)
    pieces, from_left, from_above, from_corner = lax.optimization_barrier(
        (pieces, from_left, from_above, from_corner))
    share = jnp.sum(pieces, axis=0)

    new = update(info, object_pieces, own, from_left, from_above, from_corner, light[0])
    share, new = lax.optimization_barrier((share, new))
    gathered = exchange(jnp.broadcast_to(share[None], (N_CHIP, PART, SIDE)))
    new_parts = [new] + [turned(new, j) for j in (1, 2, 3)]
    gathered, *new_parts = lax.optimization_barrier((gathered, *new_parts))
    gathered = gathered.reshape(3, SIDE, SIDE)
    probe_grad = join_channels(info, gathered, core_swap(gathered))
    return (join_pieces(info, new_parts), probe_grad)


def solution(mesh):
    return jax.shard_map(
        body,
        mesh=mesh,
        in_specs=(
            P("tile", None, None, None),
            P("mode", None, None, None),
            P("tile", None, None),
            P("tile", None),
            P("tile"),
        ),
        out_specs=(P("tile", None, None, None), P("mode", None, None, None)),
        check_vma=False,
    )
```

```python
import math

import jax
import jax.numpy as jnp
import numpy as np
from jax import lax
from jax.experimental import pallas as pl
from jax.experimental.pallas import tpu as pltpu
from jax.sharding import PartitionSpec as P

DEV_COLS = 8
TILE_R = 6
TILE_C = 4
SIDE = 256
PIECE_R = 64
PIECE_C = 128
N_MODE = 4
N_TILE = 64
SUB = PIECE_R // N_MODE
N_CHIP = N_TILE // 2
PART = 3 * SIDE // N_CHIP
VMEM_BYTES = 56 * 1024 * 1024

far_floor = 0.1
object_floor = 0.1

F32 = jnp.float32
BF16 = jnp.bfloat16
ANY = pl.BlockSpec(memory_space=pl.ANY)
SMEM = pl.BlockSpec(memory_space=pltpu.SMEM)
VMEM = pl.BlockSpec(memory_space=pltpu.VMEM)


def shifted(block, distance):
    return lax.ppermute(block, "tile", [(d, (d + distance) % N_TILE) for d in range(N_TILE)])


def turned(block, distance):
    return lax.ppermute(block, "mode", [(i, (i + distance) % N_MODE) for i in range(N_MODE)])


def core_swap(block):
    return lax.ppermute(block, "tile", [(d, d ^ 1) for d in range(N_TILE)])


def fourier_blocks():
    indices = np.arange(SIDE)
    phases = (indices[:, None] * indices[None, :] % SIDE) * (2.0 * math.pi / SIDE)
    scaling = 1.0 / math.sqrt(SIDE)
    re = (np.cos(phases) * scaling).astype(np.float32)
    im = (-np.sin(phases) * scaling).astype(np.float32)
    left = np.block([[re, -im], [im, re]])
    right = np.block([[re, im], [-im, re]])
    return jnp.asarray(left.astype(jnp.bfloat16)), jnp.asarray(right.astype(jnp.bfloat16))


def canvas_index(row, col):
    inside = jnp.where(col < TILE_C, row * TILE_C + col, 24 + row)
    below = jnp.where(col < TILE_C, 30 + (row - TILE_R) * TILE_C + col, 42 + row - TILE_R)
    return jnp.where(row < TILE_R, inside, below)


def forward_kernel(info, own, right, b0, b1, b2, b3, probe, left_table, right_table,
                   far, patch, p0, p1, p2, p3, power, sems):
    mode = pl.program_id(0)

    def piece_copy(s, q, source, index):
        target = patch.at[s, :, pl.ds(PIECE_R * (q // 2), PIECE_R), pl.ds(PIECE_C * (q % 2), PIECE_C)]
        return pltpu.make_async_copy(source.at[index], target, sems.at[s, q])

    @pl.when(mode == 0)
    def _():
        for s in range(2):
            for q in range(8):
                row = info[2 * s] + q // 2
                col = info[2 * s + 1] + q % 2
                upper = row < TILE_R
                inner = col < TILE_C

                @pl.when(upper & inner)
                def _():
                    piece_copy(s, q, own, row * TILE_C + col).start()

                @pl.when(upper & jnp.logical_not(inner))
                def _():
                    piece_copy(s, q, right, row).start()

                @pl.when(jnp.logical_not(upper))
                def _():
                    below = jnp.where(inner, (row - TILE_R) * TILE_C + col, 12 + row - TILE_R)
                    for j, source in enumerate((b0, b1, b2, b3)):
                        start = lax.rem(info[5] + N_MODE - j, N_MODE) * SUB + PIECE_R * (q // 2)
                        target = patch.at[s, :, pl.ds(pl.multiple_of(start, SUB), SUB),
                                          pl.ds(PIECE_C * (q % 2), PIECE_C)]
                        pltpu.make_async_copy(source.at[below], target, sems.at[s, q]).start()

        for s in range(2):
            for q in range(8):
                piece_copy(s, q, own, 0).wait()

    probe_re, probe_im = probe[0, 0], probe[0, 1]
    for s in range(2):
        patch_re, patch_im = patch[s, 0], patch[s, 1]
        exit_re = (probe_re * patch_re - probe_im * patch_im).astype(BF16)
        exit_im = (probe_re * patch_im + probe_im * patch_re).astype(BF16)
        half = jnp.dot(left_table[...], jnp.concatenate([exit_re, exit_im], axis=0),
                       preferred_element_type=F32).astype(BF16)
        half = jnp.concatenate([half[:SIDE], half[SIDE:]], axis=1)
        both = jnp.dot(half, right_table[...], preferred_element_type=F32)
        far_re, far_im = both[:, :SIDE], both[:, SIDE:]
        far[s, 0, 0] = far_re
        far[s, 0, 1] = far_im
        local = far_re * far_re + far_im * far_im
        power[s] = jnp.where(mode == 0, local, power[s] + local)

    @pl.when(mode == 2)
    def _():
        for j, out in enumerate((p0, p1, p2, p3)):
            start = pl.multiple_of(lax.rem(info[5] + j, N_MODE) * 64, 64)
            out[...] = power[:, pl.ds(start, 64), :]


def forward(info, own, right, below, probe, tables):
    full = lambda *shape: pl.BlockSpec(shape, lambda k: (0,) * len(shape))
    return pl.pallas_call(
        forward_kernel,
        grid=(3,),
        in_specs=[SMEM] + [ANY] * 6 + [
                  pl.BlockSpec((1, 2, SIDE, SIDE), lambda k: (k, 0, 0, 0)),
                  full(512, 512), full(512, 512)],
        out_specs=[pl.BlockSpec((2, 1, 2, SIDE, SIDE), lambda k: (0, k, 0, 0, 0)),
                   full(2, 2, SIDE, SIDE)] + [full(2, 64, SIDE)] * 4,
        out_shape=[jax.ShapeDtypeStruct((2, 3, 2, SIDE, SIDE), F32),
                   jax.ShapeDtypeStruct((2, 2, SIDE, SIDE), F32)]
        + [jax.ShapeDtypeStruct((2, 64, SIDE), F32)] * 4,
        scratch_shapes=[pltpu.VMEM((2, SIDE, SIDE), F32), pltpu.SemaphoreType.DMA((2, 8))],
        compiler_params=pltpu.CompilerParams(vmem_limit_bytes=VMEM_BYTES),
        cost_estimate=pl.CostEstimate(flops=1700000000, bytes_accessed=12000000, transcendentals=0),
        name="forward",
    )(info, own, right, *below, probe, *tables)


def backward_kernel(info, far, probe, patch, f0, f1, f2, f3, left_table, right_table,
                    mine, theirs, g0, g1, g2, g3, factor, grad):
    mode = pl.program_id(0)
    me = info[5]
    first = info[6] == 0

    @pl.when(mode == 0)
    def _():
        for j, part in enumerate((f0, f1, f2, f3)):
            start = pl.multiple_of(lax.rem(me + N_MODE - j, N_MODE) * 64, 64)
            factor[:, pl.ds(start, 64), :] = part[...]

    probe_re, probe_im = probe[0, 0], probe[0, 1]
    own_term, other_term = 0.0, 0.0
    for s in range(2):
        change_re = (factor[s] * far[s, 0, 0]).astype(BF16)
        change_im = (factor[s] * far[s, 0, 1]).astype(BF16)
        back = jnp.dot(right_table[...], jnp.concatenate([change_re, change_im], axis=0),
                       preferred_element_type=F32).astype(BF16)
        back = jnp.concatenate([back[:SIDE], back[SIDE:]], axis=1)
        both = jnp.dot(back, left_table[...], preferred_element_type=F32)
        delta_re, delta_im = both[:, :SIDE], both[:, SIDE:]
        patch_re, patch_im = patch[s, 0], patch[s, 1]
        term_re = patch_re * delta_re + patch_im * delta_im
        term_im = patch_re * delta_im - patch_im * delta_re
        own_term += jnp.where(first, term_re, term_im)
        other_term += jnp.where(first, term_im, term_re)
        grad_re = probe_re * delta_re + probe_im * delta_im
        grad_im = probe_re * delta_im - probe_im * delta_re
        grad[s, 0] = jnp.where(mode == 0, grad_re, grad[s, 0] + grad_re)
        grad[s, 1] = jnp.where(mode == 0, grad_im, grad[s, 1] + grad_im)
    mine[0] = own_term
    theirs[0] = other_term

    @pl.when(mode == 2)
    def _():
        for j, out in enumerate((g0, g1, g2, g3)):
            base = lax.rem(me + j, N_MODE) * SUB
            for q in range(8):
                start = pl.multiple_of(base + PIECE_R * (q // 2), SUB)
                out[:, q] = grad[:, :, pl.ds(start, SUB), PIECE_C * (q % 2):PIECE_C * (q % 2 + 1)]


def backward(info, far, probe, patch, factors, tables):
    full = lambda *shape: pl.BlockSpec(shape, lambda k: (0,) * len(shape))
    return pl.pallas_call(
        backward_kernel,
        grid=(3,),
        in_specs=[SMEM,
                  pl.BlockSpec((2, 1, 2, SIDE, SIDE), lambda k: (0, k, 0, 0, 0)),
                  pl.BlockSpec((1, 2, SIDE, SIDE), lambda k: (k, 0, 0, 0)),
                  full(2, 2, SIDE, SIDE)] + [full(2, 64, SIDE)] * 4
        + [full(512, 512), full(512, 512)],
        out_specs=[pl.BlockSpec((1, SIDE, SIDE), lambda k: (k, 0, 0))] * 2
        + [full(2, 8, 2, SUB, PIECE_C)] * 4,
        out_shape=[jax.ShapeDtypeStruct((3, SIDE, SIDE), F32)] * 2
        + [jax.ShapeDtypeStruct((2, 8, 2, SUB, PIECE_C), F32)] * 4,
        scratch_shapes=[pltpu.VMEM((2, SIDE, SIDE), F32), pltpu.VMEM((2, 2, SIDE, SIDE), F32)],
        compiler_params=pltpu.CompilerParams(vmem_limit_bytes=VMEM_BYTES),
        cost_estimate=pl.CostEstimate(flops=1700000000, bytes_accessed=12000000, transcendentals=0),
        name="backward",
    )(info, far, probe, patch, *factors, *tables)


def scatter_kernel(info, g0, g1, g2, g3, own, right, low, corner, canvas):
    canvas[...] = jnp.zeros_like(canvas)
    for s in range(2):
        for q in range(8):
            index = canvas_index(info[2 * s] + q // 2, info[2 * s + 1] + q % 2)
            canvas[index] += (g0[s, q] + g1[s, q]) + (g2[s, q] + g3[s, q])
    own[...] = canvas[:24]
    rows = lax.broadcasted_iota(jnp.int32, (2, SUB, PIECE_C), 1)
    note = jnp.zeros((2, SUB, PIECE_C), F32)
    for i in range(5):
        note = jnp.where(rows == i, info[i].astype(F32), note)
    for out, begin, size in ((right, 24, 6), (low, 30, 12), (corner, 42, 3)):
        out[:size] = canvas[begin:begin + size]
        out[size] = note


def scatter(info, parts):
    pieces = lambda n: jax.ShapeDtypeStruct((n, 2, SUB, PIECE_C), F32)
    return pl.pallas_call(
        scatter_kernel,
        in_specs=[SMEM] + [VMEM] * 4,
        out_specs=[VMEM] * 4,
        out_shape=[pieces(24), pieces(7), pieces(13), pieces(4)],
        scratch_shapes=[pltpu.VMEM((45, 2, SUB, PIECE_C), F32)],
        cost_estimate=pl.CostEstimate(flops=1000000, bytes_accessed=2000000, transcendentals=0),
        name="scatter",
    )(info, *parts)


def update_kernel(info, pieces, own, right, low, corner, light, new, old, weight, notes, sems):
    start = pl.multiple_of(info[5] * SUB, SUB)
    fetch = pltpu.make_async_copy(pieces.at[:, :, pl.ds(start, SUB), :], old, sems.at[3])
    fetch.start()
    reads = [pltpu.make_async_copy(part.at[size, 0], notes.at[n], sems.at[n])
             for n, (part, size) in enumerate(((right, 6), (low, 12), (corner, 3)))]
    for read in reads:
        read.start()
    weight[...] = jnp.zeros_like(weight)

    def add_slot(top, left, live, classes):
        @pl.when(live)
        def _():
            for q in classes:
                row = top + q // 2
                col = left + q % 2

                @pl.when((row >= 0) & (row < TILE_R) & (col >= 0) & (col < TILE_C))
                def _():
                    weight[row * TILE_C + col] += light[
                        q // 2, :, PIECE_C * (q % 2):PIECE_C * (q % 2 + 1)]

    for s in range(2):
        add_slot(info[2 * s], info[2 * s + 1], s < info[4], range(8))
    for read in reads:
        read.wait()
    for n, (down, across, classes) in enumerate((
            (0, TILE_C, (1, 3, 5, 7)), (TILE_R, 0, (2, 3, 4, 5, 6, 7)), (TILE_R, TILE_C, (3, 5, 7)))):
        for s in range(2):
            top = notes[n, 2 * s, 0].astype(jnp.int32) - down
            left = notes[n, 2 * s + 1, 0].astype(jnp.int32) - across
            live = s < notes[n, 4, 0].astype(jnp.int32)
            add_slot(top, left, live & (top > -4) & (left > -2), classes)
    fetch.wait()
    for p in range(TILE_R * TILE_C):
        row, col = p // TILE_C, p % TILE_C
        total = own[p]
        if row < 3:
            total = total + low[p]
        if col == 0:
            total = total + right[row]
        if row < 3 and col == 0:
            total = total + corner[row]
        new[p] = old[p] + total / (weight[p] + object_floor)[None]


def update(info, pieces, own, right, low, corner, light):
    shape = (TILE_R * TILE_C, 2, SUB, PIECE_C)
    return pl.pallas_call(
        update_kernel,
        in_specs=[SMEM, ANY] + [VMEM] * 5,
        out_specs=VMEM,
        out_shape=jax.ShapeDtypeStruct(shape, F32),
        scratch_shapes=[pltpu.VMEM(shape, F32), pltpu.VMEM((TILE_R * TILE_C, SUB, PIECE_C), F32),
                        pltpu.SMEM((3, SUB, PIECE_C), F32), pltpu.SemaphoreType.DMA((4,))],
        compiler_params=pltpu.CompilerParams(vmem_limit_bytes=VMEM_BYTES),
        cost_estimate=pl.CostEstimate(flops=1000000, bytes_accessed=2000000, transcendentals=0),
        name="update",
    )(info, pieces, own, right, low, corner, light)


def join_pieces_kernel(info, n0, n1, n2, n3, out, held, in_sems, out_sems):
    parts = (n0, n1, n2, n3)
    reads = [pltpu.make_async_copy(part, held.at[j], in_sems.at[j]) for j, part in enumerate(parts)]
    for read in reads:
        read.start()
    writes = []
    for j, read in enumerate(reads):
        start = pl.multiple_of(lax.rem(info[5] + N_MODE - j, N_MODE) * SUB, SUB)
        read.wait()
        writes.append(pltpu.make_async_copy(
            held.at[j], out.at[:, :, pl.ds(start, SUB), :], out_sems.at[j]))
        writes[j].start()
    for write in writes:
        write.wait()


def join_pieces(info, parts):
    return pl.pallas_call(
        join_pieces_kernel,
        in_specs=[SMEM] + [ANY] * 4,
        out_specs=pl.BlockSpec(memory_space=pltpu.HBM),
        out_shape=jax.ShapeDtypeStruct((TILE_R * TILE_C, 2, PIECE_R, PIECE_C), F32),
        scratch_shapes=[pltpu.VMEM((N_MODE, TILE_R * TILE_C, 2, SUB, PIECE_C), F32),
                        pltpu.SemaphoreType.DMA((N_MODE,)), pltpu.SemaphoreType.DMA((N_MODE,))],
        compiler_params=pltpu.CompilerParams(vmem_limit_bytes=VMEM_BYTES),
        cost_estimate=pl.CostEstimate(flops=0, bytes_accessed=3000000, transcendentals=0),
        name="join_pieces",
    )(info, *parts)


def join_channels_kernel(info, mine, theirs, out, held, in_sems, out_sems):
    core = info[6]
    steps = [(source, half, k) for k in range(3) for half, source in enumerate((mine, theirs))]
    reads = [pltpu.make_async_copy(source.at[k], held.at[half, k], in_sems.at[half, k])
             for source, half, k in steps]
    for read in reads:
        read.start()
    writes = []
    for (source, half, k), read in zip(steps, reads):
        read.wait()
        channel = core if half == 0 else 1 - core
        writes.append(pltpu.make_async_copy(
            held.at[half, k], out.at[k, channel], out_sems.at[half, k]))
        writes[-1].start()
    for write in writes:
        write.wait()


def join_channels(info, mine, theirs):
    return pl.pallas_call(
        join_channels_kernel,
        in_specs=[SMEM, ANY, ANY],
        out_specs=pl.BlockSpec(memory_space=pltpu.HBM),
        out_shape=jax.ShapeDtypeStruct((3, 2, SIDE, SIDE), F32),
        scratch_shapes=[pltpu.VMEM((2, 3, SIDE, SIDE), F32),
                        pltpu.SemaphoreType.DMA((2, 3)), pltpu.SemaphoreType.DMA((2, 3))],
        compiler_params=pltpu.CompilerParams(vmem_limit_bytes=VMEM_BYTES),
        cost_estimate=pl.CostEstimate(flops=0, bytes_accessed=3000000, transcendentals=0),
        name="join_channels",
    )(info, mine, theirs)


def body(object_pieces, probe_modes, intensity, positions, counts):
    tile_index = lax.axis_index("tile")
    mode_index = lax.axis_index("mode")
    tables = fourier_blocks()
    tile_grid = object_pieces.reshape(TILE_R, TILE_C, 2, PIECE_R, PIECE_C)
    own_rows = lax.dynamic_slice_in_dim(object_pieces[:12], mode_index * SUB, SUB, axis=2)
    low = shifted(own_rows, -DEV_COLS)
    corner = shifted(own_rows[::TILE_C], -DEV_COLS - 1)
    right = shifted(tile_grid[:, 0], -1)
    below = jnp.concatenate([low, corner], axis=0)
    dev_row = tile_index // DEV_COLS
    dev_col = tile_index % DEV_COLS
    rows = jnp.clip(positions[:, 0] // PIECE_R - dev_row * TILE_R, 0, TILE_R - 1)
    cols = jnp.clip(positions[:, 1] // PIECE_C - dev_col * TILE_C, 0, TILE_C - 1)
    info = jnp.stack([rows[0], cols[0], rows[1], cols[1], counts[0], mode_index,
                      tile_index % 2, tile_index]).astype(jnp.int32)
    late_modes, below = lax.optimization_barrier((probe_modes, below))
    light_local = jnp.sum(late_modes * late_modes, axis=(0, 1))
    light_parts = light_local.reshape(4, N_MODE, SUB, SIDE).transpose(1, 0, 2, 3)
    light = lax.psum_scatter(light_parts, "mode", scatter_dimension=0, tiled=True)
    below = [below] + [turned(below, j) for j in (1, 2, 3)]

    far, patch, *powers = forward(info, object_pieces, right, below, probe_modes, tables)
    received = [turned(powers[j], j) for j in (1, 2, 3)]
    power = (powers[0] + received[0]) + (received[1] + received[2])
    own_intensity = lax.dynamic_slice_in_dim(intensity, mode_index * 64, 64, axis=1)
    live = (jnp.arange(2, dtype=jnp.int32) < counts[0]).astype(F32)
    factor = live[:, None, None] * (jnp.sqrt(own_intensity) / jnp.sqrt(power + far_floor) - 1.0)
    factors = [factor] + [turned(factor, j) for j in (1, 2, 3)]

    mine, theirs, *grads = backward(info, far, probe_modes, patch, factors, tables)

    groups = [list(range(core, N_TILE, 2)) for core in range(2)]
    exchange = lambda blocks: lax.all_to_all(
        blocks, "tile", 0, 0, axis_index_groups=groups, tiled=True)
    summed = mine + core_swap(theirs)
    pieces = exchange(summed.reshape(N_CHIP, PART, SIDE))
    parts = [grads[0]] + [turned(grads[j], j) for j in (1, 2, 3)]
    own, to_right, to_low, to_corner = scatter(info, parts)
    from_above = shifted(to_low, DEV_COLS)
    from_corner = shifted(to_corner, DEV_COLS + 1)
    from_left = shifted(to_right, 1)
    pieces, from_left, from_above, from_corner = lax.optimization_barrier(
        (pieces, from_left, from_above, from_corner))
    share = jnp.sum(pieces, axis=0)

    new = update(info, object_pieces, own, from_left, from_above, from_corner, light[0])
    share, new = lax.optimization_barrier((share, new))
    gathered = exchange(jnp.broadcast_to(share[None], (N_CHIP, PART, SIDE)))
    new_parts = [new] + [turned(new, j) for j in (1, 2, 3)]
    gathered, *new_parts = lax.optimization_barrier((gathered, *new_parts))
    gathered = gathered.reshape(3, SIDE, SIDE)
    probe_grad = join_channels(info, gathered, core_swap(gathered))
    return (join_pieces(info, new_parts), probe_grad)


def solution(mesh):
    return jax.shard_map(
        body,
        mesh=mesh,
        in_specs=(
            P("tile", None, None, None),
            P("mode", None, None, None),
            P("tile", None, None),
            P("tile", None),
            P("tile"),
        ),
        out_specs=(P("tile", None, None, None), P("mode", None, None, None)),
        check_vma=False,
    )
```

```python
import math

import jax
import jax.numpy as jnp
import numpy as np
from jax import lax
from jax.experimental import pallas as pl
from jax.experimental.pallas import tpu as pltpu
from jax.sharding import PartitionSpec as P

DEV_COLS = 8
TILE_R = 6
TILE_C = 4
SIDE = 256
PIECE_R = 64
PIECE_C = 128
N_MODE = 4
N_TILE = 64
SUB = PIECE_R // N_MODE
N_CHIP = N_TILE // 2
PART = 3 * SIDE // N_CHIP
VMEM_BYTES = 24 * 1024 * 1024
FORWARD_BYTES = 56 * 1024 * 1024
SMALL_BYTES = 8 * 1024 * 1024

far_floor = 0.1
object_floor = 0.1

F32 = jnp.float32
BF16 = jnp.bfloat16
ANY = pl.BlockSpec(memory_space=pl.ANY)
HBM = pl.BlockSpec(memory_space=pltpu.HBM)
SMEM = pl.BlockSpec(memory_space=pltpu.SMEM)
VMEM = pl.BlockSpec(memory_space=pltpu.VMEM)


def shifted(block, distance):
    return lax.ppermute(block, "tile", [(d, (d + distance) % N_TILE) for d in range(N_TILE)])


def turned(block, distance):
    return lax.ppermute(block, "mode", [(i, (i + distance) % N_MODE) for i in range(N_MODE)])


def core_swap(block):
    return lax.ppermute(block, "tile", [(d, d ^ 1) for d in range(N_TILE)])


def fourier_table():
    indices = np.arange(SIDE)
    phases = (indices[:, None] * indices[None, :] % SIDE) * (2.0 * math.pi / SIDE)
    scaling = 1.0 / math.sqrt(SIDE)
    both = np.stack([np.cos(phases) * scaling, -np.sin(phases) * scaling])
    return jnp.asarray(both.astype(np.float32).astype(jnp.bfloat16))


def expand_table(table, held, left, right, sem):
    fetch = pltpu.make_async_copy(table, held, sem)
    fetch.start()
    fetch.wait()
    re, im = held[0], held[1]
    for out in (left, right):
        out[:SIDE, :SIDE] = re
        out[SIDE:, SIDE:] = re
    left[:SIDE, SIDE:] = -im
    left[SIDE:, :SIDE] = im
    right[:SIDE, SIDE:] = im
    right[SIDE:, :SIDE] = -im


def canvas_index(row, col):
    inside = jnp.where(col < TILE_C, row * TILE_C + col, 24 + row)
    below = jnp.where(col < TILE_C, 30 + (row - TILE_R) * TILE_C + col, 42 + row - TILE_R)
    return jnp.where(row < TILE_R, inside, below)


def forward_kernel(info, own, right, b0, b1, b2, b3, probe, table,
                   far, patch, p0, p1, p2, p3, power, held, left_table, right_table, sems, table_sem):
    mode = pl.program_id(0)

    def piece_copy(s, q, source, index):
        target = patch.at[s, :, pl.ds(PIECE_R * (q // 2), PIECE_R), pl.ds(PIECE_C * (q % 2), PIECE_C)]
        return pltpu.make_async_copy(source.at[index], target, sems.at[s, q])

    @pl.when(mode == 0)
    def _():
        for s in range(2):
            for q in range(8):
                row = info[2 * s] + q // 2
                col = info[2 * s + 1] + q % 2
                upper = row < TILE_R
                inner = col < TILE_C

                @pl.when(upper & inner)
                def _():
                    piece_copy(s, q, own, row * TILE_C + col).start()

                @pl.when(upper & jnp.logical_not(inner))
                def _():
                    piece_copy(s, q, right, row).start()

                @pl.when(jnp.logical_not(upper))
                def _():
                    below = jnp.where(inner, (row - TILE_R) * TILE_C + col, 12 + row - TILE_R)
                    for j, source in enumerate((b0, b1, b2, b3)):
                        start = lax.rem(info[5] + N_MODE - j, N_MODE) * SUB + PIECE_R * (q // 2)
                        target = patch.at[s, :, pl.ds(pl.multiple_of(start, SUB), SUB),
                                          pl.ds(PIECE_C * (q % 2), PIECE_C)]
                        pltpu.make_async_copy(source.at[below], target, sems.at[s, q]).start()

        expand_table(table, held, left_table, right_table, table_sem)
        for s in range(2):
            for q in range(8):
                piece_copy(s, q, own, 0).wait()

    probe_re, probe_im = probe[0, 0], probe[0, 1]
    for s in range(2):
        patch_re, patch_im = patch[s, 0], patch[s, 1]
        exit_re = (probe_re * patch_re - probe_im * patch_im).astype(BF16)
        exit_im = (probe_re * patch_im + probe_im * patch_re).astype(BF16)
        half = jnp.dot(left_table[...], jnp.concatenate([exit_re, exit_im], axis=0),
                       preferred_element_type=F32).astype(BF16)
        half = jnp.concatenate([half[:SIDE], half[SIDE:]], axis=1)
        both = jnp.dot(half, right_table[...], preferred_element_type=F32)
        far_re, far_im = both[:, :SIDE], both[:, SIDE:]
        far[s, 0, 0] = far_re
        far[s, 0, 1] = far_im
        local = far_re * far_re + far_im * far_im
        power[s] = jnp.where(mode == 0, local, power[s] + local)

    @pl.when(mode == 2)
    def _():
        for j, out in enumerate((p0, p1, p2, p3)):
            start = pl.multiple_of(lax.rem(info[5] + j, N_MODE) * 64, 64)
            out[...] = power[:, pl.ds(start, 64), :]


def forward(info, own, right, below, probe, table):
    full = lambda *shape: pl.BlockSpec(shape, lambda k: (0,) * len(shape))
    return pl.pallas_call(
        forward_kernel,
        grid=(3,),
        in_specs=[SMEM] + [HBM] * 6 + [
                  pl.BlockSpec((1, 2, SIDE, SIDE), lambda k: (k, 0, 0, 0)),
                  HBM],
        out_specs=[pl.BlockSpec((2, 1, 2, SIDE, SIDE), lambda k: (0, k, 0, 0, 0)),
                   full(2, 2, SIDE, SIDE)] + [full(2, 64, SIDE)] * 4,
        out_shape=[pltpu.HBM((2, 3, 2, SIDE, SIDE), F32),
                   jax.ShapeDtypeStruct((2, 2, SIDE, SIDE), F32)]
        + [jax.ShapeDtypeStruct((2, 64, SIDE), F32)] * 4,
        scratch_shapes=[pltpu.VMEM((2, SIDE, SIDE), F32), pltpu.VMEM((2, SIDE, SIDE), BF16), pltpu.VMEM((512, 512), BF16),
                        pltpu.VMEM((512, 512), BF16),
                        pltpu.SemaphoreType.DMA((2, 8)), pltpu.SemaphoreType.DMA],
        compiler_params=pltpu.CompilerParams(vmem_limit_bytes=FORWARD_BYTES),
        cost_estimate=pl.CostEstimate(flops=1700000000, bytes_accessed=12000000, transcendentals=0),
        name="forward",
    )(info, own, right, *below, probe, table)


def backward_kernel(info, far, probe, patch, f0, f1, f2, f3, table,
                    mine, theirs, g0, g1, g2, g3, factor, grad, held, left_table, right_table,
                    table_sem):
    mode = pl.program_id(0)
    me = info[5]
    first = info[6] == 0

    @pl.when(mode == 0)
    def _():
        expand_table(table, held, left_table, right_table, table_sem)
        for j, part in enumerate((f0, f1, f2, f3)):
            start = pl.multiple_of(lax.rem(me + N_MODE - j, N_MODE) * 64, 64)
            factor[:, pl.ds(start, 64), :] = part[...]

    probe_re, probe_im = probe[0, 0], probe[0, 1]
    own_term, other_term = 0.0, 0.0
    for s in range(2):
        change_re = (factor[s] * far[s, 0, 0]).astype(BF16)
        change_im = (factor[s] * far[s, 0, 1]).astype(BF16)
        back = jnp.dot(right_table[...], jnp.concatenate([change_re, change_im], axis=0),
                       preferred_element_type=F32).astype(BF16)
        back = jnp.concatenate([back[:SIDE], back[SIDE:]], axis=1)
        both = jnp.dot(back, left_table[...], preferred_element_type=F32)
        delta_re, delta_im = both[:, :SIDE], both[:, SIDE:]
        patch_re, patch_im = patch[s, 0], patch[s, 1]
        term_re = patch_re * delta_re + patch_im * delta_im
        term_im = patch_re * delta_im - patch_im * delta_re
        own_term += jnp.where(first, term_re, term_im)
        other_term += jnp.where(first, term_im, term_re)
        grad_re = probe_re * delta_re + probe_im * delta_im
        grad_im = probe_re * delta_im - probe_im * delta_re
        grad[s, 0] = jnp.where(mode == 0, grad_re, grad[s, 0] + grad_re)
        grad[s, 1] = jnp.where(mode == 0, grad_im, grad[s, 1] + grad_im)
    mine[0] = own_term
    theirs[0] = other_term

    @pl.when(mode == 2)
    def _():
        for j, out in enumerate((g0, g1, g2, g3)):
            base = lax.rem(me + j, N_MODE) * SUB
            for q in range(8):
                start = pl.multiple_of(base + PIECE_R * (q // 2), SUB)
                out[:, q] = grad[:, :, pl.ds(start, SUB), PIECE_C * (q % 2):PIECE_C * (q % 2 + 1)]


def backward(info, far, probe, patch, factors, table):
    full = lambda *shape: pl.BlockSpec(shape, lambda k: (0,) * len(shape))
    return pl.pallas_call(
        backward_kernel,
        grid=(3,),
        in_specs=[SMEM,
                  pl.BlockSpec((2, 1, 2, SIDE, SIDE), lambda k: (0, k, 0, 0, 0)),
                  pl.BlockSpec((1, 2, SIDE, SIDE), lambda k: (k, 0, 0, 0)),
                  full(2, 2, SIDE, SIDE)] + [full(2, 64, SIDE)] * 4
        + [HBM],
        out_specs=[pl.BlockSpec((1, SIDE, SIDE), lambda k: (k, 0, 0))] * 2
        + [full(2, 8, 2, SUB, PIECE_C)] * 4,
        out_shape=[jax.ShapeDtypeStruct((3, SIDE, SIDE), F32)] * 2
        + [jax.ShapeDtypeStruct((2, 8, 2, SUB, PIECE_C), F32)] * 4,
        scratch_shapes=[pltpu.VMEM((2, SIDE, SIDE), F32), pltpu.VMEM((2, 2, SIDE, SIDE), F32),
                        pltpu.VMEM((2, SIDE, SIDE), BF16), pltpu.VMEM((512, 512), BF16),
                        pltpu.VMEM((512, 512), BF16),
                        pltpu.SemaphoreType.DMA],
        compiler_params=pltpu.CompilerParams(vmem_limit_bytes=VMEM_BYTES),
        cost_estimate=pl.CostEstimate(flops=1700000000, bytes_accessed=12000000, transcendentals=0),
        name="backward",
    )(info, far, probe, patch, *factors, table)


def scatter_kernel(info, g0, g1, g2, g3, own, right, low, corner, canvas):
    canvas[...] = jnp.zeros_like(canvas)
    for s in range(2):
        for q in range(8):
            index = canvas_index(info[2 * s] + q // 2, info[2 * s + 1] + q % 2)
            canvas[index] += (g0[s, q] + g1[s, q]) + (g2[s, q] + g3[s, q])
    own[...] = canvas[:24]
    rows = lax.broadcasted_iota(jnp.int32, (2, SUB, PIECE_C), 1)
    note = jnp.zeros((2, SUB, PIECE_C), F32)
    for i in range(5):
        note = jnp.where(rows == i, info[i].astype(F32), note)
    for out, begin, size in ((right, 24, 6), (low, 30, 12), (corner, 42, 3)):
        out[:size] = canvas[begin:begin + size]
        out[size] = note


def scatter(info, parts):
    pieces = lambda n: jax.ShapeDtypeStruct((n, 2, SUB, PIECE_C), F32)
    return pl.pallas_call(
        scatter_kernel,
        in_specs=[SMEM] + [VMEM] * 4,
        out_specs=[VMEM] * 4,
        out_shape=[pieces(24), pieces(7), pieces(13), pieces(4)],
        scratch_shapes=[pltpu.VMEM((45, 2, SUB, PIECE_C), F32)],
        compiler_params=pltpu.CompilerParams(vmem_limit_bytes=SMALL_BYTES),
        cost_estimate=pl.CostEstimate(flops=1000000, bytes_accessed=2000000, transcendentals=0),
        name="scatter",
    )(info, *parts)


def update_kernel(info, pieces, own, right, low, corner, light, new, old, weight, notes, sems):
    start = pl.multiple_of(info[5] * SUB, SUB)
    fetch = pltpu.make_async_copy(pieces.at[:, :, pl.ds(start, SUB), :], old, sems.at[3])
    fetch.start()
    reads = [pltpu.make_async_copy(part.at[size, 0], notes.at[n], sems.at[n])
             for n, (part, size) in enumerate(((right, 6), (low, 12), (corner, 3)))]
    for read in reads:
        read.start()
    weight[...] = jnp.zeros_like(weight)

    def add_slot(top, left, live, classes):
        @pl.when(live)
        def _():
            for q in classes:
                row = top + q // 2
                col = left + q % 2

                @pl.when((row >= 0) & (row < TILE_R) & (col >= 0) & (col < TILE_C))
                def _():
                    weight[row * TILE_C + col] += light[
                        q // 2, :, PIECE_C * (q % 2):PIECE_C * (q % 2 + 1)]

    for s in range(2):
        add_slot(info[2 * s], info[2 * s + 1], s < info[4], range(8))
    for read in reads:
        read.wait()
    for n, (down, across, classes) in enumerate((
            (0, TILE_C, (1, 3, 5, 7)), (TILE_R, 0, (2, 3, 4, 5, 6, 7)), (TILE_R, TILE_C, (3, 5, 7)))):
        for s in range(2):
            top = notes[n, 2 * s, 0].astype(jnp.int32) - down
            left = notes[n, 2 * s + 1, 0].astype(jnp.int32) - across
            live = s < notes[n, 4, 0].astype(jnp.int32)
            add_slot(top, left, live & (top > -4) & (left > -2), classes)
    fetch.wait()
    for p in range(TILE_R * TILE_C):
        row, col = p // TILE_C, p % TILE_C
        total = own[p]
        if row < 3:
            total = total + low[p]
        if col == 0:
            total = total + right[row]
        if row < 3 and col == 0:
            total = total + corner[row]
        new[p] = old[p] + total / (weight[p] + object_floor)[None]


def update(info, pieces, own, right, low, corner, light):
    shape = (TILE_R * TILE_C, 2, SUB, PIECE_C)
    return pl.pallas_call(
        update_kernel,
        in_specs=[SMEM, ANY] + [VMEM] * 5,
        out_specs=VMEM,
        out_shape=jax.ShapeDtypeStruct(shape, F32),
        scratch_shapes=[pltpu.VMEM(shape, F32), pltpu.VMEM((TILE_R * TILE_C, SUB, PIECE_C), F32),
                        pltpu.SMEM((3, SUB, PIECE_C), F32), pltpu.SemaphoreType.DMA((4,))],
        compiler_params=pltpu.CompilerParams(vmem_limit_bytes=SMALL_BYTES),
        cost_estimate=pl.CostEstimate(flops=1000000, bytes_accessed=2000000, transcendentals=0),
        name="update",
    )(info, pieces, own, right, low, corner, light)


def join_pieces_kernel(info, n0, n1, n2, n3, out, sems):
    writes = []
    for j, part in enumerate((n0, n1, n2, n3)):
        start = pl.multiple_of(lax.rem(info[5] + N_MODE - j, N_MODE) * SUB, SUB)
        writes.append(pltpu.make_async_copy(part, out.at[:, :, pl.ds(start, SUB), :], sems.at[j]))
        writes[j].start()
    for write in writes:
        write.wait()


def join_pieces(info, parts):
    return pl.pallas_call(
        join_pieces_kernel,
        in_specs=[SMEM] + [ANY] * 4,
        out_specs=pl.BlockSpec(memory_space=pltpu.HBM),
        out_shape=jax.ShapeDtypeStruct((TILE_R * TILE_C, 2, PIECE_R, PIECE_C), F32),
        scratch_shapes=[pltpu.SemaphoreType.DMA((N_MODE,))],
        compiler_params=pltpu.CompilerParams(vmem_limit_bytes=2 * 1024 * 1024),
        cost_estimate=pl.CostEstimate(flops=0, bytes_accessed=3000000, transcendentals=0),
        name="join_pieces",
    )(info, *parts)


def join_channels_kernel(info, mine, theirs, out, sems):
    core = info[6]
    writes = []
    for half, source in enumerate((mine, theirs)):
        channel = core if half == 0 else 1 - core
        for k in range(3):
            writes.append(pltpu.make_async_copy(
                source.at[k], out.at[k, channel], sems.at[half, k]))
            writes[-1].start()
    for write in writes:
        write.wait()


def join_channels(info, mine, theirs):
    return pl.pallas_call(
        join_channels_kernel,
        in_specs=[SMEM, ANY, ANY],
        out_specs=pl.BlockSpec(memory_space=pltpu.HBM),
        out_shape=jax.ShapeDtypeStruct((3, 2, SIDE, SIDE), F32),
        scratch_shapes=[pltpu.SemaphoreType.DMA((2, 3))],
        compiler_params=pltpu.CompilerParams(vmem_limit_bytes=2 * 1024 * 1024),
        cost_estimate=pl.CostEstimate(flops=0, bytes_accessed=3000000, transcendentals=0),
        name="join_channels",
    )(info, mine, theirs)


def body(object_pieces, probe_modes, intensity, positions, counts):
    tile_index = lax.axis_index("tile")
    mode_index = lax.axis_index("mode")
    table = fourier_table()
    tile_grid = object_pieces.reshape(TILE_R, TILE_C, 2, PIECE_R, PIECE_C)
    own_rows = lax.dynamic_slice_in_dim(object_pieces[:12], mode_index * SUB, SUB, axis=2)
    low = shifted(own_rows, -DEV_COLS)
    corner = shifted(own_rows[::TILE_C], -DEV_COLS - 1)
    right = shifted(tile_grid[:, 0], -1)
    below = jnp.concatenate([low, corner], axis=0)
    dev_row = tile_index // DEV_COLS
    dev_col = tile_index % DEV_COLS
    rows = jnp.clip(positions[:, 0] // PIECE_R - dev_row * TILE_R, 0, TILE_R - 1)
    cols = jnp.clip(positions[:, 1] // PIECE_C - dev_col * TILE_C, 0, TILE_C - 1)
    info = jnp.stack([rows[0], cols[0], rows[1], cols[1], counts[0], mode_index,
                      tile_index % 2, tile_index]).astype(jnp.int32)
    late_modes, below = lax.optimization_barrier((probe_modes, below))
    light_local = jnp.sum(late_modes * late_modes, axis=(0, 1))
    light_parts = light_local.reshape(4, N_MODE, SUB, SIDE).transpose(1, 0, 2, 3)
    light = lax.psum_scatter(light_parts, "mode", scatter_dimension=0, tiled=True)
    below = [below] + [turned(below, j) for j in (1, 2, 3)]

    far, patch, *powers = forward(info, object_pieces, right, below, probe_modes, table)
    received = [turned(powers[j], j) for j in (1, 2, 3)]
    power = (powers[0] + received[0]) + (received[1] + received[2])
    own_intensity = lax.dynamic_slice_in_dim(intensity, mode_index * 64, 64, axis=1)
    live = (jnp.arange(2, dtype=jnp.int32) < counts[0]).astype(F32)
    factor = live[:, None, None] * (jnp.sqrt(own_intensity) / jnp.sqrt(power + far_floor) - 1.0)
    factors = [factor] + [turned(factor, j) for j in (1, 2, 3)]

    mine, theirs, *grads = backward(info, far, probe_modes, patch, factors, table)

    groups = [list(range(core, N_TILE, 2)) for core in range(2)]
    exchange = lambda blocks: lax.all_to_all(
        blocks, "tile", 0, 0, axis_index_groups=groups, tiled=True)
    summed = mine + core_swap(theirs)
    pieces = exchange(summed.reshape(N_CHIP, PART, SIDE))
    parts = [grads[0]] + [turned(grads[j], j) for j in (1, 2, 3)]
    own, to_right, to_low, to_corner = scatter(info, parts)
    from_above = shifted(to_low, DEV_COLS)
    from_corner = shifted(to_corner, DEV_COLS + 1)
    from_left = shifted(to_right, 1)
    pieces, from_left, from_above, from_corner = lax.optimization_barrier(
        (pieces, from_left, from_above, from_corner))
    share = jnp.sum(pieces, axis=0)

    new = update(info, object_pieces, own, from_left, from_above, from_corner, light[0])
    share, new = lax.optimization_barrier((share, new))
    gathered = exchange(jnp.broadcast_to(share[None], (N_CHIP, PART, SIDE)))
    new_parts = [new] + [turned(new, j) for j in (1, 2, 3)]
    gathered, *new_parts = lax.optimization_barrier((gathered, *new_parts))
    gathered = gathered.reshape(3, SIDE, SIDE)
    probe_grad = join_channels(info, gathered, core_swap(gathered))
    return (join_pieces(info, new_parts), probe_grad)


def solution(mesh):
    return jax.shard_map(
        body,
        mesh=mesh,
        in_specs=(
            P("tile", None, None, None),
            P("mode", None, None, None),
            P("tile", None, None),
            P("tile", None),
            P("tile"),
        ),
        out_specs=(P("tile", None, None, None), P("mode", None, None, None)),
        check_vma=False,
    )
```

```python
import math

import jax
import jax.numpy as jnp
import numpy as np
from jax import lax
from jax.experimental import pallas as pl
from jax.experimental.pallas import tpu as pltpu
from jax.sharding import PartitionSpec as P

DEV_COLS = 8
TILE_R = 6
TILE_C = 4
SIDE = 256
PIECE_R = 64
PIECE_C = 128
N_MODE = 4
N_TILE = 64
SUB = PIECE_R // N_MODE
N_CHIP = N_TILE // 2
PART = 3 * SIDE // N_CHIP
VMEM_BYTES = 24 * 1024 * 1024
FORWARD_BYTES = 40 * 1024 * 1024
SMALL_BYTES = 8 * 1024 * 1024

far_floor = 0.1
object_floor = 0.1

F32 = jnp.float32
BF16 = jnp.bfloat16
ANY = pl.BlockSpec(memory_space=pl.ANY)
HBM = pl.BlockSpec(memory_space=pltpu.HBM)
SMEM = pl.BlockSpec(memory_space=pltpu.SMEM)
VMEM = pl.BlockSpec(memory_space=pltpu.VMEM)


def shifted(block, distance):
    return lax.ppermute(block, "tile", [(d, (d + distance) % N_TILE) for d in range(N_TILE)])


def turned(block, distance):
    return lax.ppermute(block, "mode", [(i, (i + distance) % N_MODE) for i in range(N_MODE)])


def core_swap(block):
    return lax.ppermute(block, "tile", [(d, d ^ 1) for d in range(N_TILE)])


def in_hbm(block):
    return pltpu.with_memory_space_constraint(block, pltpu.HBM)


def fourier_table():
    indices = np.arange(SIDE)
    phases = (indices[:, None] * indices[None, :] % SIDE) * (2.0 * math.pi / SIDE)
    scaling = 1.0 / math.sqrt(SIDE)
    both = np.stack([np.cos(phases) * scaling, -np.sin(phases) * scaling])
    return jnp.asarray(both.astype(np.float32).astype(jnp.bfloat16))


def expand_table(table, held, left, right, sem):
    fetch = pltpu.make_async_copy(table, held, sem)
    fetch.start()
    fetch.wait()
    re, im = held[0], held[1]
    for out in (left, right):
        out[:SIDE, :SIDE] = re
        out[SIDE:, SIDE:] = re
    left[:SIDE, SIDE:] = -im
    left[SIDE:, :SIDE] = im
    right[:SIDE, SIDE:] = im
    right[SIDE:, :SIDE] = -im


def canvas_index(row, col):
    inside = jnp.where(col < TILE_C, row * TILE_C + col, 24 + row)
    below = jnp.where(col < TILE_C, 30 + (row - TILE_R) * TILE_C + col, 42 + row - TILE_R)
    return jnp.where(row < TILE_R, inside, below)


def forward_kernel(info, own, right, b0, b1, b2, b3, probe, table,
                   far, patch, p0, p1, p2, p3, power, held, left_table, right_table, sems, table_sem):
    mode = pl.program_id(0)

    def piece_copy(s, q, source, index):
        target = patch.at[s, :, pl.ds(PIECE_R * (q // 2), PIECE_R), pl.ds(PIECE_C * (q % 2), PIECE_C)]
        return pltpu.make_async_copy(source.at[index], target, sems.at[s, q])

    @pl.when(mode == 0)
    def _():
        for s in range(2):
            for q in range(8):
                row = info[2 * s] + q // 2
                col = info[2 * s + 1] + q % 2
                upper = row < TILE_R
                inner = col < TILE_C

                @pl.when(upper & inner)
                def _():
                    piece_copy(s, q, own, row * TILE_C + col).start()

                @pl.when(upper & jnp.logical_not(inner))
                def _():
                    piece_copy(s, q, right, row).start()

                @pl.when(jnp.logical_not(upper))
                def _():
                    below = jnp.where(inner, (row - TILE_R) * TILE_C + col, 12 + row - TILE_R)
                    for j, source in enumerate((b0, b1, b2, b3)):
                        start = lax.rem(info[5] + N_MODE - j, N_MODE) * SUB + PIECE_R * (q // 2)
                        target = patch.at[s, :, pl.ds(pl.multiple_of(start, SUB), SUB),
                                          pl.ds(PIECE_C * (q % 2), PIECE_C)]
                        pltpu.make_async_copy(source.at[below], target, sems.at[s, q]).start()

        expand_table(table, held, left_table, right_table, table_sem)
        for s in range(2):
            for q in range(8):
                piece_copy(s, q, own, 0).wait()

    probe_re, probe_im = probe[0, 0], probe[0, 1]
    for s in range(2):
        patch_re, patch_im = patch[s, 0], patch[s, 1]
        exit_re = (probe_re * patch_re - probe_im * patch_im).astype(BF16)
        exit_im = (probe_re * patch_im + probe_im * patch_re).astype(BF16)
        half = jnp.dot(left_table[...], jnp.concatenate([exit_re, exit_im], axis=0),
                       preferred_element_type=F32).astype(BF16)
        half = jnp.concatenate([half[:SIDE], half[SIDE:]], axis=1)
        both = jnp.dot(half, right_table[...], preferred_element_type=F32)
        far_re, far_im = both[:, :SIDE], both[:, SIDE:]
        far[s, 0, 0] = far_re
        far[s, 0, 1] = far_im
        local = far_re * far_re + far_im * far_im
        power[s] = jnp.where(mode == 0, local, power[s] + local)

    @pl.when(mode == 2)
    def _():
        for j, out in enumerate((p0, p1, p2, p3)):
            start = pl.multiple_of(lax.rem(info[5] + j, N_MODE) * 64, 64)
            out[...] = power[:, pl.ds(start, 64), :]


def forward(info, own, right, below, probe, table):
    full = lambda *shape: pl.BlockSpec(shape, lambda k: (0,) * len(shape))
    return pl.pallas_call(
        forward_kernel,
        grid=(3,),
        in_specs=[SMEM] + [HBM] * 6 + [
                  pl.BlockSpec((1, 2, SIDE, SIDE), lambda k: (k, 0, 0, 0)),
                  HBM],
        out_specs=[pl.BlockSpec((2, 1, 2, SIDE, SIDE), lambda k: (0, k, 0, 0, 0)),
                   full(2, 2, SIDE, SIDE)] + [full(2, 64, SIDE)] * 4,
        out_shape=[pltpu.HBM((2, 3, 2, SIDE, SIDE), F32),
                   jax.ShapeDtypeStruct((2, 2, SIDE, SIDE), F32)]
        + [jax.ShapeDtypeStruct((2, 64, SIDE), F32)] * 4,
        scratch_shapes=[pltpu.VMEM((2, SIDE, SIDE), F32), pltpu.VMEM((2, SIDE, SIDE), BF16), pltpu.VMEM((512, 512), BF16),
                        pltpu.VMEM((512, 512), BF16),
                        pltpu.SemaphoreType.DMA((2, 8)), pltpu.SemaphoreType.DMA],
        compiler_params=pltpu.CompilerParams(vmem_limit_bytes=FORWARD_BYTES),
        cost_estimate=pl.CostEstimate(flops=1700000000, bytes_accessed=12000000, transcendentals=0),
        name="forward",
    )(info, own, right, *below, probe, table)


def backward_kernel(info, far, probe, patch, f0, f1, f2, f3, table,
                    mine, theirs, g0, g1, g2, g3, factor, grad, held, left_table, right_table,
                    table_sem):
    mode = pl.program_id(0)
    me = info[5]
    first = info[6] == 0

    @pl.when(mode == 0)
    def _():
        expand_table(table, held, left_table, right_table, table_sem)
        for j, part in enumerate((f0, f1, f2, f3)):
            start = pl.multiple_of(lax.rem(me + N_MODE - j, N_MODE) * 64, 64)
            factor[:, pl.ds(start, 64), :] = part[...]

    probe_re, probe_im = probe[0, 0], probe[0, 1]
    own_term, other_term = 0.0, 0.0
    for s in range(2):
        change_re = (factor[s] * far[s, 0, 0]).astype(BF16)
        change_im = (factor[s] * far[s, 0, 1]).astype(BF16)
        back = jnp.dot(right_table[...], jnp.concatenate([change_re, change_im], axis=0),
                       preferred_element_type=F32).astype(BF16)
        back = jnp.concatenate([back[:SIDE], back[SIDE:]], axis=1)
        both = jnp.dot(back, left_table[...], preferred_element_type=F32)
        delta_re, delta_im = both[:, :SIDE], both[:, SIDE:]
        patch_re, patch_im = patch[s, 0], patch[s, 1]
        term_re = patch_re * delta_re + patch_im * delta_im
        term_im = patch_re * delta_im - patch_im * delta_re
        own_term += jnp.where(first, term_re, term_im)
        other_term += jnp.where(first, term_im, term_re)
        grad_re = probe_re * delta_re + probe_im * delta_im
        grad_im = probe_re * delta_im - probe_im * delta_re
        grad[s, 0] = jnp.where(mode == 0, grad_re, grad[s, 0] + grad_re)
        grad[s, 1] = jnp.where(mode == 0, grad_im, grad[s, 1] + grad_im)
    mine[0] = own_term
    theirs[0] = other_term

    @pl.when(mode == 2)
    def _():
        for j, out in enumerate((g0, g1, g2, g3)):
            base = lax.rem(me + j, N_MODE) * SUB
            for q in range(8):
                start = pl.multiple_of(base + PIECE_R * (q // 2), SUB)
                out[:, q] = grad[:, :, pl.ds(start, SUB), PIECE_C * (q % 2):PIECE_C * (q % 2 + 1)]


def backward(info, far, probe, patch, factors, table):
    full = lambda *shape: pl.BlockSpec(shape, lambda k: (0,) * len(shape))
    return pl.pallas_call(
        backward_kernel,
        grid=(3,),
        in_specs=[SMEM,
                  pl.BlockSpec((2, 1, 2, SIDE, SIDE), lambda k: (0, k, 0, 0, 0)),
                  pl.BlockSpec((1, 2, SIDE, SIDE), lambda k: (k, 0, 0, 0)),
                  full(2, 2, SIDE, SIDE)] + [full(2, 64, SIDE)] * 4
        + [HBM],
        out_specs=[pl.BlockSpec((1, SIDE, SIDE), lambda k: (k, 0, 0))] * 2
        + [full(2, 8, 2, SUB, PIECE_C)] * 4,
        out_shape=[jax.ShapeDtypeStruct((3, SIDE, SIDE), F32)] * 2
        + [jax.ShapeDtypeStruct((2, 8, 2, SUB, PIECE_C), F32)] * 4,
        scratch_shapes=[pltpu.VMEM((2, SIDE, SIDE), F32), pltpu.VMEM((2, 2, SIDE, SIDE), F32),
                        pltpu.VMEM((2, SIDE, SIDE), BF16), pltpu.VMEM((512, 512), BF16),
                        pltpu.VMEM((512, 512), BF16),
                        pltpu.SemaphoreType.DMA],
        compiler_params=pltpu.CompilerParams(vmem_limit_bytes=VMEM_BYTES),
        cost_estimate=pl.CostEstimate(flops=1700000000, bytes_accessed=12000000, transcendentals=0),
        name="backward",
    )(info, far, probe, patch, *factors, table)


def scatter_kernel(info, g0, g1, g2, g3, own, right, low, corner, canvas):
    canvas[...] = jnp.zeros_like(canvas)
    for s in range(2):
        for q in range(8):
            index = canvas_index(info[2 * s] + q // 2, info[2 * s + 1] + q % 2)
            canvas[index] += (g0[s, q] + g1[s, q]) + (g2[s, q] + g3[s, q])
    own[...] = canvas[:24]
    rows = lax.broadcasted_iota(jnp.int32, (2, SUB, PIECE_C), 1)
    note = jnp.zeros((2, SUB, PIECE_C), F32)
    for i in range(5):
        note = jnp.where(rows == i, info[i].astype(F32), note)
    for out, begin, size in ((right, 24, 6), (low, 30, 12), (corner, 42, 3)):
        out[:size] = canvas[begin:begin + size]
        out[size] = note


def scatter(info, parts):
    pieces = lambda n: jax.ShapeDtypeStruct((n, 2, SUB, PIECE_C), F32)
    return pl.pallas_call(
        scatter_kernel,
        in_specs=[SMEM] + [VMEM] * 4,
        out_specs=[VMEM] * 4,
        out_shape=[pieces(24), pieces(7), pieces(13), pieces(4)],
        scratch_shapes=[pltpu.VMEM((45, 2, SUB, PIECE_C), F32)],
        compiler_params=pltpu.CompilerParams(vmem_limit_bytes=SMALL_BYTES),
        cost_estimate=pl.CostEstimate(flops=1000000, bytes_accessed=2000000, transcendentals=0),
        name="scatter",
    )(info, *parts)


def update_kernel(info, pieces, own, right, low, corner, light, new, old, weight, notes, sems):
    start = pl.multiple_of(info[5] * SUB, SUB)
    fetch = pltpu.make_async_copy(pieces.at[:, :, pl.ds(start, SUB), :], old, sems.at[3])
    fetch.start()
    reads = [pltpu.make_async_copy(part.at[size, 0], notes.at[n], sems.at[n])
             for n, (part, size) in enumerate(((right, 6), (low, 12), (corner, 3)))]
    for read in reads:
        read.start()
    weight[...] = jnp.zeros_like(weight)

    def add_slot(top, left, live, classes):
        @pl.when(live)
        def _():
            for q in classes:
                row = top + q // 2
                col = left + q % 2

                @pl.when((row >= 0) & (row < TILE_R) & (col >= 0) & (col < TILE_C))
                def _():
                    weight[row * TILE_C + col] += light[
                        q // 2, :, PIECE_C * (q % 2):PIECE_C * (q % 2 + 1)]

    for s in range(2):
        add_slot(info[2 * s], info[2 * s + 1], s < info[4], range(8))
    for read in reads:
        read.wait()
    for n, (down, across, classes) in enumerate((
            (0, TILE_C, (1, 3, 5, 7)), (TILE_R, 0, (2, 3, 4, 5, 6, 7)), (TILE_R, TILE_C, (3, 5, 7)))):
        for s in range(2):
            top = notes[n, 2 * s, 0].astype(jnp.int32) - down
            left = notes[n, 2 * s + 1, 0].astype(jnp.int32) - across
            live = s < notes[n, 4, 0].astype(jnp.int32)
            add_slot(top, left, live & (top > -4) & (left > -2), classes)
    fetch.wait()
    for p in range(TILE_R * TILE_C):
        row, col = p // TILE_C, p % TILE_C
        total = own[p]
        if row < 3:
            total = total + low[p]
        if col == 0:
            total = total + right[row]
        if row < 3 and col == 0:
            total = total + corner[row]
        new[p] = old[p] + total / (weight[p] + object_floor)[None]


def update(info, pieces, own, right, low, corner, light):
    shape = (TILE_R * TILE_C, 2, SUB, PIECE_C)
    return pl.pallas_call(
        update_kernel,
        in_specs=[SMEM, ANY] + [VMEM] * 5,
        out_specs=VMEM,
        out_shape=jax.ShapeDtypeStruct(shape, F32),
        scratch_shapes=[pltpu.VMEM(shape, F32), pltpu.VMEM((TILE_R * TILE_C, SUB, PIECE_C), F32),
                        pltpu.SMEM((3, SUB, PIECE_C), F32), pltpu.SemaphoreType.DMA((4,))],
        compiler_params=pltpu.CompilerParams(vmem_limit_bytes=SMALL_BYTES),
        cost_estimate=pl.CostEstimate(flops=1000000, bytes_accessed=2000000, transcendentals=0),
        name="update",
    )(info, pieces, own, right, low, corner, light)


def join_pieces_kernel(info, n0, n1, n2, n3, out, sems):
    writes = []
    for j, part in enumerate((n0, n1, n2, n3)):
        start = pl.multiple_of(lax.rem(info[5] + N_MODE - j, N_MODE) * SUB, SUB)
        writes.append(pltpu.make_async_copy(part, out.at[:, :, pl.ds(start, SUB), :], sems.at[j]))
        writes[j].start()
    for write in writes:
        write.wait()


def join_pieces(info, parts):
    return pl.pallas_call(
        join_pieces_kernel,
        in_specs=[SMEM] + [ANY] * 4,
        out_specs=pl.BlockSpec(memory_space=pltpu.HBM),
        out_shape=jax.ShapeDtypeStruct((TILE_R * TILE_C, 2, PIECE_R, PIECE_C), F32),
        scratch_shapes=[pltpu.SemaphoreType.DMA((N_MODE,))],
        compiler_params=pltpu.CompilerParams(vmem_limit_bytes=2 * 1024 * 1024),
        cost_estimate=pl.CostEstimate(flops=0, bytes_accessed=3000000, transcendentals=0),
        name="join_pieces",
    )(info, *parts)


def join_channels_kernel(info, mine, theirs, out, sems):
    core = info[6]
    writes = []
    for half, source in enumerate((mine, theirs)):
        channel = core if half == 0 else 1 - core
        for k in range(3):
            writes.append(pltpu.make_async_copy(
                source.at[k], out.at[k, channel], sems.at[half, k]))
            writes[-1].start()
    for write in writes:
        write.wait()


def join_channels(info, mine, theirs):
    return pl.pallas_call(
        join_channels_kernel,
        in_specs=[SMEM, ANY, ANY],
        out_specs=pl.BlockSpec(memory_space=pltpu.HBM),
        out_shape=jax.ShapeDtypeStruct((3, 2, SIDE, SIDE), F32),
        scratch_shapes=[pltpu.SemaphoreType.DMA((2, 3))],
        compiler_params=pltpu.CompilerParams(vmem_limit_bytes=2 * 1024 * 1024),
        cost_estimate=pl.CostEstimate(flops=0, bytes_accessed=3000000, transcendentals=0),
        name="join_channels",
    )(info, mine, theirs)


def body(object_pieces, probe_modes, intensity, positions, counts):
    tile_index = lax.axis_index("tile")
    mode_index = lax.axis_index("mode")
    table = fourier_table()
    tile_grid = object_pieces.reshape(TILE_R, TILE_C, 2, PIECE_R, PIECE_C)
    own_rows = lax.dynamic_slice_in_dim(object_pieces[:12], mode_index * SUB, SUB, axis=2)
    low = shifted(own_rows, -DEV_COLS)
    corner = shifted(own_rows[::TILE_C], -DEV_COLS - 1)
    right = shifted(tile_grid[:, 0], -1)
    below = jnp.concatenate([low, corner], axis=0)
    dev_row = tile_index // DEV_COLS
    dev_col = tile_index % DEV_COLS
    rows = jnp.clip(positions[:, 0] // PIECE_R - dev_row * TILE_R, 0, TILE_R - 1)
    cols = jnp.clip(positions[:, 1] // PIECE_C - dev_col * TILE_C, 0, TILE_C - 1)
    info = jnp.stack([rows[0], cols[0], rows[1], cols[1], counts[0], mode_index,
                      tile_index % 2, tile_index]).astype(jnp.int32)
    late_modes, below = lax.optimization_barrier((probe_modes, below))
    light_local = jnp.sum(late_modes * late_modes, axis=(0, 1))
    light_parts = light_local.reshape(4, N_MODE, SUB, SIDE).transpose(1, 0, 2, 3)
    light = lax.psum_scatter(light_parts, "mode", scatter_dimension=0, tiled=True)
    below = [below] + [turned(below, j) for j in (1, 2, 3)]

    far, patch, *powers = forward(info, in_hbm(object_pieces), in_hbm(right),
                                  [in_hbm(block) for block in below], probe_modes, in_hbm(table))
    received = [turned(powers[j], j) for j in (1, 2, 3)]
    power = (powers[0] + received[0]) + (received[1] + received[2])
    own_intensity = lax.dynamic_slice_in_dim(intensity, mode_index * 64, 64, axis=1)
    live = (jnp.arange(2, dtype=jnp.int32) < counts[0]).astype(F32)
    factor = live[:, None, None] * (jnp.sqrt(own_intensity) / jnp.sqrt(power + far_floor) - 1.0)
    factors = [factor] + [turned(factor, j) for j in (1, 2, 3)]

    mine, theirs, *grads = backward(info, in_hbm(far), probe_modes, patch, factors, in_hbm(table))

    groups = [list(range(core, N_TILE, 2)) for core in range(2)]
    exchange = lambda blocks: lax.all_to_all(
        blocks, "tile", 0, 0, axis_index_groups=groups, tiled=True)
    summed = mine + core_swap(theirs)
    pieces = exchange(summed.reshape(N_CHIP, PART, SIDE))
    parts = [grads[0]] + [turned(grads[j], j) for j in (1, 2, 3)]
    own, to_right, to_low, to_corner = scatter(info, parts)
    from_above = shifted(to_low, DEV_COLS)
    from_corner = shifted(to_corner, DEV_COLS + 1)
    from_left = shifted(to_right, 1)
    pieces, from_left, from_above, from_corner = lax.optimization_barrier(
        (pieces, from_left, from_above, from_corner))
    share = jnp.sum(pieces, axis=0)

    new = update(info, object_pieces, own, from_left, from_above, from_corner, in_hbm(light[0]))
    share, new = lax.optimization_barrier((share, new))
    gathered = exchange(jnp.broadcast_to(share[None], (N_CHIP, PART, SIDE)))
    new_parts = [new] + [turned(new, j) for j in (1, 2, 3)]
    gathered, *new_parts = lax.optimization_barrier((gathered, *new_parts))
    gathered = gathered.reshape(3, SIDE, SIDE)
    probe_grad = join_channels(info, gathered, core_swap(gathered))
    return (join_pieces(info, new_parts), probe_grad)


def solution(mesh):
    return jax.shard_map(
        body,
        mesh=mesh,
        in_specs=(
            P("tile", None, None, None),
            P("mode", None, None, None),
            P("tile", None, None),
            P("tile", None),
            P("tile"),
        ),
        out_specs=(P("tile", None, None, None), P("mode", None, None, None)),
        check_vma=False,
    )
```

```python
import math

import jax
import jax.numpy as jnp
import numpy as np
from jax import lax
from jax.experimental import pallas as pl
from jax.experimental.pallas import tpu as pltpu
from jax.sharding import PartitionSpec as P

DEV_COLS = 8
TILE_R = 6
TILE_C = 4
SIDE = 256
PIECE_R = 64
PIECE_C = 128
N_MODE = 4
N_TILE = 64
SUB = PIECE_R // N_MODE
N_CHIP = N_TILE // 2
PART = 3 * SIDE // N_CHIP
VMEM_BYTES = 24 * 1024 * 1024
FORWARD_BYTES = 40 * 1024 * 1024
SMALL_BYTES = 8 * 1024 * 1024

far_floor = 0.1
object_floor = 0.1

F32 = jnp.float32
BF16 = jnp.bfloat16
ANY = pl.BlockSpec(memory_space=pl.ANY)
HBM = pl.BlockSpec(memory_space=pltpu.HBM)
SMEM = pl.BlockSpec(memory_space=pltpu.SMEM)
VMEM = pl.BlockSpec(memory_space=pltpu.VMEM)


def shifted(block, distance):
    return lax.ppermute(block, "tile", [(d, (d + distance) % N_TILE) for d in range(N_TILE)])


def turned(block, distance):
    return lax.ppermute(block, "mode", [(i, (i + distance) % N_MODE) for i in range(N_MODE)])


def core_swap(block):
    return lax.ppermute(block, "tile", [(d, d ^ 1) for d in range(N_TILE)])


def in_hbm(block):
    return pltpu.with_memory_space_constraint(block, pltpu.HBM)


def fourier_table():
    indices = np.arange(SIDE)
    phases = (indices[:, None] * indices[None, :] % SIDE) * (2.0 * math.pi / SIDE)
    scaling = 1.0 / math.sqrt(SIDE)
    both = np.stack([np.cos(phases) * scaling, -np.sin(phases) * scaling])
    return jnp.asarray(both.astype(np.float32).astype(jnp.bfloat16))


def expand_table(table, held, left, right, sem):
    fetch = pltpu.make_async_copy(table, held, sem)
    fetch.start()
    fetch.wait()
    re, im = held[0], held[1]
    for out in (left, right):
        out[:SIDE, :SIDE] = re
        out[SIDE:, SIDE:] = re
    left[:SIDE, SIDE:] = -im
    left[SIDE:, :SIDE] = im
    right[:SIDE, SIDE:] = im
    right[SIDE:, :SIDE] = -im


def canvas_index(row, col):
    inside = jnp.where(col < TILE_C, row * TILE_C + col, 24 + row)
    below = jnp.where(col < TILE_C, 30 + (row - TILE_R) * TILE_C + col, 42 + row - TILE_R)
    return jnp.where(row < TILE_R, inside, below)


def forward_kernel(info, own, right, b0, b1, b2, b3, probe, table,
                   far, patch, p0, p1, p2, p3, power, held, left_table, right_table, sems, table_sem):
    mode = pl.program_id(0)

    def piece_copy(s, q, source, index):
        target = patch.at[s, :, pl.ds(PIECE_R * (q // 2), PIECE_R), pl.ds(PIECE_C * (q % 2), PIECE_C)]
        return pltpu.make_async_copy(source.at[index], target, sems.at[s, q])

    @pl.when(mode == 0)
    def _():
        for s in range(2):
            for q in range(8):
                row = info[2 * s] + q // 2
                col = info[2 * s + 1] + q % 2
                upper = row < TILE_R
                inner = col < TILE_C

                @pl.when(upper & inner)
                def _():
                    piece_copy(s, q, own, row * TILE_C + col).start()

                @pl.when(upper & jnp.logical_not(inner))
                def _():
                    piece_copy(s, q, right, row).start()

                @pl.when(jnp.logical_not(upper))
                def _():
                    below = jnp.where(inner, (row - TILE_R) * TILE_C + col, 12 + row - TILE_R)
                    for j, source in enumerate((b0, b1, b2, b3)):
                        start = lax.rem(info[5] + N_MODE - j, N_MODE) * SUB + PIECE_R * (q // 2)
                        target = patch.at[s, :, pl.ds(pl.multiple_of(start, SUB), SUB),
                                          pl.ds(PIECE_C * (q % 2), PIECE_C)]
                        pltpu.make_async_copy(source.at[below], target, sems.at[s, q]).start()

        expand_table(table, held, left_table, right_table, table_sem)
        for s in range(2):
            for q in range(8):
                piece_copy(s, q, own, 0).wait()

    probe_re, probe_im = probe[0, 0], probe[0, 1]
    for s in range(2):
        patch_re, patch_im = patch[s, 0], patch[s, 1]
        exit_re = (probe_re * patch_re - probe_im * patch_im).astype(BF16)
        exit_im = (probe_re * patch_im + probe_im * patch_re).astype(BF16)
        half = jnp.dot(left_table[...], jnp.concatenate([exit_re, exit_im], axis=0),
                       preferred_element_type=F32).astype(BF16)
        half = jnp.concatenate([half[:SIDE], half[SIDE:]], axis=1)
        both = jnp.dot(half, right_table[...], preferred_element_type=F32)
        far_re, far_im = both[:, :SIDE], both[:, SIDE:]
        far[s, 0, 0] = far_re
        far[s, 0, 1] = far_im
        local = far_re * far_re + far_im * far_im
        power[s] = jnp.where(mode == 0, local, power[s] + local)

    @pl.when(mode == 2)
    def _():
        for j, out in enumerate((p0, p1, p2, p3)):
            start = pl.multiple_of(lax.rem(info[5] + j, N_MODE) * 64, 64)
            out[...] = power[:, pl.ds(start, 64), :]


def forward(info, own, right, below, probe, table):
    full = lambda *shape: pl.BlockSpec(shape, lambda k: (0,) * len(shape))
    return pl.pallas_call(
        forward_kernel,
        grid=(3,),
        in_specs=[SMEM] + [HBM] * 6 + [
                  pl.BlockSpec((1, 2, SIDE, SIDE), lambda k: (k, 0, 0, 0)),
                  HBM],
        out_specs=[pl.BlockSpec((2, 1, 2, SIDE, SIDE), lambda k: (0, k, 0, 0, 0)),
                   full(2, 2, SIDE, SIDE)] + [full(2, 64, SIDE)] * 4,
        out_shape=[pltpu.HBM((2, 3, 2, SIDE, SIDE), F32),
                   jax.ShapeDtypeStruct((2, 2, SIDE, SIDE), F32)]
        + [jax.ShapeDtypeStruct((2, 64, SIDE), F32)] * 4,
        scratch_shapes=[pltpu.VMEM((2, SIDE, SIDE), F32), pltpu.VMEM((2, SIDE, SIDE), BF16), pltpu.VMEM((512, 512), BF16),
                        pltpu.VMEM((512, 512), BF16),
                        pltpu.SemaphoreType.DMA((2, 8)), pltpu.SemaphoreType.DMA],
        compiler_params=pltpu.CompilerParams(vmem_limit_bytes=FORWARD_BYTES),
        cost_estimate=pl.CostEstimate(flops=1700000000, bytes_accessed=12000000, transcendentals=0),
        name="forward",
    )(info, own, right, *below, probe, table)


def backward_kernel(info, far, probe, patch, f0, f1, f2, f3, table,
                    mine, theirs, g0, g1, g2, g3, factor, grad, held, left_table, right_table,
                    table_sem):
    mode = pl.program_id(0)
    me = info[5]
    first = info[6] == 0

    @pl.when(mode == 0)
    def _():
        expand_table(table, held, left_table, right_table, table_sem)
        for j, part in enumerate((f0, f1, f2, f3)):
            start = pl.multiple_of(lax.rem(me + N_MODE - j, N_MODE) * 64, 64)
            factor[:, pl.ds(start, 64), :] = part[...]

    probe_re, probe_im = probe[0, 0], probe[0, 1]
    own_term, other_term = 0.0, 0.0
    for s in range(2):
        change_re = (factor[s] * far[s, 0, 0]).astype(BF16)
        change_im = (factor[s] * far[s, 0, 1]).astype(BF16)
        back = jnp.dot(right_table[...], jnp.concatenate([change_re, change_im], axis=0),
                       preferred_element_type=F32).astype(BF16)
        back = jnp.concatenate([back[:SIDE], back[SIDE:]], axis=1)
        both = jnp.dot(back, left_table[...], preferred_element_type=F32)
        delta_re, delta_im = both[:, :SIDE], both[:, SIDE:]
        patch_re, patch_im = patch[s, 0], patch[s, 1]
        term_re = patch_re * delta_re + patch_im * delta_im
        term_im = patch_re * delta_im - patch_im * delta_re
        own_term += jnp.where(first, term_re, term_im)
        other_term += jnp.where(first, term_im, term_re)
        grad_re = probe_re * delta_re + probe_im * delta_im
        grad_im = probe_re * delta_im - probe_im * delta_re
        grad[s, 0] = jnp.where(mode == 0, grad_re, grad[s, 0] + grad_re)
        grad[s, 1] = jnp.where(mode == 0, grad_im, grad[s, 1] + grad_im)
    mine[0] = own_term
    theirs[0] = other_term

    @pl.when(mode == 2)
    def _():
        for j, out in enumerate((g0, g1, g2, g3)):
            base = lax.rem(me + j, N_MODE) * SUB
            for q in range(8):
                start = pl.multiple_of(base + PIECE_R * (q // 2), SUB)
                out[:, q] = grad[:, :, pl.ds(start, SUB), PIECE_C * (q % 2):PIECE_C * (q % 2 + 1)]


def backward(info, far, probe, patch, factors, table):
    full = lambda *shape: pl.BlockSpec(shape, lambda k: (0,) * len(shape))
    return pl.pallas_call(
        backward_kernel,
        grid=(3,),
        in_specs=[SMEM,
                  pl.BlockSpec((2, 1, 2, SIDE, SIDE), lambda k: (0, k, 0, 0, 0)),
                  pl.BlockSpec((1, 2, SIDE, SIDE), lambda k: (k, 0, 0, 0)),
                  full(2, 2, SIDE, SIDE)] + [full(2, 64, SIDE)] * 4
        + [HBM],
        out_specs=[pl.BlockSpec((1, SIDE, SIDE), lambda k: (k, 0, 0))] * 2
        + [full(2, 8, 2, SUB, PIECE_C)] * 4,
        out_shape=[jax.ShapeDtypeStruct((3, SIDE, SIDE), F32)] * 2
        + [jax.ShapeDtypeStruct((2, 8, 2, SUB, PIECE_C), F32)] * 4,
        scratch_shapes=[pltpu.VMEM((2, SIDE, SIDE), F32), pltpu.VMEM((2, 2, SIDE, SIDE), F32),
                        pltpu.VMEM((2, SIDE, SIDE), BF16), pltpu.VMEM((512, 512), BF16),
                        pltpu.VMEM((512, 512), BF16),
                        pltpu.SemaphoreType.DMA],
        compiler_params=pltpu.CompilerParams(vmem_limit_bytes=VMEM_BYTES),
        cost_estimate=pl.CostEstimate(flops=1700000000, bytes_accessed=12000000, transcendentals=0),
        name="backward",
    )(info, far, probe, patch, *factors, table)


def scatter_kernel(info, g0, g1, g2, g3, own, right, low, corner, canvas):
    canvas[...] = jnp.zeros_like(canvas)
    for s in range(2):
        for q in range(8):
            index = canvas_index(info[2 * s] + q // 2, info[2 * s + 1] + q % 2)
            canvas[index] += (g0[s, q] + g1[s, q]) + (g2[s, q] + g3[s, q])
    own[...] = canvas[:24]
    rows = lax.broadcasted_iota(jnp.int32, (2, SUB, PIECE_C), 1)
    note = jnp.zeros((2, SUB, PIECE_C), F32)
    for i in range(5):
        note = jnp.where(rows == i, info[i].astype(F32), note)
    for out, begin, size in ((right, 24, 6), (low, 30, 12), (corner, 42, 3)):
        out[:size] = canvas[begin:begin + size]
        out[size] = note


def scatter(info, parts):
    pieces = lambda n: jax.ShapeDtypeStruct((n, 2, SUB, PIECE_C), F32)
    return pl.pallas_call(
        scatter_kernel,
        in_specs=[SMEM] + [VMEM] * 4,
        out_specs=[VMEM] * 4,
        out_shape=[pieces(24), pieces(7), pieces(13), pieces(4)],
        scratch_shapes=[pltpu.VMEM((45, 2, SUB, PIECE_C), F32)],
        compiler_params=pltpu.CompilerParams(vmem_limit_bytes=SMALL_BYTES),
        cost_estimate=pl.CostEstimate(flops=1000000, bytes_accessed=2000000, transcendentals=0),
        name="scatter",
    )(info, *parts)


def update_kernel(info, pieces, own, right, low, corner, light, new, old, weight, notes, sems):
    start = pl.multiple_of(info[5] * SUB, SUB)
    fetch = pltpu.make_async_copy(pieces.at[:, :, pl.ds(start, SUB), :], old, sems.at[3])
    fetch.start()
    reads = [pltpu.make_async_copy(part.at[size, 0], notes.at[n], sems.at[n])
             for n, (part, size) in enumerate(((right, 6), (low, 12), (corner, 3)))]
    for read in reads:
        read.start()
    weight[...] = jnp.zeros_like(weight)

    def add_slot(top, left, live, classes):
        @pl.when(live)
        def _():
            for q in classes:
                row = top + q // 2
                col = left + q % 2

                @pl.when((row >= 0) & (row < TILE_R) & (col >= 0) & (col < TILE_C))
                def _():
                    weight[row * TILE_C + col] += light[
                        q // 2, :, PIECE_C * (q % 2):PIECE_C * (q % 2 + 1)]

    for s in range(2):
        add_slot(info[2 * s], info[2 * s + 1], s < info[4], range(8))
    for read in reads:
        read.wait()
    for n, (down, across, classes) in enumerate((
            (0, TILE_C, (1, 3, 5, 7)), (TILE_R, 0, (2, 3, 4, 5, 6, 7)), (TILE_R, TILE_C, (3, 5, 7)))):
        for s in range(2):
            top = notes[n, 2 * s, 0].astype(jnp.int32) - down
            left = notes[n, 2 * s + 1, 0].astype(jnp.int32) - across
            live = s < notes[n, 4, 0].astype(jnp.int32)
            add_slot(top, left, live & (top > -4) & (left > -2), classes)
    fetch.wait()
    for p in range(TILE_R * TILE_C):
        row, col = p // TILE_C, p % TILE_C
        total = own[p]
        if row < 3:
            total = total + low[p]
        if col == 0:
            total = total + right[row]
        if row < 3 and col == 0:
            total = total + corner[row]
        new[p] = old[p] + total / (weight[p] + object_floor)[None]


def update(info, pieces, own, right, low, corner, light):
    shape = (TILE_R * TILE_C, 2, SUB, PIECE_C)
    return pl.pallas_call(
        update_kernel,
        in_specs=[SMEM, ANY] + [VMEM] * 5,
        out_specs=VMEM,
        out_shape=jax.ShapeDtypeStruct(shape, F32),
        scratch_shapes=[pltpu.VMEM(shape, F32), pltpu.VMEM((TILE_R * TILE_C, SUB, PIECE_C), F32),
                        pltpu.SMEM((3, SUB, PIECE_C), F32), pltpu.SemaphoreType.DMA((4,))],
        compiler_params=pltpu.CompilerParams(vmem_limit_bytes=SMALL_BYTES),
        cost_estimate=pl.CostEstimate(flops=1000000, bytes_accessed=2000000, transcendentals=0),
        name="update",
    )(info, pieces, own, right, low, corner, light)


def join_pieces_kernel(info, n0, n1, n2, n3, out, sems):
    writes = []
    for j, part in enumerate((n0, n1, n2, n3)):
        start = pl.multiple_of(lax.rem(info[5] + N_MODE - j, N_MODE) * SUB, SUB)
        writes.append(pltpu.make_async_copy(part, out.at[:, :, pl.ds(start, SUB), :], sems.at[j]))
        writes[j].start()
    for write in writes:
        write.wait()


def join_pieces(info, parts):
    return pl.pallas_call(
        join_pieces_kernel,
        in_specs=[SMEM] + [ANY] * 4,
        out_specs=pl.BlockSpec(memory_space=pltpu.HBM),
        out_shape=jax.ShapeDtypeStruct((TILE_R * TILE_C, 2, PIECE_R, PIECE_C), F32),
        scratch_shapes=[pltpu.SemaphoreType.DMA((N_MODE,))],
        compiler_params=pltpu.CompilerParams(vmem_limit_bytes=2 * 1024 * 1024),
        cost_estimate=pl.CostEstimate(flops=0, bytes_accessed=3000000, transcendentals=0),
        name="join_pieces",
    )(info, *parts)


def join_channels_kernel(info, mine, theirs, out, sems):
    core = info[6]
    writes = []
    for half, source in enumerate((mine, theirs)):
        channel = core if half == 0 else 1 - core
        for k in range(3):
            writes.append(pltpu.make_async_copy(
                source.at[k], out.at[k, channel], sems.at[half, k]))
            writes[-1].start()
    for write in writes:
        write.wait()


def join_channels(info, mine, theirs):
    return pl.pallas_call(
        join_channels_kernel,
        in_specs=[SMEM, ANY, ANY],
        out_specs=pl.BlockSpec(memory_space=pltpu.HBM),
        out_shape=jax.ShapeDtypeStruct((3, 2, SIDE, SIDE), F32),
        scratch_shapes=[pltpu.SemaphoreType.DMA((2, 3))],
        compiler_params=pltpu.CompilerParams(vmem_limit_bytes=2 * 1024 * 1024),
        cost_estimate=pl.CostEstimate(flops=0, bytes_accessed=3000000, transcendentals=0),
        name="join_channels",
    )(info, mine, theirs)


def spread_sum_kernel(pieces, out):
    total = jnp.sum(pieces[...], axis=0)
    out[...] = jnp.broadcast_to(total[None], out.shape)


def spread_sum(pieces):
    return pl.pallas_call(
        spread_sum_kernel,
        in_specs=[VMEM],
        out_specs=VMEM,
        out_shape=jax.ShapeDtypeStruct(pieces.shape, F32),
        compiler_params=pltpu.CompilerParams(vmem_limit_bytes=SMALL_BYTES),
        cost_estimate=pl.CostEstimate(flops=200000, bytes_accessed=1600000, transcendentals=0),
        name="spread_sum",
    )(pieces)


def body(object_pieces, probe_modes, intensity, positions, counts):
    tile_index = lax.axis_index("tile")
    mode_index = lax.axis_index("mode")
    table = fourier_table()
    tile_grid = object_pieces.reshape(TILE_R, TILE_C, 2, PIECE_R, PIECE_C)
    own_rows = lax.dynamic_slice_in_dim(object_pieces[:12], mode_index * SUB, SUB, axis=2)
    low = shifted(own_rows, -DEV_COLS)
    corner = shifted(own_rows[::TILE_C], -DEV_COLS - 1)
    right = shifted(tile_grid[:, 0], -1)
    below = jnp.concatenate([low, corner], axis=0)
    dev_row = tile_index // DEV_COLS
    dev_col = tile_index % DEV_COLS
    rows = jnp.clip(positions[:, 0] // PIECE_R - dev_row * TILE_R, 0, TILE_R - 1)
    cols = jnp.clip(positions[:, 1] // PIECE_C - dev_col * TILE_C, 0, TILE_C - 1)
    info = jnp.stack([rows[0], cols[0], rows[1], cols[1], counts[0], mode_index,
                      tile_index % 2, tile_index]).astype(jnp.int32)
    late_modes, below = lax.optimization_barrier((probe_modes, below))
    light_local = jnp.sum(late_modes * late_modes, axis=(0, 1))
    light_parts = light_local.reshape(4, N_MODE, SUB, SIDE).transpose(1, 0, 2, 3)
    light = lax.psum_scatter(light_parts, "mode", scatter_dimension=0, tiled=True)
    below = [below] + [turned(below, j) for j in (1, 2, 3)]

    far, patch, *powers = forward(info, in_hbm(object_pieces), in_hbm(right),
                                  [in_hbm(block) for block in below], probe_modes, in_hbm(table))
    received = [turned(powers[j], j) for j in (1, 2, 3)]
    power = (powers[0] + received[0]) + (received[1] + received[2])
    own_intensity = lax.dynamic_slice_in_dim(intensity, mode_index * 64, 64, axis=1)
    live = (jnp.arange(2, dtype=jnp.int32) < counts[0]).astype(F32)
    factor = live[:, None, None] * (jnp.sqrt(own_intensity) / jnp.sqrt(power + far_floor) - 1.0)
    factors = [factor] + [turned(factor, j) for j in (1, 2, 3)]

    mine, theirs, *grads = backward(info, in_hbm(far), probe_modes, patch, factors, in_hbm(table))

    groups = [list(range(core, N_TILE, 2)) for core in range(2)]
    exchange = lambda blocks: lax.all_to_all(
        blocks, "tile", 0, 0, axis_index_groups=groups, tiled=True)
    summed = mine + core_swap(theirs)
    pieces = exchange(summed.reshape(N_CHIP, PART, SIDE))
    parts = [grads[0]] + [turned(grads[j], j) for j in (1, 2, 3)]
    own, to_right, to_low, to_corner = scatter(info, parts)
    from_above = shifted(to_low, DEV_COLS)
    from_corner = shifted(to_corner, DEV_COLS + 1)
    from_left = shifted(to_right, 1)
    shares = spread_sum(pieces)
    shares, from_left, from_above, from_corner = lax.optimization_barrier(
        (shares, from_left, from_above, from_corner))

    new = update(info, object_pieces, own, from_left, from_above, from_corner, in_hbm(light[0]))
    shares, new = lax.optimization_barrier((shares, new))
    gathered = exchange(shares)
    new_parts = [new] + [turned(new, j) for j in (1, 2, 3)]
    gathered, *new_parts = lax.optimization_barrier((gathered, *new_parts))
    gathered = gathered.reshape(3, SIDE, SIDE)
    probe_grad = join_channels(info, gathered, core_swap(gathered))
    return (join_pieces(info, new_parts), probe_grad)


def solution(mesh):
    return jax.shard_map(
        body,
        mesh=mesh,
        in_specs=(
            P("tile", None, None, None),
            P("mode", None, None, None),
            P("tile", None, None),
            P("tile", None),
            P("tile"),
        ),
        out_specs=(P("tile", None, None, None), P("mode", None, None, None)),
        check_vma=False,
    )
```

```python
import math

import jax
import jax.numpy as jnp
import numpy as np
from jax import lax
from jax.experimental import pallas as pl
from jax.experimental.pallas import tpu as pltpu
from jax.sharding import PartitionSpec as P

DEV_COLS = 8
TILE_R = 6
TILE_C = 4
SIDE = 256
PIECE_R = 64
PIECE_C = 128
N_MODE = 4
N_TILE = 64
SUB = PIECE_R // N_MODE
N_CHIP = N_TILE // 2
PART = 3 * SIDE // N_CHIP
VMEM_BYTES = 24 * 1024 * 1024
FORWARD_BYTES = 40 * 1024 * 1024
SMALL_BYTES = 8 * 1024 * 1024

far_floor = 0.1
object_floor = 0.1

F32 = jnp.float32
BF16 = jnp.bfloat16
ANY = pl.BlockSpec(memory_space=pl.ANY)
HBM = pl.BlockSpec(memory_space=pltpu.HBM)
SMEM = pl.BlockSpec(memory_space=pltpu.SMEM)
VMEM = pl.BlockSpec(memory_space=pltpu.VMEM)


def shifted(block, distance):
    return lax.ppermute(block, "tile", [(d, (d + distance) % N_TILE) for d in range(N_TILE)])


def turned(block, distance):
    return lax.ppermute(block, "mode", [(i, (i + distance) % N_MODE) for i in range(N_MODE)])


def core_swap(block):
    return lax.ppermute(block, "tile", [(d, d ^ 1) for d in range(N_TILE)])


def in_hbm(block):
    return pltpu.with_memory_space_constraint(block, pltpu.HBM)


def fourier_table():
    indices = np.arange(SIDE)
    phases = (indices[:, None] * indices[None, :] % SIDE) * (2.0 * math.pi / SIDE)
    scaling = 1.0 / math.sqrt(SIDE)
    both = np.stack([np.cos(phases) * scaling, -np.sin(phases) * scaling])
    return jnp.asarray(both.astype(np.float32).astype(jnp.bfloat16))


def expand_table(table, held, left, right, sem):
    fetch = pltpu.make_async_copy(table, held, sem)
    fetch.start()
    fetch.wait()
    re, im = held[0], held[1]
    for out in (left, right):
        out[:SIDE, :SIDE] = re
        out[SIDE:, SIDE:] = re
    left[:SIDE, SIDE:] = -im
    left[SIDE:, :SIDE] = im
    right[:SIDE, SIDE:] = im
    right[SIDE:, :SIDE] = -im


def canvas_index(row, col):
    inside = jnp.where(col < TILE_C, row * TILE_C + col, 24 + row)
    below = jnp.where(col < TILE_C, 30 + (row - TILE_R) * TILE_C + col, 42 + row - TILE_R)
    return jnp.where(row < TILE_R, inside, below)


def forward_kernel(info, own, right, b0, b1, b2, b3, probe, table,
                   far, patch, p0, p1, p2, p3, power, held, left_table, right_table, sems, table_sem):
    mode = pl.program_id(0)

    def piece_copy(s, q, source, index):
        target = patch.at[s, :, pl.ds(PIECE_R * (q // 2), PIECE_R), pl.ds(PIECE_C * (q % 2), PIECE_C)]
        return pltpu.make_async_copy(source.at[index], target, sems.at[s, q])

    @pl.when(mode == 0)
    def _():
        for s in range(2):
            for q in range(8):
                row = info[2 * s] + q // 2
                col = info[2 * s + 1] + q % 2
                upper = row < TILE_R
                inner = col < TILE_C

                @pl.when(upper & inner)
                def _():
                    piece_copy(s, q, own, row * TILE_C + col).start()

                @pl.when(upper & jnp.logical_not(inner))
                def _():
                    piece_copy(s, q, right, row).start()

                @pl.when(jnp.logical_not(upper))
                def _():
                    below = jnp.where(inner, (row - TILE_R) * TILE_C + col, 12 + row - TILE_R)
                    for j, source in enumerate((b0, b1, b2, b3)):
                        start = lax.rem(info[5] + N_MODE - j, N_MODE) * SUB + PIECE_R * (q // 2)
                        target = patch.at[s, :, pl.ds(pl.multiple_of(start, SUB), SUB),
                                          pl.ds(PIECE_C * (q % 2), PIECE_C)]
                        pltpu.make_async_copy(source.at[below], target, sems.at[s, q]).start()

        expand_table(table, held, left_table, right_table, table_sem)
        for s in range(2):
            for q in range(8):
                piece_copy(s, q, own, 0).wait()

    probe_re, probe_im = probe[0, 0], probe[0, 1]
    for s in range(2):
        patch_re, patch_im = patch[s, 0], patch[s, 1]
        exit_re = (probe_re * patch_re - probe_im * patch_im).astype(BF16)
        exit_im = (probe_re * patch_im + probe_im * patch_re).astype(BF16)
        half = jnp.dot(left_table[...], jnp.concatenate([exit_re, exit_im], axis=0),
                       preferred_element_type=F32).astype(BF16)
        half = jnp.concatenate([half[:SIDE], half[SIDE:]], axis=1)
        both = jnp.dot(half, right_table[...], preferred_element_type=F32)
        far_re, far_im = both[:, :SIDE], both[:, SIDE:]
        far[s, 0, 0] = far_re
        far[s, 0, 1] = far_im
        local = far_re * far_re + far_im * far_im
        power[s] = jnp.where(mode == 0, local, power[s] + local)

    @pl.when(mode == 2)
    def _():
        for j, out in enumerate((p0, p1, p2, p3)):
            start = pl.multiple_of(lax.rem(info[5] + j, N_MODE) * 64, 64)
            out[...] = power[:, pl.ds(start, 64), :]


def forward(info, own, right, below, probe, table):
    full = lambda *shape: pl.BlockSpec(shape, lambda k: (0,) * len(shape))
    return pl.pallas_call(
        forward_kernel,
        grid=(3,),
        in_specs=[SMEM] + [HBM] * 6 + [
                  pl.BlockSpec((1, 2, SIDE, SIDE), lambda k: (k, 0, 0, 0)),
                  HBM],
        out_specs=[pl.BlockSpec((2, 1, 2, SIDE, SIDE), lambda k: (0, k, 0, 0, 0)),
                   full(2, 2, SIDE, SIDE)] + [full(2, 64, SIDE)] * 4,
        out_shape=[pltpu.HBM((2, 3, 2, SIDE, SIDE), F32),
                   jax.ShapeDtypeStruct((2, 2, SIDE, SIDE), F32)]
        + [jax.ShapeDtypeStruct((2, 64, SIDE), F32)] * 4,
        scratch_shapes=[pltpu.VMEM((2, SIDE, SIDE), F32), pltpu.VMEM((2, SIDE, SIDE), BF16), pltpu.VMEM((512, 512), BF16),
                        pltpu.VMEM((512, 512), BF16),
                        pltpu.SemaphoreType.DMA((2, 8)), pltpu.SemaphoreType.DMA],
        compiler_params=pltpu.CompilerParams(vmem_limit_bytes=FORWARD_BYTES),
        cost_estimate=pl.CostEstimate(flops=1700000000, bytes_accessed=12000000, transcendentals=0),
        name="forward",
    )(info, own, right, *below, probe, table)


def backward_kernel(info, far, probe, patch, f0, f1, f2, f3, table,
                    mine, theirs, g0, g1, g2, g3, factor, grad, held, left_table, right_table,
                    table_sem):
    mode = pl.program_id(0)
    me = info[5]
    first = info[6] == 0

    @pl.when(mode == 0)
    def _():
        expand_table(table, held, left_table, right_table, table_sem)
        for j, part in enumerate((f0, f1, f2, f3)):
            start = pl.multiple_of(lax.rem(me + N_MODE - j, N_MODE) * 64, 64)
            factor[:, pl.ds(start, 64), :] = part[...]

    probe_re, probe_im = probe[0, 0], probe[0, 1]
    own_term, other_term = 0.0, 0.0
    for s in range(2):
        change_re = (factor[s] * far[s, 0, 0]).astype(BF16)
        change_im = (factor[s] * far[s, 0, 1]).astype(BF16)
        back = jnp.dot(right_table[...], jnp.concatenate([change_re, change_im], axis=0),
                       preferred_element_type=F32).astype(BF16)
        back = jnp.concatenate([back[:SIDE], back[SIDE:]], axis=1)
        both = jnp.dot(back, left_table[...], preferred_element_type=F32)
        delta_re, delta_im = both[:, :SIDE], both[:, SIDE:]
        patch_re, patch_im = patch[s, 0], patch[s, 1]
        term_re = patch_re * delta_re + patch_im * delta_im
        term_im = patch_re * delta_im - patch_im * delta_re
        own_term += jnp.where(first, term_re, term_im)
        other_term += jnp.where(first, term_im, term_re)
        grad_re = probe_re * delta_re + probe_im * delta_im
        grad_im = probe_re * delta_im - probe_im * delta_re
        grad[s, 0] = jnp.where(mode == 0, grad_re, grad[s, 0] + grad_re)
        grad[s, 1] = jnp.where(mode == 0, grad_im, grad[s, 1] + grad_im)
    mine[0] = own_term
    theirs[0] = other_term

    @pl.when(mode == 2)
    def _():
        for j, out in enumerate((g0, g1, g2, g3)):
            base = lax.rem(me + j, N_MODE) * SUB
            for q in range(8):
                start = pl.multiple_of(base + PIECE_R * (q // 2), SUB)
                out[:, q] = grad[:, :, pl.ds(start, SUB), PIECE_C * (q % 2):PIECE_C * (q % 2 + 1)]


def backward(info, far, probe, patch, factors, table):
    full = lambda *shape: pl.BlockSpec(shape, lambda k: (0,) * len(shape))
    return pl.pallas_call(
        backward_kernel,
        grid=(3,),
        in_specs=[SMEM,
                  pl.BlockSpec((2, 1, 2, SIDE, SIDE), lambda k: (0, k, 0, 0, 0)),
                  pl.BlockSpec((1, 2, SIDE, SIDE), lambda k: (k, 0, 0, 0)),
                  full(2, 2, SIDE, SIDE)] + [full(2, 64, SIDE)] * 4
        + [HBM],
        out_specs=[pl.BlockSpec((1, SIDE, SIDE), lambda k: (k, 0, 0))] * 2
        + [full(2, 8, 2, SUB, PIECE_C)] * 4,
        out_shape=[jax.ShapeDtypeStruct((3, SIDE, SIDE), F32)] * 2
        + [jax.ShapeDtypeStruct((2, 8, 2, SUB, PIECE_C), F32)] * 4,
        scratch_shapes=[pltpu.VMEM((2, SIDE, SIDE), F32), pltpu.VMEM((2, 2, SIDE, SIDE), F32),
                        pltpu.VMEM((2, SIDE, SIDE), BF16), pltpu.VMEM((512, 512), BF16),
                        pltpu.VMEM((512, 512), BF16),
                        pltpu.SemaphoreType.DMA],
        compiler_params=pltpu.CompilerParams(vmem_limit_bytes=VMEM_BYTES),
        cost_estimate=pl.CostEstimate(flops=1700000000, bytes_accessed=12000000, transcendentals=0),
        name="backward",
    )(info, far, probe, patch, *factors, table)


def scatter_kernel(info, g0, g1, g2, g3, own, right, low, corner, canvas):
    canvas[...] = jnp.zeros_like(canvas)
    for s in range(2):
        for q in range(8):
            index = canvas_index(info[2 * s] + q // 2, info[2 * s + 1] + q % 2)
            canvas[index] += (g0[s, q] + g1[s, q]) + (g2[s, q] + g3[s, q])
    own[...] = canvas[:24]
    rows = lax.broadcasted_iota(jnp.int32, (2, SUB, PIECE_C), 1)
    note = jnp.zeros((2, SUB, PIECE_C), F32)
    for i in range(5):
        note = jnp.where(rows == i, info[i].astype(F32), note)
    for out, begin, size in ((right, 24, 6), (low, 30, 12), (corner, 42, 3)):
        out[:size] = canvas[begin:begin + size]
        out[size] = note


def scatter(info, parts):
    pieces = lambda n: jax.ShapeDtypeStruct((n, 2, SUB, PIECE_C), F32)
    return pl.pallas_call(
        scatter_kernel,
        in_specs=[SMEM] + [VMEM] * 4,
        out_specs=[VMEM] * 4,
        out_shape=[pieces(24), pieces(7), pieces(13), pieces(4)],
        scratch_shapes=[pltpu.VMEM((45, 2, SUB, PIECE_C), F32)],
        compiler_params=pltpu.CompilerParams(vmem_limit_bytes=SMALL_BYTES),
        cost_estimate=pl.CostEstimate(flops=1000000, bytes_accessed=2000000, transcendentals=0),
        name="scatter",
    )(info, *parts)


def update_kernel(info, pieces, own, right, low, corner, light, new, old, weight, notes, sems):
    start = pl.multiple_of(info[5] * SUB, SUB)
    fetch = pltpu.make_async_copy(pieces.at[:, :, pl.ds(start, SUB), :], old, sems.at[3])
    fetch.start()
    reads = [pltpu.make_async_copy(part.at[size, 0], notes.at[n], sems.at[n])
             for n, (part, size) in enumerate(((right, 6), (low, 12), (corner, 3)))]
    for read in reads:
        read.start()
    weight[...] = jnp.zeros_like(weight)

    def add_slot(top, left, live, classes):
        @pl.when(live)
        def _():
            for q in classes:
                row = top + q // 2
                col = left + q % 2

                @pl.when((row >= 0) & (row < TILE_R) & (col >= 0) & (col < TILE_C))
                def _():
                    weight[row * TILE_C + col] += light[
                        q // 2, :, PIECE_C * (q % 2):PIECE_C * (q % 2 + 1)]

    for s in range(2):
        add_slot(info[2 * s], info[2 * s + 1], s < info[4], range(8))
    for read in reads:
        read.wait()
    for n, (down, across, classes) in enumerate((
            (0, TILE_C, (1, 3, 5, 7)), (TILE_R, 0, (2, 3, 4, 5, 6, 7)), (TILE_R, TILE_C, (3, 5, 7)))):
        for s in range(2):
            top = notes[n, 2 * s, 0].astype(jnp.int32) - down
            left = notes[n, 2 * s + 1, 0].astype(jnp.int32) - across
            live = s < notes[n, 4, 0].astype(jnp.int32)
            add_slot(top, left, live & (top > -4) & (left > -2), classes)
    fetch.wait()
    for p in range(TILE_R * TILE_C):
        row, col = p // TILE_C, p % TILE_C
        total = own[p]
        if row < 3:
            total = total + low[p]
        if col == 0:
            total = total + right[row]
        if row < 3 and col == 0:
            total = total + corner[row]
        new[p] = old[p] + total / (weight[p] + object_floor)[None]


def update(info, pieces, own, right, low, corner, light):
    shape = (TILE_R * TILE_C, 2, SUB, PIECE_C)
    return pl.pallas_call(
        update_kernel,
        in_specs=[SMEM, ANY] + [VMEM] * 5,
        out_specs=VMEM,
        out_shape=jax.ShapeDtypeStruct(shape, F32),
        scratch_shapes=[pltpu.VMEM(shape, F32), pltpu.VMEM((TILE_R * TILE_C, SUB, PIECE_C), F32),
                        pltpu.SMEM((3, SUB, PIECE_C), F32), pltpu.SemaphoreType.DMA((4,))],
        compiler_params=pltpu.CompilerParams(vmem_limit_bytes=SMALL_BYTES),
        cost_estimate=pl.CostEstimate(flops=1000000, bytes_accessed=2000000, transcendentals=0),
        name="update",
    )(info, pieces, own, right, low, corner, light)


def join_pieces_kernel(info, n0, n1, n2, n3, out, sems):
    writes = []
    for j, part in enumerate((n0, n1, n2, n3)):
        start = pl.multiple_of(lax.rem(info[5] + N_MODE - j, N_MODE) * SUB, SUB)
        writes.append(pltpu.make_async_copy(part, out.at[:, :, pl.ds(start, SUB), :], sems.at[j]))
        writes[j].start()
    for write in writes:
        write.wait()


def join_pieces(info, parts):
    return pl.pallas_call(
        join_pieces_kernel,
        in_specs=[SMEM] + [ANY] * 4,
        out_specs=pl.BlockSpec(memory_space=pltpu.HBM),
        out_shape=jax.ShapeDtypeStruct((TILE_R * TILE_C, 2, PIECE_R, PIECE_C), F32),
        scratch_shapes=[pltpu.SemaphoreType.DMA((N_MODE,))],
        compiler_params=pltpu.CompilerParams(vmem_limit_bytes=2 * 1024 * 1024),
        cost_estimate=pl.CostEstimate(flops=0, bytes_accessed=3000000, transcendentals=0),
        name="join_pieces",
    )(info, *parts)


def join_channels_kernel(info, mine, theirs, out, sems):
    core = info[6]
    writes = []
    for half, source in enumerate((mine, theirs)):
        channel = core if half == 0 else 1 - core
        for k in range(3):
            writes.append(pltpu.make_async_copy(
                source.at[k], out.at[k, channel], sems.at[half, k]))
            writes[-1].start()
    for write in writes:
        write.wait()


def join_channels(info, mine, theirs):
    return pl.pallas_call(
        join_channels_kernel,
        in_specs=[SMEM, ANY, ANY],
        out_specs=pl.BlockSpec(memory_space=pltpu.HBM),
        out_shape=jax.ShapeDtypeStruct((3, 2, SIDE, SIDE), F32),
        scratch_shapes=[pltpu.SemaphoreType.DMA((2, 3))],
        compiler_params=pltpu.CompilerParams(vmem_limit_bytes=2 * 1024 * 1024),
        cost_estimate=pl.CostEstimate(flops=0, bytes_accessed=3000000, transcendentals=0),
        name="join_channels",
    )(info, mine, theirs)


def body(object_pieces, probe_modes, intensity, positions, counts):
    tile_index = lax.axis_index("tile")
    mode_index = lax.axis_index("mode")
    table = fourier_table()
    tile_grid = object_pieces.reshape(TILE_R, TILE_C, 2, PIECE_R, PIECE_C)
    own_rows = lax.dynamic_slice_in_dim(object_pieces[:12], mode_index * SUB, SUB, axis=2)
    low = shifted(own_rows, -DEV_COLS)
    corner = shifted(own_rows[::TILE_C], -DEV_COLS - 1)
    right = shifted(tile_grid[:, 0], -1)
    below = jnp.concatenate([low, corner], axis=0)
    dev_row = tile_index // DEV_COLS
    dev_col = tile_index % DEV_COLS
    rows = jnp.clip(positions[:, 0] // PIECE_R - dev_row * TILE_R, 0, TILE_R - 1)
    cols = jnp.clip(positions[:, 1] // PIECE_C - dev_col * TILE_C, 0, TILE_C - 1)
    info = jnp.stack([rows[0], cols[0], rows[1], cols[1], counts[0], mode_index,
                      tile_index % 2, tile_index]).astype(jnp.int32)
    late_modes, below = lax.optimization_barrier((probe_modes, below))
    light_local = jnp.sum(late_modes * late_modes, axis=(0, 1))
    light_parts = light_local.reshape(4, N_MODE, SUB, SIDE).transpose(1, 0, 2, 3)
    light = lax.psum_scatter(light_parts, "mode", scatter_dimension=0, tiled=True)
    below = [below] + [turned(below, j) for j in (1, 2, 3)]

    far, patch, *powers = forward(info, in_hbm(object_pieces), in_hbm(right),
                                  [in_hbm(block) for block in below], probe_modes, in_hbm(table))
    received = [turned(powers[j], j) for j in (1, 2, 3)]
    power = (powers[0] + received[0]) + (received[1] + received[2])
    own_intensity = lax.dynamic_slice_in_dim(intensity, mode_index * 64, 64, axis=1)
    live = (jnp.arange(2, dtype=jnp.int32) < counts[0]).astype(F32)
    factor = live[:, None, None] * (jnp.sqrt(own_intensity) / jnp.sqrt(power + far_floor) - 1.0)
    factors = [factor] + [turned(factor, j) for j in (1, 2, 3)]

    mine, theirs, *grads = backward(info, in_hbm(far), probe_modes, patch, factors, in_hbm(table))

    groups = [list(range(core, N_TILE, 2)) for core in range(2)]
    exchange = lambda blocks: lax.all_to_all(
        blocks, "tile", 0, 0, axis_index_groups=groups, tiled=True)
    summed = mine + core_swap(theirs)
    pieces = exchange(summed.reshape(N_CHIP, PART, SIDE))
    parts = [grads[0]] + [turned(grads[j], j) for j in (1, 2, 3)]
    own, to_right, to_low, to_corner = scatter(info, parts)
    from_above = shifted(to_low, DEV_COLS)
    from_corner = shifted(to_corner, DEV_COLS + 1)
    from_left = shifted(to_right, 1)
    shares = jnp.broadcast_to(jnp.sum(pieces, axis=0)[None], (N_CHIP, PART, SIDE))
    shares, from_left, from_above, from_corner = lax.optimization_barrier(
        (shares, from_left, from_above, from_corner))

    new = update(info, object_pieces, own, from_left, from_above, from_corner, in_hbm(light[0]))
    shares, new = lax.optimization_barrier((shares, new))
    gathered = exchange(shares)
    new_parts = [new] + [turned(new, j) for j in (1, 2, 3)]
    gathered, *new_parts = lax.optimization_barrier((gathered, *new_parts))
    gathered = gathered.reshape(3, SIDE, SIDE)
    probe_grad = join_channels(info, gathered, core_swap(gathered))
    return (join_pieces(info, new_parts), probe_grad)


def solution(mesh):
    return jax.shard_map(
        body,
        mesh=mesh,
        in_specs=(
            P("tile", None, None, None),
            P("mode", None, None, None),
            P("tile", None, None),
            P("tile", None),
            P("tile"),
        ),
        out_specs=(P("tile", None, None, None), P("mode", None, None, None)),
        check_vma=False,
    )
```

```python
import math

import jax
import jax.numpy as jnp
import numpy as np
from jax import lax
from jax.experimental import pallas as pl
from jax.experimental.pallas import tpu as pltpu
from jax.sharding import PartitionSpec as P

DEV_COLS = 8
TILE_R = 6
TILE_C = 4
SIDE = 256
PIECE_R = 64
PIECE_C = 128
N_MODE = 4
N_TILE = 64
SUB = PIECE_R // N_MODE
N_CHIP = N_TILE // 2
PART = 3 * SIDE // N_CHIP
VMEM_BYTES = 24 * 1024 * 1024
FORWARD_BYTES = 40 * 1024 * 1024
SMALL_BYTES = 8 * 1024 * 1024

far_floor = 0.1
object_floor = 0.1

F32 = jnp.float32
BF16 = jnp.bfloat16
ANY = pl.BlockSpec(memory_space=pl.ANY)
HBM = pl.BlockSpec(memory_space=pltpu.HBM)
SMEM = pl.BlockSpec(memory_space=pltpu.SMEM)
VMEM = pl.BlockSpec(memory_space=pltpu.VMEM)


def shifted(block, distance):
    return lax.ppermute(block, "tile", [(d, (d + distance) % N_TILE) for d in range(N_TILE)])


def turned(block, distance):
    return lax.ppermute(block, "mode", [(i, (i + distance) % N_MODE) for i in range(N_MODE)])


def core_swap(block):
    return lax.ppermute(block, "tile", [(d, d ^ 1) for d in range(N_TILE)])


def in_hbm(block):
    return pltpu.with_memory_space_constraint(block, pltpu.HBM)


def fourier_table():
    indices = np.arange(SIDE)
    phases = (indices[:, None] * indices[None, :] % SIDE) * (2.0 * math.pi / SIDE)
    scaling = 1.0 / math.sqrt(SIDE)
    both = np.stack([np.cos(phases) * scaling, -np.sin(phases) * scaling])
    return jnp.asarray(both.astype(np.float32).astype(jnp.bfloat16))


def expand_table(table, held, left, right, sem):
    pltpu.make_async_copy(table, held, sem).wait()
    re, im = held[0], held[1]
    for out in (left, right):
        out[:SIDE, :SIDE] = re
        out[SIDE:, SIDE:] = re
    left[:SIDE, SIDE:] = -im
    left[SIDE:, :SIDE] = im
    right[:SIDE, SIDE:] = im
    right[SIDE:, :SIDE] = -im


def canvas_index(row, col):
    inside = jnp.where(col < TILE_C, row * TILE_C + col, 24 + row)
    below = jnp.where(col < TILE_C, 30 + (row - TILE_R) * TILE_C + col, 42 + row - TILE_R)
    return jnp.where(row < TILE_R, inside, below)


def forward_kernel(info, own, right, b0, b1, b2, b3, probe, table,
                   far, patch, p0, p1, p2, p3, power, held, left_table, right_table, sems, table_sem):
    mode = pl.program_id(0)

    def piece_copy(s, q, source, index):
        target = patch.at[s, :, pl.ds(PIECE_R * (q // 2), PIECE_R), pl.ds(PIECE_C * (q % 2), PIECE_C)]
        return pltpu.make_async_copy(source.at[index], target, sems.at[s, q])

    @pl.when(mode == 0)
    def _():
        pltpu.make_async_copy(table, held, table_sem).start()
        for s in range(2):
            for q in range(8):
                row = info[2 * s] + q // 2
                col = info[2 * s + 1] + q % 2
                upper = row < TILE_R
                inner = col < TILE_C

                @pl.when(upper & inner)
                def _():
                    piece_copy(s, q, own, row * TILE_C + col).start()

                @pl.when(upper & jnp.logical_not(inner))
                def _():
                    piece_copy(s, q, right, row).start()

                @pl.when(jnp.logical_not(upper))
                def _():
                    below = jnp.where(inner, (row - TILE_R) * TILE_C + col, 12 + row - TILE_R)
                    for j, source in enumerate((b0, b1, b2, b3)):
                        start = lax.rem(info[5] + N_MODE - j, N_MODE) * SUB + PIECE_R * (q // 2)
                        target = patch.at[s, :, pl.ds(pl.multiple_of(start, SUB), SUB),
                                          pl.ds(PIECE_C * (q % 2), PIECE_C)]
                        pltpu.make_async_copy(source.at[below], target, sems.at[s, q]).start()

        expand_table(table, held, left_table, right_table, table_sem)
        for s in range(2):
            for q in range(8):
                piece_copy(s, q, own, 0).wait()

    probe_re, probe_im = probe[0, 0], probe[0, 1]
    for s in range(2):
        patch_re, patch_im = patch[s, 0], patch[s, 1]
        exit_re = (probe_re * patch_re - probe_im * patch_im).astype(BF16)
        exit_im = (probe_re * patch_im + probe_im * patch_re).astype(BF16)
        half = jnp.dot(left_table[...], jnp.concatenate([exit_re, exit_im], axis=0),
                       preferred_element_type=F32).astype(BF16)
        half = jnp.concatenate([half[:SIDE], half[SIDE:]], axis=1)
        both = jnp.dot(half, right_table[...], preferred_element_type=F32)
        far_re, far_im = both[:, :SIDE], both[:, SIDE:]
        far[s, 0, 0] = far_re
        far[s, 0, 1] = far_im
        local = far_re * far_re + far_im * far_im
        power[s] = jnp.where(mode == 0, local, power[s] + local)

    @pl.when(mode == 2)
    def _():
        for j, out in enumerate((p0, p1, p2, p3)):
            start = pl.multiple_of(lax.rem(info[5] + j, N_MODE) * 64, 64)
            out[...] = power[:, pl.ds(start, 64), :]


def forward(info, own, right, below, probe, table):
    full = lambda *shape: pl.BlockSpec(shape, lambda k: (0,) * len(shape))
    return pl.pallas_call(
        forward_kernel,
        grid=(3,),
        in_specs=[SMEM] + [HBM] * 6 + [
                  pl.BlockSpec((1, 2, SIDE, SIDE), lambda k: (k, 0, 0, 0)),
                  HBM],
        out_specs=[pl.BlockSpec((2, 1, 2, SIDE, SIDE), lambda k: (0, k, 0, 0, 0)),
                   full(2, 2, SIDE, SIDE)] + [full(2, 64, SIDE)] * 4,
        out_shape=[pltpu.HBM((2, 3, 2, SIDE, SIDE), F32),
                   jax.ShapeDtypeStruct((2, 2, SIDE, SIDE), F32)]
        + [jax.ShapeDtypeStruct((2, 64, SIDE), F32)] * 4,
        scratch_shapes=[pltpu.VMEM((2, SIDE, SIDE), F32), pltpu.VMEM((2, SIDE, SIDE), BF16), pltpu.VMEM((512, 512), BF16),
                        pltpu.VMEM((512, 512), BF16),
                        pltpu.SemaphoreType.DMA((2, 8)), pltpu.SemaphoreType.DMA],
        compiler_params=pltpu.CompilerParams(vmem_limit_bytes=FORWARD_BYTES),
        cost_estimate=pl.CostEstimate(flops=1700000000, bytes_accessed=12000000, transcendentals=0),
        name="forward",
    )(info, own, right, *below, probe, table)


def backward_kernel(info, far, probe, patch, f0, f1, f2, f3, table,
                    mine, theirs, g0, g1, g2, g3, factor, grad, held, left_table, right_table,
                    table_sem):
    mode = pl.program_id(0)
    me = info[5]
    first = info[6] == 0

    @pl.when(mode == 0)
    def _():
        pltpu.make_async_copy(table, held, table_sem).start()
        for j, part in enumerate((f0, f1, f2, f3)):
            start = pl.multiple_of(lax.rem(me + N_MODE - j, N_MODE) * 64, 64)
            factor[:, pl.ds(start, 64), :] = part[...]
        expand_table(table, held, left_table, right_table, table_sem)

    probe_re, probe_im = probe[0, 0], probe[0, 1]
    own_term, other_term = 0.0, 0.0
    for s in range(2):
        change_re = (factor[s] * far[s, 0, 0]).astype(BF16)
        change_im = (factor[s] * far[s, 0, 1]).astype(BF16)
        back = jnp.dot(right_table[...], jnp.concatenate([change_re, change_im], axis=0),
                       preferred_element_type=F32).astype(BF16)
        back = jnp.concatenate([back[:SIDE], back[SIDE:]], axis=1)
        both = jnp.dot(back, left_table[...], preferred_element_type=F32)
        delta_re, delta_im = both[:, :SIDE], both[:, SIDE:]
        patch_re, patch_im = patch[s, 0], patch[s, 1]
        term_re = patch_re * delta_re + patch_im * delta_im
        term_im = patch_re * delta_im - patch_im * delta_re
        own_term += jnp.where(first, term_re, term_im)
        other_term += jnp.where(first, term_im, term_re)
        grad_re = probe_re * delta_re + probe_im * delta_im
        grad_im = probe_re * delta_im - probe_im * delta_re
        grad[s, 0] = jnp.where(mode == 0, grad_re, grad[s, 0] + grad_re)
        grad[s, 1] = jnp.where(mode == 0, grad_im, grad[s, 1] + grad_im)
    mine[0] = own_term
    theirs[0] = other_term

    @pl.when(mode == 2)
    def _():
        for j, out in enumerate((g0, g1, g2, g3)):
            base = lax.rem(me + j, N_MODE) * SUB
            for q in range(8):
                start = pl.multiple_of(base + PIECE_R * (q // 2), SUB)
                out[:, q] = grad[:, :, pl.ds(start, SUB), PIECE_C * (q % 2):PIECE_C * (q % 2 + 1)]


def backward(info, far, probe, patch, factors, table):
    full = lambda *shape: pl.BlockSpec(shape, lambda k: (0,) * len(shape))
    return pl.pallas_call(
        backward_kernel,
        grid=(3,),
        in_specs=[SMEM,
                  pl.BlockSpec((2, 1, 2, SIDE, SIDE), lambda k: (0, k, 0, 0, 0)),
                  pl.BlockSpec((1, 2, SIDE, SIDE), lambda k: (k, 0, 0, 0)),
                  full(2, 2, SIDE, SIDE)] + [full(2, 64, SIDE)] * 4
        + [HBM],
        out_specs=[pl.BlockSpec((1, SIDE, SIDE), lambda k: (k, 0, 0))] * 2
        + [full(2, 8, 2, SUB, PIECE_C)] * 4,
        out_shape=[jax.ShapeDtypeStruct((3, SIDE, SIDE), F32)] * 2
        + [jax.ShapeDtypeStruct((2, 8, 2, SUB, PIECE_C), F32)] * 4,
        scratch_shapes=[pltpu.VMEM((2, SIDE, SIDE), F32), pltpu.VMEM((2, 2, SIDE, SIDE), F32),
                        pltpu.VMEM((2, SIDE, SIDE), BF16), pltpu.VMEM((512, 512), BF16),
                        pltpu.VMEM((512, 512), BF16),
                        pltpu.SemaphoreType.DMA],
        compiler_params=pltpu.CompilerParams(vmem_limit_bytes=VMEM_BYTES),
        cost_estimate=pl.CostEstimate(flops=1700000000, bytes_accessed=12000000, transcendentals=0),
        name="backward",
    )(info, far, probe, patch, *factors, table)


def scatter_kernel(info, g0, g1, g2, g3, own, right, low, corner, canvas):
    canvas[...] = jnp.zeros_like(canvas)
    for s in range(2):
        for q in range(8):
            index = canvas_index(info[2 * s] + q // 2, info[2 * s + 1] + q % 2)
            canvas[index] += (g0[s, q] + g1[s, q]) + (g2[s, q] + g3[s, q])
    own[...] = canvas[:24]
    rows = lax.broadcasted_iota(jnp.int32, (2, SUB, PIECE_C), 1)
    note = jnp.zeros((2, SUB, PIECE_C), F32)
    for i in range(5):
        note = jnp.where(rows == i, info[i].astype(F32), note)
    for out, begin, size in ((right, 24, 6), (low, 30, 12), (corner, 42, 3)):
        out[:size] = canvas[begin:begin + size]
        out[size] = note


def scatter(info, parts):
    pieces = lambda n: jax.ShapeDtypeStruct((n, 2, SUB, PIECE_C), F32)
    return pl.pallas_call(
        scatter_kernel,
        in_specs=[SMEM] + [VMEM] * 4,
        out_specs=[VMEM] * 4,
        out_shape=[pieces(24), pieces(7), pieces(13), pieces(4)],
        scratch_shapes=[pltpu.VMEM((45, 2, SUB, PIECE_C), F32)],
        compiler_params=pltpu.CompilerParams(vmem_limit_bytes=SMALL_BYTES),
        cost_estimate=pl.CostEstimate(flops=1000000, bytes_accessed=2000000, transcendentals=0),
        name="scatter",
    )(info, *parts)


def update_kernel(info, pieces, own, right, low, corner, light, new, old, weight, notes, sems):
    start = pl.multiple_of(info[5] * SUB, SUB)
    fetch = pltpu.make_async_copy(pieces.at[:, :, pl.ds(start, SUB), :], old, sems.at[3])
    fetch.start()
    reads = [pltpu.make_async_copy(part.at[size, 0], notes.at[n], sems.at[n])
             for n, (part, size) in enumerate(((right, 6), (low, 12), (corner, 3)))]
    for read in reads:
        read.start()
    weight[...] = jnp.zeros_like(weight)

    def add_slot(top, left, live, classes):
        @pl.when(live)
        def _():
            for q in classes:
                row = top + q // 2
                col = left + q % 2

                @pl.when((row >= 0) & (row < TILE_R) & (col >= 0) & (col < TILE_C))
                def _():
                    weight[row * TILE_C + col] += light[
                        q // 2, :, PIECE_C * (q % 2):PIECE_C * (q % 2 + 1)]

    for s in range(2):
        add_slot(info[2 * s], info[2 * s + 1], s < info[4], range(8))
    for read in reads:
        read.wait()
    for n, (down, across, classes) in enumerate((
            (0, TILE_C, (1, 3, 5, 7)), (TILE_R, 0, (2, 3, 4, 5, 6, 7)), (TILE_R, TILE_C, (3, 5, 7)))):
        for s in range(2):
            top = notes[n, 2 * s, 0].astype(jnp.int32) - down
            left = notes[n, 2 * s + 1, 0].astype(jnp.int32) - across
            live = s < notes[n, 4, 0].astype(jnp.int32)
            add_slot(top, left, live & (top > -4) & (left > -2), classes)
    fetch.wait()
    for p in range(TILE_R * TILE_C):
        row, col = p // TILE_C, p % TILE_C
        total = own[p]
        if row < 3:
            total = total + low[p]
        if col == 0:
            total = total + right[row]
        if row < 3 and col == 0:
            total = total + corner[row]
        new[p] = old[p] + total / (weight[p] + object_floor)[None]


def update(info, pieces, own, right, low, corner, light):
    shape = (TILE_R * TILE_C, 2, SUB, PIECE_C)
    return pl.pallas_call(
        update_kernel,
        in_specs=[SMEM, ANY] + [VMEM] * 5,
        out_specs=VMEM,
        out_shape=jax.ShapeDtypeStruct(shape, F32),
        scratch_shapes=[pltpu.VMEM(shape, F32), pltpu.VMEM((TILE_R * TILE_C, SUB, PIECE_C), F32),
                        pltpu.SMEM((3, SUB, PIECE_C), F32), pltpu.SemaphoreType.DMA((4,))],
        compiler_params=pltpu.CompilerParams(vmem_limit_bytes=SMALL_BYTES),
        cost_estimate=pl.CostEstimate(flops=1000000, bytes_accessed=2000000, transcendentals=0),
        name="update",
    )(info, pieces, own, right, low, corner, light)


def join_pieces_kernel(info, n0, n1, n2, n3, out, sems):
    writes = []
    for j, part in enumerate((n0, n1, n2, n3)):
        start = pl.multiple_of(lax.rem(info[5] + N_MODE - j, N_MODE) * SUB, SUB)
        writes.append(pltpu.make_async_copy(part, out.at[:, :, pl.ds(start, SUB), :], sems.at[j]))
        writes[j].start()
    for write in writes:
        write.wait()


def join_pieces(info, parts):
    return pl.pallas_call(
        join_pieces_kernel,
        in_specs=[SMEM] + [ANY] * 4,
        out_specs=pl.BlockSpec(memory_space=pltpu.HBM),
        out_shape=jax.ShapeDtypeStruct((TILE_R * TILE_C, 2, PIECE_R, PIECE_C), F32),
        scratch_shapes=[pltpu.SemaphoreType.DMA((N_MODE,))],
        compiler_params=pltpu.CompilerParams(vmem_limit_bytes=2 * 1024 * 1024),
        cost_estimate=pl.CostEstimate(flops=0, bytes_accessed=3000000, transcendentals=0),
        name="join_pieces",
    )(info, *parts)


def join_channels_kernel(info, mine, theirs, out, sems):
    core = info[6]
    writes = []
    for half, source in enumerate((mine, theirs)):
        channel = core if half == 0 else 1 - core
        for k in range(3):
            writes.append(pltpu.make_async_copy(
                source.at[k], out.at[k, channel], sems.at[half, k]))
            writes[-1].start()
    for write in writes:
        write.wait()


def join_channels(info, mine, theirs):
    return pl.pallas_call(
        join_channels_kernel,
        in_specs=[SMEM, ANY, ANY],
        out_specs=pl.BlockSpec(memory_space=pltpu.HBM),
        out_shape=jax.ShapeDtypeStruct((3, 2, SIDE, SIDE), F32),
        scratch_shapes=[pltpu.SemaphoreType.DMA((2, 3))],
        compiler_params=pltpu.CompilerParams(vmem_limit_bytes=2 * 1024 * 1024),
        cost_estimate=pl.CostEstimate(flops=0, bytes_accessed=3000000, transcendentals=0),
        name="join_channels",
    )(info, mine, theirs)


def body(object_pieces, probe_modes, intensity, positions, counts):
    tile_index = lax.axis_index("tile")
    mode_index = lax.axis_index("mode")
    table = fourier_table()
    tile_grid = object_pieces.reshape(TILE_R, TILE_C, 2, PIECE_R, PIECE_C)
    own_rows = lax.dynamic_slice_in_dim(object_pieces[:12], mode_index * SUB, SUB, axis=2)
    low = shifted(own_rows, -DEV_COLS)
    corner = shifted(own_rows[::TILE_C], -DEV_COLS - 1)
    right = shifted(tile_grid[:, 0], -1)
    below = jnp.concatenate([low, corner], axis=0)
    dev_row = tile_index // DEV_COLS
    dev_col = tile_index % DEV_COLS
    rows = jnp.clip(positions[:, 0] // PIECE_R - dev_row * TILE_R, 0, TILE_R - 1)
    cols = jnp.clip(positions[:, 1] // PIECE_C - dev_col * TILE_C, 0, TILE_C - 1)
    info = jnp.stack([rows[0], cols[0], rows[1], cols[1], counts[0], mode_index,
                      tile_index % 2, tile_index]).astype(jnp.int32)
    late_modes, below = lax.optimization_barrier((probe_modes, below))
    light_local = jnp.sum(late_modes * late_modes, axis=(0, 1))
    light_parts = light_local.reshape(4, N_MODE, SUB, SIDE).transpose(1, 0, 2, 3)
    light = lax.psum_scatter(light_parts, "mode", scatter_dimension=0, tiled=True)
    below = [below] + [turned(below, j) for j in (1, 2, 3)]

    far, patch, *powers = forward(info, in_hbm(object_pieces), in_hbm(right),
                                  [in_hbm(block) for block in below], probe_modes, in_hbm(table))
    received = [turned(powers[j], j) for j in (1, 2, 3)]
    power = (powers[0] + received[0]) + (received[1] + received[2])
    own_intensity = lax.dynamic_slice_in_dim(intensity, mode_index * 64, 64, axis=1)
    live = (jnp.arange(2, dtype=jnp.int32) < counts[0]).astype(F32)
    factor = live[:, None, None] * (jnp.sqrt(own_intensity) / jnp.sqrt(power + far_floor) - 1.0)
    factors = [factor] + [turned(factor, j) for j in (1, 2, 3)]

    mine, theirs, *grads = backward(info, in_hbm(far), probe_modes, patch, factors, in_hbm(table))

    groups = [list(range(core, N_TILE, 2)) for core in range(2)]
    exchange = lambda blocks: lax.all_to_all(
        blocks, "tile", 0, 0, axis_index_groups=groups, tiled=True)
    summed = mine + core_swap(theirs)
    pieces = exchange(summed.reshape(N_CHIP, PART, SIDE))
    parts = [grads[0]] + [turned(grads[j], j) for j in (1, 2, 3)]
    own, to_right, to_low, to_corner = scatter(info, parts)
    from_above = shifted(to_low, DEV_COLS)
    from_corner = shifted(to_corner, DEV_COLS + 1)
    from_left = shifted(to_right, 1)
    shares = jnp.broadcast_to(jnp.sum(pieces, axis=0)[None], (N_CHIP, PART, SIDE))
    shares, from_left, from_above, from_corner = lax.optimization_barrier(
        (shares, from_left, from_above, from_corner))

    new = update(info, object_pieces, own, from_left, from_above, from_corner, in_hbm(light[0]))
    shares, new = lax.optimization_barrier((shares, new))
    gathered = exchange(shares)
    new_parts = [new] + [turned(new, j) for j in (1, 2, 3)]
    gathered, *new_parts = lax.optimization_barrier((gathered, *new_parts))
    gathered = gathered.reshape(3, SIDE, SIDE)
    probe_grad = join_channels(info, gathered, core_swap(gathered))
    return (join_pieces(info, new_parts), probe_grad)


def solution(mesh):
    return jax.shard_map(
        body,
        mesh=mesh,
        in_specs=(
            P("tile", None, None, None),
            P("mode", None, None, None),
            P("tile", None, None),
            P("tile", None),
            P("tile"),
        ),
        out_specs=(P("tile", None, None, None), P("mode", None, None, None)),
        check_vma=False,
    )
```
